128 devices in a mesh: seq: 32 (over y, x_hi, z), dp: 4 (over x_lo, core).
Axes of the slice: x: 4 (x_hi: 2, x_lo: 2; x = x_hi * 2 + x_lo), y: 4, z: 4, core: 2. Of those that a mesh axis runs over, the one named last changes fastest.
Arguments:
- spectra_in: bfloat16 [24, 2048, 768], P('dp', 'seq'), may hold values from -6 to 6
- cotangent: bfloat16 [24, 2048, 768], P('dp', 'seq'), may hold values from -6 to 6
- tok_in_w: bfloat16 [2048, 1024], P('seq'), may hold values from -0.125 to 0.125
- tok_out_w: bfloat16 [2048, 1024], P('seq'), may hold values from -0.1875 to 0.1875
- ch_in_w: bfloat16 [1536, 768], replicated, may hold values from -0.21875 to 0.21875
- ch_out_w: bfloat16 [1536, 768], replicated, may hold values from -0.15625 to 0.15625
Outputs:
- grad_input: bfloat16 [24, 2048, 768], P('dp', 'seq')
- grad_tok_in: float32 [2048, 1024], P(('seq', 'dp'))
- grad_tok_out: float32 [2048, 1024], P(('seq', 'dp'))
- grad_ch_in: float32 [1536, 768], P(('seq', 'dp'))
- grad_ch_out: float32 [1536, 768], P(('seq', 'dp'))
The draws below stay inside these ranges and needn't reach their ends.
All inputs are finite; a program needn't handle non-finite values.
Results may differ from the reference program's by a relative error of at most 0.012.
Values may be sent and summed in bfloat16 or wider, within the bound.
A program may use at most 192 MiB of HBM per device.

```python
import math
import jax
import jax.numpy as jnp
from jax import lax

CHANNELS = 768
PATCHES = 2048
TOK_HID = 1024
CH_HID = 1536
SPECTRA = 24


def level_of(stream_key, dims, cuts, least, largest):
    def one(position, blocks):
        draws = jax.random.uniform(jax.random.fold_in(jax.random.fold_in(stream_key, 6), position), (blocks,), jnp.float32, least / len(cuts), largest / len(cuts))
        return jnp.repeat(jnp.exp(draws), dims[position] // blocks).reshape((-1,) + (1,) * (len(dims) - position - 1))

    factor_of = one(*cuts[0])
    for cut in cuts[1:]:
        factor_of = factor_of * one(*cut)
    return factor_of


def normal_values(rng, shape, spread, most, split=(), kind=jnp.bfloat16):
    gain = level_of(rng, shape, split, -0.22, 0.18) if split else 1.0
    values = jax.random.normal(rng, shape, jnp.float32) * spread * gain
    return jnp.minimum(jnp.maximum(values, -most), most).astype(kind)


def setup_inputs(seed: int = 0) -> dict:
    seeds = jax.random.split(jax.random.key(seed), 7)
    spectra_in = normal_values(seeds[0], (SPECTRA, PATCHES, CHANNELS), 1.0, 6.0, ((0, 4), (1, 32)))
    cotangent = normal_values(seeds[1], (SPECTRA, PATCHES, CHANNELS), 1.0, 6.0, ((0, 4), (1, 32)))
    tok_in_w = normal_values(seeds[2], (PATCHES, TOK_HID), PATCHES ** -0.5, 0.125, ((0, 32),))
    tok_out_w = normal_values(seeds[3], (PATCHES, TOK_HID), TOK_HID ** -0.5, 0.1875, ((0, 32),))
    ch_in_w = normal_values(seeds[4], (CH_HID, CHANNELS), CHANNELS ** -0.5, 0.21875)
    ch_out_w = normal_values(seeds[5], (CH_HID, CHANNELS), CH_HID ** -0.5, 0.15625)
    return {"spectra_in": spectra_in, "cotangent": cotangent, "tok_in_w": tok_in_w, "tok_out_w": tok_out_w, "ch_in_w": ch_in_w, "ch_out_w": ch_out_w}


def normalize(values):
    center = values - lax.optimization_barrier(jnp.mean(values, axis=-1, keepdims=True))
    inv_scale = lax.rsqrt(lax.optimization_barrier(jnp.mean(center * center, axis=-1, keepdims=True)) + 1e-05)
    return (center * inv_scale, inv_scale)

def norm_back(unit, inv_scale, upstream):
    first = lax.optimization_barrier(jnp.mean(upstream, axis=-1, keepdims=True))
    second = lax.optimization_barrier(jnp.mean(upstream * unit, axis=-1, keepdims=True))
    return inv_scale * (upstream - first - unit * second)

def gelu_pair(values):
    factor = math.sqrt(2.0 / math.pi)
    inner = factor * (values + 0.044715 * values * values * values)
    tangent = jnp.tanh(inner)
    result = 0.5 * values * (1.0 + tangent)
    slope = 0.5 * (1.0 + tangent) + 0.5 * values * (1.0 - tangent * tangent) * factor * (1.0 + 3.0 * 0.044715 * values * values)
    return (result, slope)

def mixed(form, left, right):
    return jnp.einsum(form, left.astype(jnp.float32), right.astype(jnp.float32))

def reference(spectra_in, cotangent, tok_in_w, tok_out_w, ch_in_w, ch_out_w):
    source = spectra_in.astype(jnp.float32)
    unit_first, scale_first = normalize(source)
    normed = unit_first.astype(jnp.bfloat16)
    hidden = mixed('spc,pj->scj', normed, tok_in_w)
    hidden_val, hidden_slope = gelu_pair(hidden)
    token_act = hidden_val.astype(jnp.bfloat16)
    token_mix = mixed('scj,pj->spc', token_act, tok_out_w).astype(jnp.bfloat16)
    middle = (source + token_mix.astype(jnp.float32)).astype(jnp.bfloat16)
    unit_second, scale_second = normalize(middle.astype(jnp.float32))
    normed_second = unit_second.astype(jnp.bfloat16)
    chan_pre = mixed('spc,hc->sph', normed_second, ch_in_w)
    chan_val, chan_slope = gelu_pair(chan_pre)
    chan_act = chan_val.astype(jnp.bfloat16)
    chan_grad = (mixed('spc,hc->sph', cotangent, ch_out_w) * chan_slope).astype(jnp.bfloat16)
    grad_ch_in = mixed('sph,spc->hc', chan_grad, normed_second)
    grad_ch_out = mixed('sph,spc->hc', chan_act, cotangent)
    second_up = mixed('sph,hc->spc', chan_grad, ch_in_w)
    middle_grad = cotangent.astype(jnp.float32) + norm_back(unit_second, scale_second, second_up)
    mix_grad = middle_grad.astype(jnp.bfloat16)
    hidden_grad = (mixed('spc,pj->scj', mix_grad, tok_out_w) * hidden_slope).astype(jnp.bfloat16)
    grad_tok_in = mixed('spc,scj->pj', normed, hidden_grad)
    grad_tok_out = mixed('spc,scj->pj', mix_grad, token_act)
    normed_grad = mixed('scj,pj->spc', hidden_grad, tok_in_w).astype(jnp.bfloat16)
    grad_input = (middle_grad + norm_back(unit_first, scale_first, normed_grad.astype(jnp.float32))).astype(jnp.bfloat16)
    return (grad_input, grad_tok_in, grad_tok_out, grad_ch_in, grad_ch_out)
```

```python
import functools
import math

import jax
import jax.numpy as jnp
from jax import lax
from jax.experimental import pallas as pl
from jax.experimental.pallas import tpu as pltpu
from jax.sharding import PartitionSpec as P

BF = jnp.bfloat16
F32 = jnp.float32
MESH = pl.DeviceIdType.MESH
ANY = pl.BlockSpec(memory_space=pl.ANY)
LANES = 128


def normalize(values):
    center = values - jnp.mean(values, axis=-1, keepdims=True)
    inv_scale = lax.rsqrt(jnp.mean(center * center, axis=-1, keepdims=True) + 1e-05)
    return (center * inv_scale, inv_scale)


def norm_back(unit, inv_scale, upstream):
    first = jnp.mean(upstream, axis=-1, keepdims=True)
    second = jnp.mean(upstream * unit, axis=-1, keepdims=True)
    return inv_scale * (upstream - first - unit * second)


def gelu_pair(values):
    factor = math.sqrt(2.0 / math.pi)
    inner = factor * (values + 0.044715 * values * values * values)
    tangent = jnp.tanh(inner)
    result = 0.5 * values * (1.0 + tangent)
    slope = 0.5 * (1.0 + tangent) + 0.5 * values * (1.0 - tangent * tangent) * factor * (
        1.0 + 3.0 * 0.044715 * values * values
    )
    return (result, slope)


class Here:
    def __init__(self):
        self.q = lax.axis_index("seq")
        self.d = lax.axis_index("dp")
        self.y = self.q // 8
        self.xh = (self.q // 4) % 2
        self.z = self.q % 4
        self.xl = self.d // 2
        self.c = self.d % 2
        self.x = self.xh * 2 + self.xl

    def at(self, x=None, y=None, z=None, c=None):
        x = self.x if x is None else x
        y = self.y if y is None else y
        z = self.z if z is None else z
        c = self.c if c is None else c
        return {"seq": (y * 2 + x // 2) * 4 + z, "dp": (x % 2) * 2 + c}

    def peer(self, q):
        return {"seq": q, "dp": self.d}

    def sibling(self):
        return {"seq": self.q, "dp": self.d + 1 - 2 * self.c}

    def extra_of(self, e):
        return 8 * e + ((e + self.d // 2) % 2) * 4 + (e + self.d) % 4

    def has_extra(self):
        return self.q == self.extra_of(self.y)


def remote(src, dst, send, recv, device):
    return pltpu.make_async_remote_copy(
        src_ref=src, dst_ref=dst, send_sem=send, recv_sem=recv,
        device_id=device, device_id_type=MESH,
    )


def drain(ref, sem):
    pltpu.make_async_copy(ref, ref, sem).wait()


def greet(devices):
    barrier = pltpu.get_barrier_semaphore()
    for device in devices:
        pl.semaphore_signal(barrier, inc=1, device_id=device, device_id_type=MESH)
    return len(devices)


def greet_seq(here):
    barrier = pltpu.get_barrier_semaphore()

    def body(i, carry):
        pl.semaphore_signal(
            barrier, inc=1, device_id=here.peer((here.q + i) % 32), device_id_type=MESH
        )
        return carry

    lax.fori_loop(1, 32, body, 0)
    return 31


def rows(start, size):
    return pl.ds(pl.multiple_of(start * size, size), size)


def tile_of(ref, s, b):
    return ref.at[rows(s, 64), pl.ds(pl.multiple_of(b * LANES, LANES), LANES)]


def send_to_channels(here, src, cols, zero, sems):
    send, recv, own, esend, erecv = sems
    mine = rows(here.q, 64)

    def body(i, carry):
        dest = (here.q + i) % 32
        remote(
            tile_of(src, dest // 6, dest % 6), cols.at[mine, pl.ds(0, LANES)],
            send, recv, here.peer(dest),
        ).start()
        return carry

    lax.fori_loop(1, 32, body, 0)
    pltpu.make_async_copy(
        tile_of(src, here.q // 6, here.q % 6), cols.at[mine, pl.ds(0, LANES)], own
    ).start()
    for e in range(4):
        dest = here.extra_of(e)
        block = tile_of(src, 5, 2 + e)
        place = cols.at[mine, pl.ds(LANES, LANES)]

        @pl.when(dest != here.q)
        def _():
            remote(block, place, esend.at[e], erecv, here.peer(dest)).start()

        @pl.when(dest == here.q)
        def _():
            pltpu.make_async_copy(block, place, esend.at[e]).start()

    @pl.when(jnp.logical_not(here.has_extra()))
    def _():
        zero[...] = jnp.zeros_like(zero)
        for k in range(8):
            pltpu.make_async_copy(
                zero, cols.at[pl.ds(k * 256, 256), pl.ds(LANES, LANES)], erecv
            ).start()


def wait_to_channels(here, src, cols, zero, sems):
    send, recv, own, esend, erecv = sems
    many = cols.at[pl.ds(0, 31 * 64), pl.ds(0, LANES)]
    drain(many, send)
    drain(many, recv)
    drain(cols.at[pl.ds(0, 64), pl.ds(0, LANES)], own)
    for e in range(4):
        drain(cols.at[pl.ds(0, 64), pl.ds(0, LANES)], esend.at[e])

    @pl.when(here.has_extra())
    def _():
        drain(cols.at[pl.ds(0, 31 * 64), pl.ds(LANES, LANES)], erecv)

    @pl.when(jnp.logical_not(here.has_extra()))
    def _():
        drain(cols.at[:, pl.ds(LANES, LANES)], erecv)


CHANNEL_SEMS = [
    pltpu.SemaphoreType.DMA, pltpu.SemaphoreType.DMA, pltpu.SemaphoreType.DMA,
    pltpu.SemaphoreType.DMA((4,)), pltpu.SemaphoreType.DMA,
]


def send_to_patches(here, cols, out, sems):
    send, recv, own, esend, erecv = sems
    place = tile_of(out, here.q // 6, here.q % 6)
    place_extra = tile_of(out, 5, 2 + here.y)

    def body(i, carry):
        dest = (here.q + i) % 32
        remote(
            cols.at[rows(dest, 64), pl.ds(0, LANES)], place, send, recv, here.peer(dest)
        ).start()
        return carry

    lax.fori_loop(1, 32, body, 0)
    pltpu.make_async_copy(cols.at[rows(here.q, 64), pl.ds(0, LANES)], place, own).start()

    @pl.when(here.has_extra())
    def _():
        def more(i, carry):
            dest = (here.q + i) % 32
            remote(
                cols.at[rows(dest, 64), pl.ds(LANES, LANES)], place_extra,
                esend, erecv.at[here.y], here.peer(dest),
            ).start()
            return carry

        lax.fori_loop(1, 32, more, 0)
        pltpu.make_async_copy(
            cols.at[rows(here.q, 64), pl.ds(LANES, LANES)], place_extra, erecv.at[here.y]
        ).start()


def wait_to_patches(here, cols, out, sems):
    send, recv, own, esend, erecv = sems
    many = cols.at[pl.ds(0, 31 * 64), pl.ds(0, LANES)]
    one = cols.at[pl.ds(0, 64), pl.ds(0, LANES)]
    drain(many, send)
    drain(many, recv)
    drain(one, own)
    for e in range(4):
        drain(one, erecv.at[e])

    @pl.when(here.has_extra())
    def _():
        drain(many, esend)


PATCH_SEMS = [
    pltpu.SemaphoreType.DMA, pltpu.SemaphoreType.DMA, pltpu.SemaphoreType.DMA,
    pltpu.SemaphoreType.DMA, pltpu.SemaphoreType.DMA((4,)),
]


def params(cid, vmem=None):
    return pltpu.CompilerParams(
        collective_id=cid, has_side_effects=True, vmem_limit_bytes=vmem
    )


def to_channels_kernel(src, cols, zero, *sems):
    here = Here()
    pl.semaphore_wait(pltpu.get_barrier_semaphore(), greet_seq(here))
    send_to_channels(here, src, cols, zero, sems)
    wait_to_channels(here, src, cols, zero, sems)


def to_channels(values, cid):
    return pl.pallas_call(
        to_channels_kernel,
        out_shape=jax.ShapeDtypeStruct((2048, 2 * LANES), BF),
        in_specs=[ANY], out_specs=ANY,
        scratch_shapes=[pltpu.VMEM((256, LANES), BF)] + CHANNEL_SEMS,
        compiler_params=params(cid),
        name="to_channels",
    )(values)


def to_patches_kernel(cols, out, *sems):
    here = Here()
    pl.semaphore_wait(pltpu.get_barrier_semaphore(), greet_seq(here))
    send_to_patches(here, cols, out, sems)
    wait_to_patches(here, cols, out, sems)


def to_patches(cols, cid):
    return pl.pallas_call(
        to_patches_kernel,
        out_shape=jax.ShapeDtypeStruct((384, 768), BF),
        in_specs=[ANY], out_specs=ANY,
        scratch_shapes=PATCH_SEMS,
        compiler_params=params(cid),
        name="to_patches",
    )(cols)


def gather_kernel(src, w_in, w_out, cols, full_in, full_out, zero, *sems):
    a2a, (own, send, recv, bsend, brecv) = sems[:5], sems[5:]
    here = Here()
    c, y, xh, z = here.c, here.y, here.xh, here.z
    sib = here.sibling()
    count = greet_seq(here) + greet([sib])
    pl.semaphore_wait(pltpu.get_barrier_semaphore(), count)

    fulls = (full_in, full_out)
    started = []

    def push(w, k, ref, device):
        copy = remote(ref, ref, send.at[w, k], recv.at[w, k], device)
        copy.start()
        started.append(copy)
        return copy

    def share(w, k, ref):
        copy = remote(ref, ref, bsend.at[w, k], brecv.at[w, k], sib)
        copy.start()
        started.append(copy)

    locals_ = []
    crossing = []
    for w, part in enumerate((w_in, w_out)):
        copy = pltpu.make_async_copy(part, fulls[w].at[y, xh, z], own.at[w])
        copy.start()
        locals_.append(copy)
        copy = remote(
            part.at[c], fulls[w].at[y, xh, z, c], send.at[w, 0], recv.at[w, 0],
            here.at(x=(here.x + 2) % 4),
        )
        copy.start()
        crossing.append(copy)
    send_to_channels(here, src, cols, zero, a2a)

    def chunk(w, stage, pos, half=None):
        h = slice(None) if half is None else half
        along_z = (stage == 0) == (w == 0)
        if along_z:
            if stage == 0:
                return fulls[w].at[y, h, pos, c]
            return fulls[w].at[:, h, pos, c]
        if stage == 0:
            return fulls[w].at[pos, h, z, c]
        return fulls[w].at[pos, h, :, c]

    for w in range(2):
        locals_[w].wait()
        crossing[w].wait_recv()
        share(w, 0, fulls[w].at[y, 1 - xh, z, c])
    for stage in range(2):
        base = 1 + 4 * stage
        legs = []
        for w in range(2):
            along_z = (stage == 0) == (w == 0)
            me = z if along_z else y
            up, down = (me + 1) % 4, (me + 3) % 4
            far = (me + 2) % 4
            if along_z:
                to_up, to_down = here.at(z=up), here.at(z=down)
            else:
                to_up, to_down = here.at(y=up), here.at(y=down)
            rise = push(w, base, chunk(w, stage, me), to_up)
            fall = push(w, base + 1, chunk(w, stage, me), to_down)
            legs.append((up, down, far, to_up, to_down, rise, fall))
        late = []
        for w in range(2):
            up, down, far, to_up, to_down, rise, fall = legs[w]
            rise.wait_recv()
            one = push(w, base + 2, chunk(w, stage, down, 0), to_up)
            share(w, base, chunk(w, stage, down))
            fall.wait_recv()
            two = push(w, base + 3, chunk(w, stage, up, 1), to_down)
            share(w, base + 1, chunk(w, stage, up))
            late.append((one, two))
        for w in range(2):
            far = legs[w][2]
            late[w][0].wait_recv()
            share(w, base + 2, chunk(w, stage, far, 0))
            late[w][1].wait_recv()
            share(w, base + 3, chunk(w, stage, far, 1))

    for w in range(2):
        crossing[w].wait_send()
    for copy in started:
        copy.wait_send()
    other = 1 - c
    for w in range(2):
        def theirs(stage, pos, half=None):
            h = slice(None) if half is None else half
            along_z = (stage == 0) == (w == 0)
            if along_z:
                return fulls[w].at[y, h, pos, other] if stage == 0 else fulls[w].at[:, h, pos, other]
            return fulls[w].at[pos, h, z, other] if stage == 0 else fulls[w].at[pos, h, :, other]

        drain(fulls[w].at[y, 1 - xh, z, other], brecv.at[w, 0])
        for stage in range(2):
            along_z = (stage == 0) == (w == 0)
            me = z if along_z else y
            base = 1 + 4 * stage
            drain(theirs(stage, (me + 3) % 4), brecv.at[w, base])
            drain(theirs(stage, (me + 1) % 4), brecv.at[w, base + 1])
            drain(theirs(stage, (me + 2) % 4, 0), brecv.at[w, base + 2])
            drain(theirs(stage, (me + 2) % 4, 1), brecv.at[w, base + 3])
    wait_to_channels(here, src, cols, zero, a2a)


def gather(values, w_in, w_out, cid):
    full = jax.ShapeDtypeStruct((4, 2, 4, 2, 32, 1024), BF)
    return pl.pallas_call(
        gather_kernel,
        out_shape=(jax.ShapeDtypeStruct((2048, 2 * LANES), BF), full, full),
        in_specs=[ANY] * 3, out_specs=(ANY,) * 3,
        scratch_shapes=[pltpu.VMEM((256, LANES), BF)] + CHANNEL_SEMS + [
            pltpu.SemaphoreType.DMA((2,)),
            pltpu.SemaphoreType.DMA((2, 9)), pltpu.SemaphoreType.DMA((2, 9)),
            pltpu.SemaphoreType.DMA((2, 9)), pltpu.SemaphoreType.DMA((2, 9)),
        ],
        compiler_params=params(cid),
        name="gather_and_to_channels",
    )(values, w_in.reshape(2, 32, 1024), w_out.reshape(2, 32, 1024))


ORDERS = ("yzx", "zxy", "xyz")


def add_into(target, other):
    lead = target.shape[:-2]
    count = math.prod(lead)

    def body(i, carry):
        index = []
        rest = i
        for size in reversed(lead):
            index.append(rest % size)
            rest = rest // size
        index = tuple(reversed(index))
        target[index] = (target[index].astype(F32) + other[index].astype(F32)).astype(BF)
        return carry

    if count == 1:
        index = (0,) * len(lead)
        target[index] = (target[index].astype(F32) + other[index].astype(F32)).astype(BF)
    else:
        lax.fori_loop(0, count, body, 0)


def sums_kernel(g0, g1, g2, cols, o0, o1, o2, patches, *scratch):
    here = Here()
    c = here.c
    acc, pair = scratch[0:3], scratch[3:6]
    bufs = [scratch[6 + 12 * p:18 + 12 * p] for p in range(3)]
    last = scratch[42]
    lsem, psend, precv, send, recv, fsem = scratch[43:49]
    a2a = scratch[49:54]
    sib = here.sibling()
    near = []
    for k in (1, 2, 3):
        near += [here.at(x=(here.x + k) % 4), here.at(y=(here.y + k) % 4), here.at(z=(here.z + k) % 4)]
    count = greet_seq(here) + greet(
        [sib, here.at(x=(here.x + 1) % 4), here.at(x=(here.x + 3) % 4)]
    )
    pl.semaphore_wait(pltpu.get_barrier_semaphore(), count)

    def side(p, ref, which):
        if p < 2:
            return ref.at[:, :, :, :, which]
        return ref.at[:, :, :, :, :, pl.ds(pl.multiple_of(which * 384, 384), 384)]

    ins = (g0, g1, g2)
    loads, pairs = [], []
    send_to_patches(here, cols, patches, a2a)
    for p in range(3):
        pairs.append(remote(side(p, ins[p], 1 - c), pair[p], psend.at[p], precv.at[p], sib))
        pairs[p].start()
        loads.append(pltpu.make_async_copy(side(p, ins[p], c), acc[p], lsem.at[p]))
        loads[p].start()

    def axis(p, stage):
        name = ORDERS[p][stage]
        me = getattr(here, name)
        up, down = (me + 1) % 4, (me + 3) % 4
        return name, me, up, down, here.at(**{name: up}), here.at(**{name: down})

    def chunk(p, stage, pos, half=None):
        done = ORDERS[p][:stage]
        name = ORDERS[p][stage]
        index = {"y": slice(None), "xh": slice(None), "z": slice(None), "xl": slice(None)}
        for other in done:
            if other == "x":
                index["xh"], index["xl"] = here.xh, here.xl
            else:
                index[other] = getattr(here, other)
        if name == "x":
            index["xh"], index["xl"] = pos // 2, pos % 2
        else:
            index[name] = pos
        tail = []
        if half is not None:
            for other in ("y", "xh", "z", "xl"):
                if isinstance(index[other], slice):
                    size = {"y": 4, "xh": 2, "z": 4, "xl": 2}[other]
                    index[other] = pl.ds(half * (size // 2), size // 2)
                    break
            else:
                width = acc[p].shape[-1]
                if width == 1024:
                    tail = [slice(None), pl.ds(half * 512, 512)]
                else:
                    tail = [pl.ds(16 * half, 16 + 16 * half)]
        return acc[p].at[tuple([index["y"], index["xh"], index["z"], index["xl"]] + tail)]

    waits = []
    for p in range(3):
        loads[p].wait()
        pairs[p].wait_recv()
        add_into(acc[p], pair[p])
        waits.append(pairs[p])

    for stage in range(3):
        first = []
        for p in range(3):
            name, me, up, down, to_up, to_down = axis(p, stage)
            a, b, f, g = bufs[p][4 * stage:4 * stage + 4]
            far = (me + 2) % 4
            k = 4 * stage
            one = remote(chunk(p, stage, far, 0), a, send.at[p, k], recv.at[p, k], to_up)
            one.start()
            two = remote(chunk(p, stage, far, 1), b, send.at[p, k + 1], recv.at[p, k + 1], to_down)
            two.start()
            first.append((one, two))
        second = []
        for p in range(3):
            name, me, up, down, to_up, to_down = axis(p, stage)
            a, b, f, g = bufs[p][4 * stage:4 * stage + 4]
            k = 4 * stage
            first[p][0].wait_recv()
            add_into(chunk(p, stage, up, 0), a)
            three = remote(chunk(p, stage, up), f, send.at[p, k + 2], recv.at[p, k + 2], to_up)
            three.start()
            first[p][1].wait_recv()
            add_into(chunk(p, stage, down, 1), b)
            four = remote(chunk(p, stage, down), g, send.at[p, k + 3], recv.at[p, k + 3], to_down)
            four.start()
            second.append((three, four))
            waits += [first[p][0], first[p][1], three, four]
        for p in range(3):
            name, me, up, down, to_up, to_down = axis(p, stage)
            a, b, f, g = bufs[p][4 * stage:4 * stage + 4]
            second[p][0].wait_recv()
            second[p][1].wait_recv()
            mine = chunk(p, stage, me)
            if stage < 2:
                add_into(mine, f)
                add_into(mine, g)
            else:
                total = mine[...].astype(F32) + f[...].astype(F32) + g[...].astype(F32)
                if p < 2:
                    (o0, o1)[p][...] = total
                else:
                    last[c] = total
    swap = remote(last.at[c], last.at[c], fsem.at[0], fsem.at[1], sib)
    swap.start()
    for copy in waits:
        copy.wait_send()
    swap.wait()
    o2[:, 0:384] = last[0]
    o2[:, 384:768] = last[1]
    wait_to_patches(here, cols, patches, a2a)


def sums(g_in, g_out, g_chan, cols, cid):
    scratch = []
    tails = ((16, 1024), (16, 1024), (48, 384))
    for _ in range(2):
        scratch += [pltpu.VMEM((4, 2, 4, 2) + tail, BF) for tail in tails]
    for p in range(3):
        for stage in range(3):
            dims = {"y": 4, "xh": 2, "z": 4, "xl": 2}
            for name in ORDERS[p][:stage + 1]:
                for key in {"x": ("xh", "xl"), "y": ("y",), "z": ("z",)}[name]:
                    del dims[key]
            lead = list(dims.values())
            tail = list(tails[p])
            if lead:
                half = [lead[0] // 2] + lead[1:] + tail
                halves = (half, half)
            elif p < 2:
                halves = ([16, 512], [16, 512])
            else:
                halves = ([16, 384], [32, 384])
            scratch += [pltpu.VMEM(tuple(h), BF) for h in halves]
            scratch += [pltpu.VMEM(tuple(lead + tail), BF)] * 2
    scratch += [pltpu.VMEM((2, 48, 384), F32)]
    dma = pltpu.SemaphoreType.DMA
    scratch += [dma((3,)), dma((3,)), dma((3,)), dma((3, 12)), dma((3, 12)), dma((2,))]
    scratch += PATCH_SEMS
    vmem = pl.BlockSpec(memory_space=pltpu.VMEM)
    return pl.pallas_call(
        sums_kernel,
        out_shape=(
            jax.ShapeDtypeStruct((16, 1024), F32),
            jax.ShapeDtypeStruct((16, 1024), F32),
            jax.ShapeDtypeStruct((48, 768), F32),
            jax.ShapeDtypeStruct((384, 768), BF),
        ),
        in_specs=[ANY] * 4, out_specs=(vmem, vmem, vmem, ANY),
        scratch_shapes=scratch,
        compiler_params=params(cid, 48 * 1024 * 1024),
        name="sums_and_to_patches",
    )(
        g_in.reshape(4, 2, 4, 2, 2, 16, 1024),
        g_out.reshape(4, 2, 4, 2, 2, 16, 1024),
        g_chan.reshape(4, 2, 4, 2, 48, 768),
        cols,
    )


def local(spectra_in, cotangent, tok_in_w, tok_out_w, ch_in_w, ch_out_w):
    source = spectra_in.reshape(384, 768).astype(F32)
    cotangent = cotangent.reshape(384, 768)
    unit_first, scale_first = normalize(source)
    normed = unit_first.astype(BF)
    normed_cols, whole_in, whole_out = gather(normed, tok_in_w, tok_out_w, 0)
    whole_in = whole_in.reshape(2048, 1024)
    whole_out = whole_out.reshape(2048, 1024)
    hidden = jnp.einsum("pc,pj->cj", normed_cols, whole_in, preferred_element_type=F32)
    hidden_val, hidden_slope = gelu_pair(hidden)
    token_act = hidden_val.astype(BF)
    mix_cols = jnp.einsum("pj,cj->pc", whole_out, token_act, preferred_element_type=F32).astype(BF)
    token_mix = to_patches(mix_cols, 1)
    middle = (source + token_mix.astype(F32)).astype(BF)
    unit_second, scale_second = normalize(middle.astype(F32))
    normed_second = unit_second.astype(BF)
    chan_pre = jnp.einsum("tc,hc->th", normed_second, ch_in_w, preferred_element_type=F32)
    chan_val, chan_slope = gelu_pair(chan_pre)
    chan_act = chan_val.astype(BF)
    chan_down = jnp.einsum("tc,hc->th", cotangent, ch_out_w, preferred_element_type=F32)
    chan_grad = (chan_down * chan_slope).astype(BF)
    second_up = jnp.einsum("th,hc->tc", chan_grad, ch_in_w, preferred_element_type=F32)
    middle_grad = cotangent.astype(F32) + norm_back(unit_second, scale_second, second_up)
    mix_grad = middle_grad.astype(BF)
    mix_cols_grad = to_channels(mix_grad, 2)
    grad_up = jnp.einsum("th,tc->hc", chan_grad, normed_second, preferred_element_type=F32).astype(BF)
    grad_down = jnp.einsum("th,tc->hc", chan_act, cotangent, preferred_element_type=F32).astype(BF)
    g_chan = jnp.concatenate([grad_up.reshape(64, 24, 768), grad_down.reshape(64, 24, 768)], axis=1)
    hidden_up = jnp.einsum("pc,pj->cj", mix_cols_grad, whole_out, preferred_element_type=F32)
    hidden_grad = (hidden_up * hidden_slope).astype(BF)
    grad_first = jnp.einsum("pc,cj->pj", normed_cols, hidden_grad, preferred_element_type=F32).astype(BF)
    grad_second = jnp.einsum("pc,cj->pj", mix_cols_grad, token_act, preferred_element_type=F32).astype(BF)
    normed_cols_grad = jnp.einsum(
        "pj,cj->pc", whole_in, hidden_grad, preferred_element_type=F32
    ).astype(BF)
    grad_tok_in, grad_tok_out, both, normed_grad = sums(
        grad_first, grad_second, g_chan, normed_cols_grad, 3
    )
    core = lax.axis_index("dp") % 2
    grad_ch_in = lax.dynamic_slice_in_dim(both, 12 * core, 12, 0)
    grad_ch_out = lax.dynamic_slice_in_dim(both, 24 + 12 * core, 12, 0)
    grad_input = (
        middle_grad + norm_back(unit_first, scale_first, normed_grad.astype(F32))
    ).astype(BF)
    return (grad_input.reshape(6, 64, 768), grad_tok_in, grad_tok_out, grad_ch_in, grad_ch_out)


def solution(mesh):
    in_specs = (
        P("dp", "seq", None),
        P("dp", "seq", None),
        P("seq", None),
        P("seq", None),
        P(),
        P(),
    )
    out_specs = (
        P("dp", "seq", None),
        P(("seq", "dp"), None),
        P(("seq", "dp"), None),
        P(("seq", "dp"), None),
        P(("seq", "dp"), None),
    )
    return jax.shard_map(local, mesh=mesh, in_specs=in_specs, out_specs=out_specs, check_vma=False)
```

```python
import math

import jax
import jax.numpy as jnp
from jax import lax
from jax.experimental import pallas as pl
from jax.experimental.pallas import tpu as pltpu
from jax.sharding import PartitionSpec as P

BF = jnp.bfloat16
F32 = jnp.float32
MESH = pl.DeviceIdType.MESH
ANY = pl.BlockSpec(memory_space=pl.ANY)
LANES = 128


def normalize(values):
    center = values - jnp.mean(values, axis=-1, keepdims=True)
    inv_scale = lax.rsqrt(jnp.mean(center * center, axis=-1, keepdims=True) + 1e-05)
    return (center * inv_scale, inv_scale)


def norm_back(unit, inv_scale, upstream):
    first = jnp.mean(upstream, axis=-1, keepdims=True)
    second = jnp.mean(upstream * unit, axis=-1, keepdims=True)
    return inv_scale * (upstream - first - unit * second)


def gelu_pair(values):
    factor = math.sqrt(2.0 / math.pi)
    inner = factor * (values + 0.044715 * values * values * values)
    tangent = jnp.tanh(inner)
    result = 0.5 * values * (1.0 + tangent)
    slope = 0.5 * (1.0 + tangent) + 0.5 * values * (1.0 - tangent * tangent) * factor * (
        1.0 + 3.0 * 0.044715 * values * values
    )
    return (result, slope)


class Here:
    def __init__(self):
        self.q = lax.axis_index("seq")
        self.d = lax.axis_index("dp")
        self.y = self.q // 8
        self.xh = (self.q // 4) % 2
        self.z = self.q % 4
        self.xl = self.d // 2
        self.c = self.d % 2
        self.x = self.xh * 2 + self.xl

    def at(self, x=None, y=None, z=None, c=None):
        x = self.x if x is None else x
        y = self.y if y is None else y
        z = self.z if z is None else z
        c = self.c if c is None else c
        return {"seq": (y * 2 + x // 2) * 4 + z, "dp": (x % 2) * 2 + c}

    def peer(self, q):
        return {"seq": q, "dp": self.d}

    def sibling(self):
        return {"seq": self.q, "dp": self.d + 1 - 2 * self.c}

    def extra_of(self, e):
        return 8 * e + ((e + self.d // 2) % 2) * 4 + (e + self.d) % 4

    def has_extra(self):
        return self.q == self.extra_of(self.y)


def remote(src, dst, send, recv, device):
    return pltpu.make_async_remote_copy(
        src_ref=src, dst_ref=dst, send_sem=send, recv_sem=recv,
        device_id=device, device_id_type=MESH,
    )


def drain(ref, sem):
    pltpu.make_async_copy(ref, ref, sem).wait()


def greet(devices):
    barrier = pltpu.get_barrier_semaphore()
    for device in devices:
        pl.semaphore_signal(barrier, inc=1, device_id=device, device_id_type=MESH)
    return len(devices)


def greet_seq(here):
    barrier = pltpu.get_barrier_semaphore()

    def body(i, carry):
        pl.semaphore_signal(
            barrier, inc=1, device_id=here.peer((here.q + i) % 32), device_id_type=MESH
        )
        return carry

    lax.fori_loop(1, 32, body, 0)
    return 31


def rows(start, size):
    return pl.ds(pl.multiple_of(start * size, size), size)


TN = (((0,), (0,)), ((), ()))
NT = (((1,), (1,)), ((), ()))
NN = (((1,), (0,)), ((), ()))


def dot(a, b, dims):
    return lax.dot_general(a, b, dims, preferred_element_type=F32)


def lanes(start, size):
    return pl.ds(pl.multiple_of(start, LANES), size)


def block_of(ref, s, b):
    return ref.at[pl.ds(2 * s, 2), :, :, lanes(b * LANES, LANES)]


def column(ref, q, slot):
    return ref.at[pl.ds(2 * q, 2), :, :, pl.ds(slot * LANES, LANES)]


class ToChannels:
    def __init__(self, here, src, cols, sems):
        self.here, self.src, self.cols = here, src, cols
        self.send, self.recv, self.esend, self.erecv = sems

        @pl.when(jnp.logical_not(here.has_extra()))
        def _():
            cols[:, :, :, LANES:] = jnp.zeros((64, 2, 16, LANES), BF)

    def start(self, half):
        here, src, cols = self.here, self.src, self.cols
        first, count = ((0, 18), (18, 14))[half]

        def body(i, carry):
            dest = first + (i + here.q) % count
            block, place = block_of(src, dest // 6, dest % 6), column(cols, here.q, 0)

            @pl.when(dest != here.q)
            def _():
                remote(block, place, self.send, self.recv, here.peer(dest)).start()

            @pl.when(dest == here.q)
            def _():
                pltpu.make_async_copy(block, place, self.recv).start()

            return carry

        lax.fori_loop(0, count, body, 0)
        if half == 1:
            for e in range(4):
                dest = here.extra_of(e)
                block, place = block_of(src, 5, 2 + e), column(cols, here.q, 1)

                @pl.when(dest != here.q)
                def _():
                    remote(block, place, self.esend.at[e], self.erecv, here.peer(dest)).start()

                @pl.when(dest == here.q)
                def _():
                    pltpu.make_async_copy(block, place, self.erecv).start()

    def arrive(self):
        drain(self.cols.at[:, :, :, pl.ds(0, LANES)], self.recv)

        @pl.when(self.here.has_extra())
        def _():
            drain(self.cols.at[:, :, :, pl.ds(LANES, LANES)], self.erecv)

    def finish(self):
        drain(self.cols.at[pl.ds(0, 62), :, :, pl.ds(0, LANES)], self.send)
        for e in range(4):
            @pl.when(self.here.extra_of(e) != self.here.q)
            def _():
                drain(self.cols.at[pl.ds(0, 2), :, :, pl.ds(0, LANES)], self.esend.at[e])


class ToPatches:
    def __init__(self, here, cols, out, sems):
        self.here, self.cols, self.out = here, cols, out
        self.send, self.recv, self.esend = sems

    def start(self, dest):
        here, cols, out = self.here, self.cols, self.out
        place = block_of(out, here.q // 6, here.q % 6)
        extra = block_of(out, 5, 2 + here.y)
        sem = self.recv.at[here.q // 18]

        @pl.when(dest != here.q)
        def _():
            remote(column(cols, dest, 0), place, self.send, sem, here.peer(dest)).start()

            @pl.when(here.has_extra())
            def _():
                remote(
                    column(cols, dest, 1), extra, self.esend, self.recv.at[1], here.peer(dest)
                ).start()

        @pl.when(dest == here.q)
        def _():
            pltpu.make_async_copy(column(cols, dest, 0), place, sem).start()

            @pl.when(here.has_extra())
            def _():
                pltpu.make_async_copy(column(cols, dest, 1), extra, self.recv.at[1]).start()

    def arrive(self, half):
        drain(self.out.at[pl.ds(6 * half, 6)], self.recv.at[half])

    def finish(self):
        many = self.cols.at[pl.ds(0, 62), :, :, pl.ds(0, LANES)]
        drain(many, self.send)

        @pl.when(self.here.has_extra())
        def _():
            drain(many, self.esend)


class Gather:
    def __init__(self, here, parts, fulls, sems):
        self.here, self.fulls = here, fulls
        self.own, self.send, self.recv, self.bsend, self.brecv = sems
        self.copies = []
        c, y, xh, z = here.c, here.y, here.xh, here.z
        self.locals, self.cross = [], []
        for w in range(2):
            copy = pltpu.make_async_copy(parts[w], fulls[w].at[y, xh, z], self.own.at[w])
            copy.start()
            self.locals.append(copy)
            copy = remote(
                parts[w].at[c], fulls[w].at[y, xh, z, c], self.send.at[w, 0], self.recv.at[w, 0],
                here.at(x=(here.x + 2) % 4),
            )
            copy.start()
            self.cross.append(copy)
            self.copies.append(copy)

    def chunk(self, w, stage, pos, c, half=None):
        here, full = self.here, self.fulls[w]
        h = slice(None) if half is None else half
        if (stage == 0) == (w == 0):
            return full.at[here.y, h, pos, c] if stage == 0 else full.at[:, h, pos, c]
        return full.at[pos, h, here.z, c] if stage == 0 else full.at[pos, h, :, c]

    def place(self, w, stage):
        here = self.here
        along_z = (stage == 0) == (w == 0)
        me = here.z if along_z else here.y
        up, down, far = (me + 1) % 4, (me + 3) % 4, (me + 2) % 4
        name = "z" if along_z else "y"
        return me, up, down, far, here.at(**{name: up}), here.at(**{name: down})

    def push(self, w, k, ref, device):
        copy = remote(ref, ref, self.send.at[w, k], self.recv.at[w, k], device)
        copy.start()
        self.copies.append(copy)
        return copy

    def share(self, w, k, ref):
        copy = remote(ref, ref, self.bsend.at[w, k], self.brecv.at[w, k], self.here.sibling())
        copy.start()
        self.copies.append(copy)

    def crossed(self, w):
        here = self.here
        self.locals[w].wait()
        self.cross[w].wait_recv()
        self.share(w, 0, self.fulls[w].at[here.y, 1 - here.xh, here.z, here.c])

    def begin(self, w, stage):
        c, base = self.here.c, 1 + 4 * stage
        me, up, down, far, to_up, to_down = self.place(w, stage)
        return (
            self.push(w, base, self.chunk(w, stage, me, c), to_up),
            self.push(w, base + 1, self.chunk(w, stage, me, c), to_down),
        )

    def relay(self, w, stage, legs):
        c, base = self.here.c, 1 + 4 * stage
        me, up, down, far, to_up, to_down = self.place(w, stage)
        legs[0].wait_recv()
        one = self.push(w, base + 2, self.chunk(w, stage, down, c, 0), to_up)
        self.share(w, base, self.chunk(w, stage, down, c))
        legs[1].wait_recv()
        two = self.push(w, base + 3, self.chunk(w, stage, up, c, 1), to_down)
        self.share(w, base + 1, self.chunk(w, stage, up, c))
        return one, two

    def end(self, w, stage, legs):
        c, base = self.here.c, 1 + 4 * stage
        far = self.place(w, stage)[3]
        legs[0].wait_recv()
        self.share(w, base + 2, self.chunk(w, stage, far, c, 0))
        legs[1].wait_recv()
        self.share(w, base + 3, self.chunk(w, stage, far, c, 1))

    def shared(self, w):
        here = self.here
        other = 1 - here.c
        drain(self.fulls[w].at[here.y, 1 - here.xh, here.z, other], self.brecv.at[w, 0])
        for stage in range(2):
            base = 1 + 4 * stage
            me, up, down, far, _, _ = self.place(w, stage)
            drain(self.chunk(w, stage, down, other), self.brecv.at[w, base])
            drain(self.chunk(w, stage, up, other), self.brecv.at[w, base + 1])
            drain(self.chunk(w, stage, far, other, 0), self.brecv.at[w, base + 2])
            drain(self.chunk(w, stage, far, other, 1), self.brecv.at[w, base + 3])

    def finish(self):
        for copy in self.copies:
            copy.wait_send()


def add_into(target, other):
    lead = target.shape[:-2]
    count = math.prod(lead)

    def body(i, carry):
        index = []
        rest = i
        for size in reversed(lead):
            index.append(rest % size)
            rest = rest // size
        index = tuple(reversed(index))
        target[index] = (target[index].astype(F32) + other[index].astype(F32)).astype(BF)
        return carry

    if count == 1:
        index = (0,) * len(lead)
        target[index] = (target[index].astype(F32) + other[index].astype(F32)).astype(BF)
    else:
        lax.fori_loop(0, count, body, 0)


ORDERS = ("yzx", "zxy", "xyz")
TAILS = ((16, 1024), (16, 1024), (48, 384))


class RingSum:
    def __init__(self, here, p, acc, bufs, send, recv):
        self.here, self.p, self.acc, self.bufs = here, p, acc, bufs
        self.send, self.recv = send, recv
        self.copies = []

    def axis(self, stage):
        name = ORDERS[self.p][stage]
        me = getattr(self.here, name)
        up, down = (me + 1) % 4, (me + 3) % 4
        return me, up, down, self.here.at(**{name: up}), self.here.at(**{name: down})

    def chunk(self, stage, pos, half=None):
        here, order = self.here, ORDERS[self.p]
        index = {"y": slice(None), "xh": slice(None), "z": slice(None), "xl": slice(None)}
        for other in order[:stage]:
            if other == "x":
                index["xh"], index["xl"] = here.xh, here.xl
            else:
                index[other] = getattr(here, other)
        if order[stage] == "x":
            index["xh"], index["xl"] = pos // 2, pos % 2
        else:
            index[order[stage]] = pos
        tail = []
        if half is not None:
            for other in ("y", "xh", "z", "xl"):
                if isinstance(index[other], slice):
                    size = {"y": 4, "xh": 2, "z": 4, "xl": 2}[other]
                    index[other] = pl.ds(half * (size // 2), size // 2)
                    break
            else:
                if self.p < 2:
                    tail = [slice(None), pl.ds(half * 512, 512)]
                else:
                    tail = [pl.ds(16 * half, 16 + 16 * half)]
        return self.acc.at[tuple([index["y"], index["xh"], index["z"], index["xl"]] + tail)]

    def push(self, k, src, dst, device):
        copy = remote(src, dst, self.send.at[self.p, k], self.recv.at[self.p, k], device)
        copy.start()
        self.copies.append(copy)
        return copy

    def begin(self, stage):
        me, up, down, to_up, to_down = self.axis(stage)
        far, k = (me + 2) % 4, 4 * stage
        self.legs = (
            self.push(k, self.chunk(stage, far, 0), self.bufs[k], to_up),
            self.push(k + 1, self.chunk(stage, far, 1), self.bufs[k + 1], to_down),
        )

    def relay(self, stage):
        me, up, down, to_up, to_down = self.axis(stage)
        k = 4 * stage
        self.legs[0].wait_recv()
        add_into(self.chunk(stage, up, 0), self.bufs[k])
        one = self.push(k + 2, self.chunk(stage, up), self.bufs[k + 2], to_up)
        self.legs[1].wait_recv()
        add_into(self.chunk(stage, down, 1), self.bufs[k + 1])
        two = self.push(k + 3, self.chunk(stage, down), self.bufs[k + 3], to_down)
        self.legs = (one, two)

    def end(self, stage):
        k = 4 * stage
        self.legs[0].wait_recv()
        self.legs[1].wait_recv()
        mine = self.chunk(stage, self.axis(stage)[0])
        if stage < 2:
            add_into(mine, self.bufs[k + 2])
            add_into(mine, self.bufs[k + 3])
            return None
        return (
            mine[...].astype(F32) + self.bufs[k + 2][...].astype(F32)
            + self.bufs[k + 3][...].astype(F32)
        )

    def finish(self):
        for copy in self.copies:
            copy.wait_send()


def ring_buffers(p):
    shapes = []
    for stage in range(3):
        dims = {"y": 4, "xh": 2, "z": 4, "xl": 2}
        for name in ORDERS[p][:stage + 1]:
            for key in {"x": ("xh", "xl"), "y": ("y",), "z": ("z",)}[name]:
                del dims[key]
        lead, tail = list(dims.values()), list(TAILS[p])
        if lead:
            half = [lead[0] // 2] + lead[1:] + tail
            shapes += [half, half]
        elif p < 2:
            shapes += [[16, 512], [16, 512]]
        else:
            shapes += [[16, 384], [32, 384]]
        shapes += [lead + tail] * 2
    return [pltpu.VMEM(tuple(s), BF) for s in shapes]


DMA = pltpu.SemaphoreType.DMA
SCRATCH = {
    "win": ((4, 2, 4, 2, 32, 1024), BF), "wout": ((4, 2, 4, 2, 32, 1024), BF),
    "chin": ((1536, 768), BF), "chout": ((1536, 768), BF),
    "normed": ((12, 2, 16, 768), BF), "tm": ((12, 2, 16, 768), BF), "ng": ((12, 2, 16, 768), BF),
    "mixg": ((12, 2, 16, 768), BF), "ns": ((384, 768), BF), "mg": ((384, 768), F32),
    "cact": ((384, 1536), BF), "cgrad": ((384, 1536), BF),
    "cact_s": ((384, 1536), BF), "cgrad_s": ((384, 1536), BF),
    "ns_s": ((384, 384), BF), "cot_s": ((384, 384), BF),
    "second": ((192, 768), F32),
    "cols": ((64, 2, 16, 256), BF), "cols2": ((64, 2, 16, 256), BF),
    "cols_s": ((64, 16, 256), BF), "cols2_s": ((64, 16, 256), BF),
    "hidden": ((256, 1024), F32), "slope": ((256, 1024), F32),
    "act": ((256, 1024), BF), "act_s": ((256, 1024), BF),
    "hg": ((256, 1024), BF), "hg_s": ((256, 1024), BF),
    "mixb": ((64, 2, 16, 256), BF), "ncg": ((64, 2, 16, 256), BF),
    "g0": ((4, 2, 4, 2, 16, 1024), BF), "g1": ((4, 2, 4, 2, 16, 1024), BF),
    "g2": ((4, 2, 4, 2, 48, 384), BF),
    "fin": ((4, 48, 384), F32),
}
SEMS = {
    "load": (2,), "a1_send": (), "a1_recv": (), "a1_esend": (4,), "a1_erecv": (),
    "a3_send": (), "a3_recv": (), "a3_esend": (4,), "a3_erecv": (),
    "a2_send": (), "a2_recv": (2,), "a2_esend": (),
    "a4_send": (), "a4_recv": (2,), "a4_esend": (),
    "w_own": (2,), "w_send": (2, 9), "w_recv": (2, 9), "w_bsend": (2, 9), "w_brecv": (2, 9),
    "r_send": (3, 12), "r_recv": (3, 12),
    "s_send": (11,), "s_recv": (11,), "f_send": (3,), "f_recv": (3,),
}


def block_kernel(spectra, cot, w_in, w_out, ch_in, ch_out, grad_input, o0, o1, o2, *scratch):
    v = dict(zip(list(SCRATCH) + list(SEMS), scratch))
    bufs = scratch[len(v):]
    here = Here()
    c = here.c
    sib = here.sibling()
    cross = here.at(x=here.xh * 2 + 1 - here.xl, c=1 - c)
    count = greet_seq(here) + greet(
        [sib, here.at(x=(here.x + 1) % 4), here.at(x=(here.x + 3) % 4), cross]
    )
    loads = [
        pltpu.make_async_copy(ch_in, v["chin"], v["load"].at[0]),
        pltpu.make_async_copy(ch_out, v["chout"], v["load"].at[1]),
    ]
    for copy in loads:
        copy.start()
    pl.semaphore_wait(pltpu.get_barrier_semaphore(), count)

    shared = []

    def share(src, dst):
        k = len(shared)
        copy = remote(src, dst, v["s_send"].at[k], v["s_recv"].at[k], sib)
        copy.start()
        shared.append(copy)
        return copy

    gather = Gather(
        here, (w_in, w_out), (v["win"], v["wout"]),
        (v["w_own"], v["w_send"], v["w_recv"], v["w_bsend"], v["w_brecv"]),
    )
    share_cot = share(cot.at[:, lanes(384 * (1 - c), 384)], v["cot_s"])

    first = ToChannels(
        here, v["normed"], v["cols"], (v["a1_send"], v["a1_recv"], v["a1_esend"], v["a1_erecv"])
    )
    for half in range(2):
        def norm_first(i, carry):
            at = half * 6 + i
            unit, _ = normalize(spectra[rows(at, 32), :].astype(F32))
            v["normed"][at] = unit.astype(BF).reshape(2, 16, 768)
            return carry

        lax.fori_loop(0, 6, norm_first, 0)
        first.start(half)

    for w in range(2):
        gather.crossed(w)
    legs = [gather.begin(w, 0) for w in range(2)]
    legs = [gather.relay(w, 0, legs[w]) for w in range(2)]
    for w in range(2):
        gather.end(w, 0, legs[w])
    legs = [gather.begin(w, 1) for w in range(2)]
    legs = [gather.relay(w, 1, legs[w]) for w in range(2)]
    gather.end(0, 1, legs[0])
    gather.shared(0)
    first.arrive()
    share_cols = share(v["cols"].at[:, 1 - c], v["cols_s"])

    def project(source, target):
        def body(weight):
            def step(y, carry):
                left = source[pl.ds(16 * y, 16)].reshape(512, 256)
                part = dot(left, weight[y].reshape(512, 1024), TN)

                @pl.when(y == 0)
                def _():
                    target[...] = part

                @pl.when(y != 0)
                def _():
                    target[...] += part

                return carry

            lax.fori_loop(0, 4, step, 0)
        return body

    project(v["cols"], v["hidden"])(v["win"])

    def token_gelu(i, carry):
        at = rows(i, 16)
        value, slope = gelu_pair(v["hidden"][at, :])
        v["act"][at, :] = value.astype(BF)
        v["slope"][at, :] = slope
        return carry

    lax.fori_loop(0, 16, token_gelu, 0)
    share_act = share(v["act"], v["act_s"])
    gather.end(1, 1, legs[1])
    gather.shared(1)

    def spread(weight, source, target, transfer):
        def step(i, carry):
            part = (here.y * 2 + here.xh + i) % 8
            left = weight[part // 2, part % 2].reshape(256, 1024)
            value = dot(left, source[...], NT).astype(BF)
            target[pl.ds(8 * part, 8)] = value.reshape(8, 2, 16, 256)
            for k in range(4):
                transfer.start(4 * part + (here.z + k) % 4)
            return carry

        lax.fori_loop(0, 8, step, 0)

    second = ToPatches(
        here, v["mixb"], v["tm"], (v["a2_send"], v["a2_recv"], v["a2_esend"])
    )
    spread(v["wout"], v["act"], v["mixb"], second)

    for copy in loads:
        copy.wait()
    third = ToChannels(
        here, v["mixg"], v["cols2"], (v["a3_send"], v["a3_recv"], v["a3_esend"], v["a3_erecv"])
    )

    def middle_of(at):
        source = spectra[rows(at, 32), :].astype(F32)
        mix = v["tm"][at].reshape(32, 768).astype(F32)
        return (source + mix).astype(BF).astype(F32)

    for half in range(2):
        second.arrive(half)
        span = pl.ds(192 * half, 192)

        def norm_second(i, carry):
            at = half * 6 + i
            v["ns"][rows(at, 32), :] = normalize(middle_of(at))[0].astype(BF)
            return carry

        lax.fori_loop(0, 6, norm_second, 0)

        def hidden_units(i, carry):
            part = lanes(256 * i, 256)
            own = rows(i, 256)
            value, slope = gelu_pair(dot(v["ns"][span, :], v["chin"][own, :], NT))
            down = dot(cot[span, :], v["chout"][own, :], NT)
            v["cact"][span, part] = value.astype(BF)
            v["cgrad"][span, part] = (down * slope).astype(BF)
            return carry

        lax.fori_loop(0, 6, hidden_units, 0)
        for name in ("cgrad", "cact"):
            share(v[name].at[span], v[name + "_s"].at[span])
        share(v["ns"].at[span, lanes(384 * (1 - c), 384)], v["ns_s"].at[span])
        v["second"][...] = dot(v["cgrad"][span, :], v["chin"][...], NN)

        def back_second(i, carry):
            at = half * 6 + i
            unit, scale = normalize(middle_of(at))
            upstream = v["second"][rows(i, 32), :]
            value = cot[rows(at, 32), :].astype(F32) + norm_back(unit, scale, upstream)
            v["mg"][rows(at, 32), :] = value
            v["mixg"][at] = value.astype(BF).reshape(2, 16, 768)
            return carry

        lax.fori_loop(0, 6, back_second, 0)
        third.start(half)

    for copy in shared:
        copy.wait_recv()
    half_lanes = lanes(384 * c, 384)
    for g, (act, tok, act_s, tok_s) in enumerate((
        ("cgrad", v["ns"], "cgrad_s", "ns_s"), ("cact", cot, "cact_s", "cot_s"),
    )):
        def channel_sum(y, carry):
            part = lanes(384 * y, 384)
            total = dot(v[act][:, part], tok[:, half_lanes], TN)
            total += dot(v[act_s][:, part], v[tok_s][...], TN)
            v["g2"][y, :, :, g] = total.astype(BF).reshape(2, 4, 48, 384)
            return carry

        lax.fori_loop(0, 4, channel_sum, 0)

    rings = [
        RingSum(here, p, v["g%d" % p], bufs[12 * p:12 * p + 12], v["r_send"], v["r_recv"])
        for p in range(3)
    ]
    rings[2].begin(0)

    third.arrive()
    share_cols2 = share(v["cols2"].at[:, 1 - c], v["cols2_s"])
    project(v["cols2"], v["hidden"])(v["wout"])

    def token_grad(i, carry):
        at = rows(i, 16)
        v["hg"][at, :] = (v["hidden"][at, :] * v["slope"][at, :]).astype(BF)
        return carry

    lax.fori_loop(0, 16, token_grad, 0)
    share_hg = share(v["hg"], v["hg_s"])
    rings[2].relay(0)

    def token_sum(target, left, left_s, right, right_s):
        def step(y, carry):
            own = v[left][pl.ds(16 * y, 16), c].reshape(256, 256)
            other = v[left_s][pl.ds(16 * y, 16)].reshape(256, 256)
            total = dot(own, v[right][...], NN) + dot(other, v[right_s][...], NN)
            v[target][y] = total.astype(BF).reshape(2, 4, 2, 16, 1024)
            return carry

        lax.fori_loop(0, 4, step, 0)

    share_cols2.wait_recv()
    token_sum("g1", "cols2", "cols2_s", "act", "act_s")
    rings[1].begin(0)
    share_hg.wait_recv()
    token_sum("g0", "cols", "cols_s", "hg", "hg_s")
    rings[0].begin(0)
    fourth = ToPatches(
        here, v["ncg"], v["ng"], (v["a4_send"], v["a4_recv"], v["a4_esend"])
    )
    spread(v["win"], v["hg"], v["ncg"], fourth)

    rings[1].relay(0)
    rings[0].relay(0)
    rings[2].end(0)
    rings[2].begin(1)

    def input_grad(half):
        fourth.arrive(half)

        def step(i, carry):
            at = half * 6 + i
            unit, scale = normalize(spectra[rows(at, 32), :].astype(F32))
            upstream = v["ng"][at].reshape(32, 768).astype(F32)
            value = v["mg"][rows(at, 32), :] + norm_back(unit, scale, upstream)
            grad_input[rows(at, 32), :] = value.astype(BF)
            return carry

        lax.fori_loop(0, 6, step, 0)

    input_grad(0)
    rings[2].relay(1)
    input_grad(1)
    rings[2].end(1)
    rings[2].begin(2)
    rings[1].end(0)
    rings[1].begin(1)
    rings[0].end(0)
    rings[0].begin(1)
    rings[2].relay(2)
    rings[1].relay(1)
    rings[0].relay(1)
    v["fin"][here.d] = rings[2].end(2)
    swaps = []
    for k, device in enumerate((sib, here.at(x=here.xh * 2 + 1 - here.xl), cross)):
        copy = remote(
            v["fin"].at[here.d], v["fin"].at[here.d], v["f_send"].at[k], v["f_recv"].at[k], device
        )
        copy.start()
        swaps.append(copy)
    rings[1].end(1)
    rings[1].begin(2)
    rings[0].end(1)
    rings[0].begin(2)
    rings[1].relay(2)
    rings[0].relay(2)
    for copy in swaps:
        copy.wait()
    for g in range(2):
        for k in range(2):
            o2[g, :, 384 * k:384 * k + 384] = v["fin"][2 * g + k]
    o1[...] = rings[1].end(2)
    o0[...] = rings[0].end(2)

    gather.finish()
    for ring in rings:
        ring.finish()
    for copy in shared:
        copy.wait_send()
    for transfer in (first, second, third, fourth):
        transfer.finish()


def local(spectra_in, cotangent, tok_in_w, tok_out_w, ch_in_w, ch_out_w):
    vmem = pl.BlockSpec(memory_space=pltpu.VMEM)
    scratch = [pltpu.VMEM(shape, kind) for shape, kind in SCRATCH.values()]
    scratch += [DMA(shape) if shape else DMA for shape in SEMS.values()]
    for p in range(3):
        scratch += ring_buffers(p)
    grad_input, grad_tok_in, grad_tok_out, both = pl.pallas_call(
        block_kernel,
        out_shape=(
            jax.ShapeDtypeStruct((384, 768), BF),
            jax.ShapeDtypeStruct((16, 1024), F32),
            jax.ShapeDtypeStruct((16, 1024), F32),
            jax.ShapeDtypeStruct((2, 48, 768), F32),
        ),
        in_specs=[vmem, vmem, ANY, ANY, ANY, ANY], out_specs=(vmem,) * 4,
        scratch_shapes=scratch,
        compiler_params=pltpu.CompilerParams(
            collective_id=0, has_side_effects=True, vmem_limit_bytes=60 * 1024 * 1024
        ),
        name="mixer_block_backward",
    )(
        spectra_in.reshape(384, 768), cotangent.reshape(384, 768),
        tok_in_w.reshape(2, 32, 1024), tok_out_w.reshape(2, 32, 1024), ch_in_w, ch_out_w,
    )
    own = lax.dynamic_slice_in_dim(both, 12 * lax.axis_index("dp"), 12, 1)
    return (grad_input.reshape(6, 64, 768), grad_tok_in, grad_tok_out, own[0], own[1])


def solution(mesh):
    in_specs = (
        P("dp", "seq", None),
        P("dp", "seq", None),
        P("seq", None),
        P("seq", None),
        P(),
        P(),
    )
    out_specs = (
        P("dp", "seq", None),
        P(("seq", "dp"), None),
        P(("seq", "dp"), None),
        P(("seq", "dp"), None),
        P(("seq", "dp"), None),
    )
    return jax.shard_map(local, mesh=mesh, in_specs=in_specs, out_specs=out_specs, check_vma=False)
```

```python
import math

import jax
import jax.numpy as jnp
from jax import lax
from jax.experimental import pallas as pl
from jax.experimental.pallas import tpu as pltpu
from jax.sharding import PartitionSpec as P

BF = jnp.bfloat16
F32 = jnp.float32
MESH = pl.DeviceIdType.MESH
ANY = pl.BlockSpec(memory_space=pl.ANY)
LANES = 128


def normalize(values):
    center = values - jnp.mean(values, axis=-1, keepdims=True)
    inv_scale = lax.rsqrt(jnp.mean(center * center, axis=-1, keepdims=True) + 1e-05)
    return (center * inv_scale, inv_scale)


def norm_back(unit, inv_scale, upstream):
    first = jnp.mean(upstream, axis=-1, keepdims=True)
    second = jnp.mean(upstream * unit, axis=-1, keepdims=True)
    return inv_scale * (upstream - first - unit * second)


def gelu_pair(values):
    factor = math.sqrt(2.0 / math.pi)
    inner = factor * (values + 0.044715 * values * values * values)
    tangent = jnp.tanh(inner)
    result = 0.5 * values * (1.0 + tangent)
    slope = 0.5 * (1.0 + tangent) + 0.5 * values * (1.0 - tangent * tangent) * factor * (
        1.0 + 3.0 * 0.044715 * values * values
    )
    return (result, slope)


class Here:
    def __init__(self):
        self.q = lax.axis_index("seq")
        self.d = lax.axis_index("dp")
        self.y = self.q // 8
        self.xh = (self.q // 4) % 2
        self.z = self.q % 4
        self.xl = self.d // 2
        self.c = self.d % 2
        self.x = self.xh * 2 + self.xl

    def at(self, x=None, y=None, z=None, c=None):
        x = self.x if x is None else x
        y = self.y if y is None else y
        z = self.z if z is None else z
        c = self.c if c is None else c
        return {"seq": (y * 2 + x // 2) * 4 + z, "dp": (x % 2) * 2 + c}

    def peer(self, q):
        return {"seq": q, "dp": self.d}

    def sibling(self):
        return {"seq": self.q, "dp": self.d + 1 - 2 * self.c}

    def extra_of(self, e):
        return 8 * e + ((e + self.d // 2) % 2) * 4 + (e + self.d) % 4

    def has_extra(self):
        return self.q == self.extra_of(self.y)


def remote(src, dst, send, recv, device):
    return pltpu.make_async_remote_copy(
        src_ref=src, dst_ref=dst, send_sem=send, recv_sem=recv,
        device_id=device, device_id_type=MESH,
    )


def drain(ref, sem):
    pltpu.make_async_copy(ref, ref, sem).wait()


def greet(devices):
    barrier = pltpu.get_barrier_semaphore()
    for device in devices:
        pl.semaphore_signal(barrier, inc=1, device_id=device, device_id_type=MESH)
    return len(devices)


def greet_seq(here):
    barrier = pltpu.get_barrier_semaphore()

    def body(i, carry):
        pl.semaphore_signal(
            barrier, inc=1, device_id=here.peer((here.q + i) % 32), device_id_type=MESH
        )
        return carry

    lax.fori_loop(1, 32, body, 0)
    return 31


def rows(start, size):
    return pl.ds(pl.multiple_of(start * size, size), size)


TN = (((0,), (0,)), ((), ()))
NT = (((1,), (1,)), ((), ()))
NN = (((1,), (0,)), ((), ()))


def dot(a, b, dims):
    return lax.dot_general(a, b, dims, preferred_element_type=F32)


def lanes(start, size):
    return pl.ds(pl.multiple_of(start, LANES), size)


def block_of(ref, s, b):
    return ref.at[pl.ds(2 * s, 2), :, :, lanes(b * LANES, LANES)]


def column(ref, q, slot):
    return ref.at[pl.ds(2 * q, 2), :, :, pl.ds(slot * LANES, LANES)]


class ToChannels:
    def __init__(self, here, src, cols, sems):
        self.here, self.src, self.cols = here, src, cols
        self.send, self.recv, self.esend, self.erecv = sems

        @pl.when(jnp.logical_not(here.has_extra()))
        def _():
            cols[:, :, :, LANES:] = jnp.zeros((64, 2, 16, LANES), BF)

    def start(self, half):
        here, src, cols = self.here, self.src, self.cols
        first, count = ((0, 18), (18, 14))[half]

        def body(i, carry):
            dest = first + (i + here.q) % count
            block, place = block_of(src, dest // 6, dest % 6), column(cols, here.q, 0)

            @pl.when(dest != here.q)
            def _():
                remote(block, place, self.send, self.recv, here.peer(dest)).start()

            @pl.when(dest == here.q)
            def _():
                pltpu.make_async_copy(block, place, self.recv).start()

            return carry

        lax.fori_loop(0, count, body, 0)
        if half == 1:
            for e in range(4):
                dest = here.extra_of(e)
                block, place = block_of(src, 5, 2 + e), column(cols, here.q, 1)

                @pl.when(dest != here.q)
                def _():
                    remote(block, place, self.esend.at[e], self.erecv, here.peer(dest)).start()

                @pl.when(dest == here.q)
                def _():
                    pltpu.make_async_copy(block, place, self.erecv).start()

    def arrive(self):
        drain(self.cols.at[:, :, :, pl.ds(0, LANES)], self.recv)

        @pl.when(self.here.has_extra())
        def _():
            drain(self.cols.at[:, :, :, pl.ds(LANES, LANES)], self.erecv)

    def finish(self):
        drain(self.cols.at[pl.ds(0, 62), :, :, pl.ds(0, LANES)], self.send)
        for e in range(4):
            @pl.when(self.here.extra_of(e) != self.here.q)
            def _():
                drain(self.cols.at[pl.ds(0, 2), :, :, pl.ds(0, LANES)], self.esend.at[e])


class ToPatches:
    def __init__(self, here, cols, out, sems):
        self.here, self.cols, self.out = here, cols, out
        self.send, self.recv, self.esend = sems

    def start(self, dest):
        here, cols, out = self.here, self.cols, self.out
        place = block_of(out, here.q // 6, here.q % 6)
        extra = block_of(out, 5, 2 + here.y)
        sem = self.recv.at[here.q // 18]

        @pl.when(dest != here.q)
        def _():
            remote(column(cols, dest, 0), place, self.send, sem, here.peer(dest)).start()

            @pl.when(here.has_extra())
            def _():
                remote(
                    column(cols, dest, 1), extra, self.esend, self.recv.at[1], here.peer(dest)
                ).start()

        @pl.when(dest == here.q)
        def _():
            pltpu.make_async_copy(column(cols, dest, 0), place, sem).start()

            @pl.when(here.has_extra())
            def _():
                pltpu.make_async_copy(column(cols, dest, 1), extra, self.recv.at[1]).start()

    def arrive(self, half):
        drain(self.out.at[pl.ds(6 * half, 6)], self.recv.at[half])

    def finish(self):
        many = self.cols.at[pl.ds(0, 62), :, :, pl.ds(0, LANES)]
        drain(many, self.send)

        @pl.when(self.here.has_extra())
        def _():
            drain(many, self.esend)


class Gather:
    def __init__(self, here, parts, fulls, sems):
        self.here, self.fulls = here, fulls
        self.own, self.send, self.recv, self.bsend, self.brecv = sems
        self.copies = []
        self.legs = [{}, {}]
        c, y, xh, z = here.c, here.y, here.xh, here.z
        self.locals, self.cross = [], []
        for w in range(2):
            copy = pltpu.make_async_copy(parts[w], fulls[w].at[y, xh, z], self.own.at[w])
            copy.start()
            self.locals.append(copy)
            copy = remote(
                parts[w].at[c], fulls[w].at[y, xh, z, c], self.send.at[w, 0], self.recv.at[w, 0],
                here.at(x=(here.x + 2) % 4),
            )
            copy.start()
            self.cross.append(copy)
            self.copies.append(copy)

    def names(self, w):
        return ("z", "y") if w == 0 else ("y", "z")

    def piece(self, w, first, second, c, half=None):
        here = self.here
        a, b = self.names(w)
        at = {a: (getattr(here, a) + first) % 4, b: (getattr(here, b) + second) % 4}
        h = slice(None) if half is None else half
        return self.fulls[w].at[at["y"], h, at["z"], c]

    def towards(self, w, axis, step):
        name = self.names(w)[axis]
        return self.here.at(**{name: (getattr(self.here, name) + step) % 4})

    def push(self, w, k, ref, device):
        copy = remote(ref, ref, self.send.at[w, k], self.recv.at[w, k], device)
        copy.start()
        self.copies.append(copy)
        self.legs[w][k] = copy

    def share(self, w, k, ref):
        copy = remote(ref, ref, self.bsend.at[w, k], self.brecv.at[w, k], self.here.sibling())
        copy.start()
        self.copies.append(copy)

    def crossed(self, w):
        here = self.here
        self.locals[w].wait()
        self.cross[w].wait_recv()
        self.share(w, 0, self.fulls[w].at[here.y, 1 - here.xh, here.z, here.c])
        own = self.piece(w, 0, 0, here.c)
        self.push(w, 1, own, self.towards(w, 0, 1))
        self.push(w, 2, own, self.towards(w, 0, 3))
        self.second(w, 0)

    def second(self, w, o):
        ref = self.piece(w, o, 0, self.here.c)
        self.push(w, 5 + 4 * o, ref, self.towards(w, 1, 1))
        self.push(w, 6 + 4 * o, ref, self.towards(w, 1, 3))

    def first_near(self, w):
        c = self.here.c
        self.legs[w][1].wait_recv()
        self.push(w, 3, self.piece(w, 3, 0, c, 0), self.towards(w, 0, 1))
        self.share(w, 1, self.piece(w, 3, 0, c))
        self.second(w, 3)
        self.legs[w][2].wait_recv()
        self.push(w, 4, self.piece(w, 1, 0, c, 1), self.towards(w, 0, 3))
        self.share(w, 2, self.piece(w, 1, 0, c))
        self.second(w, 1)

    def first_far(self, w):
        self.legs[w][3].wait_recv()
        self.legs[w][4].wait_recv()
        self.share(w, 3, self.piece(w, 2, 0, self.here.c))
        self.second(w, 2)

    def second_near(self, w, o):
        c = self.here.c
        self.legs[w][5 + 4 * o].wait_recv()
        self.push(w, 7 + 4 * o, self.piece(w, o, 3, c, 0), self.towards(w, 1, 1))
        self.share(w, 4 + 3 * o, self.piece(w, o, 3, c))
        self.legs[w][6 + 4 * o].wait_recv()
        self.push(w, 8 + 4 * o, self.piece(w, o, 1, c, 1), self.towards(w, 1, 3))
        self.share(w, 5 + 3 * o, self.piece(w, o, 1, c))

    def second_far(self, w, o):
        self.legs[w][7 + 4 * o].wait_recv()
        self.legs[w][8 + 4 * o].wait_recv()
        self.share(w, 6 + 3 * o, self.piece(w, o, 2, self.here.c))

    def shared_near(self, w):
        here = self.here
        other = 1 - here.c
        drain(self.fulls[w].at[here.y, 1 - here.xh, here.z, other], self.brecv.at[w, 0])
        for k, o in ((1, 3), (2, 1), (3, 2)):
            drain(self.piece(w, o, 0, other), self.brecv.at[w, k])
        for o in range(4):
            drain(self.piece(w, o, 3, other), self.brecv.at[w, 4 + 3 * o])
            drain(self.piece(w, o, 1, other), self.brecv.at[w, 5 + 3 * o])

    def shared_far(self, w):
        for o in range(4):
            drain(self.piece(w, o, 2, 1 - self.here.c), self.brecv.at[w, 6 + 3 * o])

    def finish(self):
        for copy in self.copies:
            copy.wait_send()


def add_into(target, *others):
    lead = target.shape[:-2]

    def body(i, carry):
        index = []
        rest = i
        for size in reversed(lead):
            index.append(rest % size)
            rest = rest // size
        index = tuple(reversed(index))
        total = target[index].astype(F32)
        for other in others:
            total += other[index].astype(F32)
        target[index] = total.astype(BF)
        return carry

    lax.fori_loop(0, math.prod(lead), body, 0)


PARTS = (
    ("x", 48, 128), ("y", 48, 128), ("z", 48, 128),
    ("y", 16, 640), ("z", 16, 768), ("x", 16, 640),
)
PLANES = {"x": ("y", "z"), "y": ("x", "z"), "z": ("x", "y")}


class PartSum:
    def __init__(self, here, p, acc, bufs, send, recv):
        self.here, self.p, self.acc = here, p, acc
        self.low, self.high, self.up_buf, self.down_buf, self.plane_buf = bufs
        self.send, self.recv = send, recv
        self.copies = []
        self.axis = PARTS[p][0]
        self.me = getattr(here, self.axis)

    def index(self, at):
        full = slice(None)
        if "x" in at:
            return (at.get("y", full), at["x"] // 2, at.get("z", full), at["x"] % 2)
        return (at.get("y", full), full, at.get("z", full), full)

    def chunk(self, pos, half=None):
        index = list(self.index({self.axis: pos}))
        if half is not None:
            if self.axis == "y":
                index[1] = half
            else:
                index[0] = pl.ds(2 * half, 2)
        return self.acc.at[tuple(index)]

    def to(self, step):
        return self.here.at(**{self.axis: (self.me + step) % 4})

    def push(self, k, src, dst, device):
        copy = remote(src, dst, self.send.at[self.p, k], self.recv.at[self.p, k], device)
        copy.start()
        self.copies.append(copy)
        return copy

    def begin(self):
        far = (self.me + 2) % 4
        self.legs = (
            self.push(0, self.chunk(far, 0), self.low, self.to(1)),
            self.push(1, self.chunk(far, 1), self.high, self.to(3)),
        )

    def relay(self):
        up, down = (self.me + 1) % 4, (self.me + 3) % 4
        self.legs[0].wait_recv()
        add_into(self.chunk(up, 0), self.low)
        one = self.push(2, self.chunk(up), self.up_buf, self.to(1))
        self.legs[1].wait_recv()
        add_into(self.chunk(down, 1), self.high)
        two = self.push(3, self.chunk(down), self.down_buf, self.to(3))
        self.legs = (one, two)

    def spot(self, pos):
        a, b = PLANES[self.axis]
        return {a: pos // 4, b: pos % 4}

    def cross(self):
        self.legs[0].wait_recv()
        self.legs[1].wait_recv()
        add_into(self.chunk(self.me), self.up_buf, self.down_buf)
        a, b = PLANES[self.axis]
        self.pos = getattr(self.here, a) * 4 + getattr(self.here, b)

        def step(k, carry):
            spot = self.spot((self.pos + k) % 16)
            block = self.acc.at[self.index({self.axis: self.me, **spot})]
            remote(
                block, self.plane_buf.at[self.pos], self.send.at[self.p, 4],
                self.recv.at[self.p, 4], self.here.at(**spot),
            ).start()
            return carry

        lax.fori_loop(1, 16, step, 0)
        own = self.acc[self.index({self.axis: self.me, **self.spot(self.pos)})]
        self.plane_buf[self.pos] = own

    def end(self):
        drain(self.plane_buf.at[pl.ds(0, 15)], self.recv.at[self.p, 4])
        total = self.plane_buf[0].astype(F32)
        for k in range(1, 16):
            total += self.plane_buf[k].astype(F32)
        return total

    def finish(self):
        for copy in self.copies:
            copy.wait_send()
        drain(self.plane_buf.at[pl.ds(0, 15)], self.send.at[self.p, 4])


def part_shape(p):
    return (4, 2, 4, 2) + PARTS[p][1:]


def part_buffers(p):
    axis, tail = PARTS[p][0], PARTS[p][1:]
    whole = {"x": (4, 4), "y": (2, 4, 2), "z": (4, 2, 2)}[axis]
    half = whole[1:] if axis == "y" else (2,) + whole[1:]
    shapes = [half + tail, half + tail, whole + tail, whole + tail, (16,) + tail]
    return [pltpu.VMEM(s, BF) for s in shapes]


DMA = pltpu.SemaphoreType.DMA
SCRATCH = {
    "win": ((4, 2, 4, 2, 32, 1024), BF), "wout": ((4, 2, 4, 2, 32, 1024), BF),
    "chin": ((1536, 768), BF), "chout": ((1536, 768), BF),
    "normed": ((12, 2, 16, 768), BF), "tm": ((12, 2, 16, 768), BF), "ng": ((12, 2, 16, 768), BF),
    "mixg": ((12, 2, 16, 768), BF), "ns": ((384, 768), BF), "mg": ((384, 768), F32),
    "cact": ((384, 1536), BF), "cgrad": ((384, 1536), BF),
    "cact_s": ((384, 1536), BF), "cgrad_s": ((384, 1536), BF),
    "ns_s": ((384, 384), BF), "cot_s": ((384, 384), BF),
    "second": ((192, 768), F32),
    "cols": ((64, 2, 16, 256), BF), "cols2": ((64, 2, 16, 256), BF),
    "cols_s": ((64, 16, 256), BF), "cols2_s": ((64, 16, 256), BF),
    "hidden": ((256, 1024), F32), "slope": ((256, 1024), F32),
    "act": ((256, 1024), BF), "act_s": ((256, 1024), BF),
    "hg": ((256, 1024), BF), "hg_s": ((256, 1024), BF),
    "mixb": ((64, 2, 16, 256), BF), "ncg": ((64, 2, 16, 256), BF),
    **{"g%d" % p: (part_shape(p), BF) for p in range(6)},
    "fin": ((4, 48, 384), F32),
}
SEMS = {
    "load": (2,), "a1_send": (), "a1_recv": (), "a1_esend": (4,), "a1_erecv": (),
    "a3_send": (), "a3_recv": (), "a3_esend": (4,), "a3_erecv": (),
    "a2_send": (), "a2_recv": (2,), "a2_esend": (),
    "a4_send": (), "a4_recv": (2,), "a4_esend": (),
    "w_own": (2,), "w_send": (2, 21), "w_recv": (2, 21), "w_bsend": (2, 16), "w_brecv": (2, 16),
    "r_send": (6, 5), "r_recv": (6, 5),
    "s_send": (11,), "s_recv": (11,), "f_send": (3,), "f_recv": (3,),
}


def block_kernel(
    spectra, cot, w_in, w_out, ch_in, ch_out, grad_input, o0, o1, o2, o3, *scratch
):
    v = dict(zip(list(SCRATCH) + list(SEMS), scratch))
    bufs = scratch[len(v):]
    here = Here()
    c = here.c
    sib = here.sibling()
    cross = here.at(x=here.xh * 2 + 1 - here.xl, c=1 - c)
    partners = [sib, cross]
    for k in (1, 3):
        x = (here.x + k) % 4
        partners += [here.at(x=x, z=(here.z + n) % 4) for n in range(4)]
        partners += [here.at(x=x, y=(here.y + n) % 4) for n in range(1, 4)]
    count = greet_seq(here) + greet(partners)
    loads = [
        pltpu.make_async_copy(ch_in, v["chin"], v["load"].at[0]),
        pltpu.make_async_copy(ch_out, v["chout"], v["load"].at[1]),
    ]
    for copy in loads:
        copy.start()

    def norm_first(i, carry):
        unit, _ = normalize(spectra[rows(i, 32), :].astype(F32))
        v["normed"][i] = unit.astype(BF).reshape(2, 16, 768)
        return carry

    lax.fori_loop(0, 12, norm_first, 0, unroll=2)
    pl.semaphore_wait(pltpu.get_barrier_semaphore(), count)

    shared = []

    def share(src, dst):
        k = len(shared)
        copy = remote(src, dst, v["s_send"].at[k], v["s_recv"].at[k], sib)
        copy.start()
        shared.append(copy)
        return copy

    gather = Gather(
        here, (w_in, w_out), (v["win"], v["wout"]),
        (v["w_own"], v["w_send"], v["w_recv"], v["w_bsend"], v["w_brecv"]),
    )
    first = ToChannels(
        here, v["normed"], v["cols"], (v["a1_send"], v["a1_recv"], v["a1_esend"], v["a1_erecv"])
    )
    first.start(0)
    first.start(1)
    share(cot.at[:, lanes(384 * (1 - c), 384)], v["cot_s"])
    both = range(2)
    for w in both:
        gather.crossed(w)
    for w in both:
        gather.first_near(w)
    for w in both:
        gather.second_near(w, 0)
    for w in both:
        gather.first_far(w)
    for o in (3, 1):
        for w in both:
            gather.second_near(w, o)
    for w in both:
        gather.second_near(w, 2)
    first.arrive()
    share(v["cols"].at[:, 1 - c], v["cols_s"])
    gather.shared_near(0)

    def project(source, weight, y, start):
        left = source[pl.ds(16 * y, 16)].reshape(512, 256)
        part = dot(left, weight[y].reshape(512, 1024), TN)
        if start:
            v["hidden"][...] = part
        else:
            v["hidden"][...] += part

    project(v["cols"], v["win"], here.y, True)
    lax.fori_loop(
        0, 2, lambda i, carry: project(v["cols"], v["win"], (here.y + 1 + 2 * i) % 4, False), None
    )
    for o in (0, 3, 1, 2):
        gather.second_far(0, o)
    gather.shared_far(0)
    project(v["cols"], v["win"], (here.y + 2) % 4, False)

    def token_gelu(i, carry):
        at = rows(i, 16)
        value, slope = gelu_pair(v["hidden"][at, :])
        v["act"][at, :] = value.astype(BF)
        v["slope"][at, :] = slope
        return carry

    lax.fori_loop(0, 16, token_gelu, 0)
    share(v["act"], v["act_s"])

    def spread(weight, source, target, transfer, z):
        def step(y, carry):
            left = weight[y, :, z].reshape(128, 1024)
            value = dot(left, source[...], NT).astype(BF).reshape(2, 2, 2, 16, 256)
            for xh in range(2):
                dest = 8 * y + 4 * xh + z
                target[pl.ds(2 * dest, 2)] = value[xh]
                transfer.start(dest)
            return carry

        lax.fori_loop(0, 4, lambda i, carry: step((here.y + i) % 4, carry), 0)

    second = ToPatches(
        here, v["mixb"], v["tm"], (v["a2_send"], v["a2_recv"], v["a2_esend"])
    )
    gather.shared_near(1)
    lax.fori_loop(
        0, 3,
        lambda i, carry: spread(
            v["wout"], v["act"], v["mixb"], second, (here.z + i + i // 2) % 4
        ),
        None,
    )
    for o in (0, 3, 1, 2):
        gather.second_far(1, o)
    gather.shared_far(1)
    spread(v["wout"], v["act"], v["mixb"], second, (here.z + 2) % 4)

    for copy in loads:
        copy.wait()
    third = ToChannels(
        here, v["mixg"], v["cols2"], (v["a3_send"], v["a3_recv"], v["a3_esend"], v["a3_erecv"])
    )

    def middle_of(at):
        source = spectra[rows(at, 32), :].astype(F32)
        mix = v["tm"][at].reshape(32, 768).astype(F32)
        return (source + mix).astype(BF).astype(F32)

    for half in range(2):
        second.arrive(half)
        span = pl.ds(192 * half, 192)

        def norm_second(i, carry):
            at = half * 6 + i
            v["ns"][rows(at, 32), :] = normalize(middle_of(at))[0].astype(BF)
            return carry

        lax.fori_loop(0, 6, norm_second, 0, unroll=2)

        def hidden_units(i, carry):
            part = lanes(256 * i, 256)
            own = rows(i, 256)
            value, slope = gelu_pair(dot(v["ns"][span, :], v["chin"][own, :], NT))
            down = dot(cot[span, :], v["chout"][own, :], NT)
            v["cact"][span, part] = value.astype(BF)
            v["cgrad"][span, part] = (down * slope).astype(BF)
            return carry

        lax.fori_loop(0, 6, hidden_units, 0)
        for name in ("cgrad", "cact"):
            share(v[name].at[span], v[name + "_s"].at[span])
        share(v["ns"].at[span, lanes(384 * (1 - c), 384)], v["ns_s"].at[span])
        v["second"][...] = dot(v["cgrad"][span, :], v["chin"][...], NN)

        def back_second(i, carry):
            at = half * 6 + i
            unit, scale = normalize(middle_of(at))
            upstream = v["second"][rows(i, 32), :]
            value = cot[rows(at, 32), :].astype(F32) + norm_back(unit, scale, upstream)
            v["mg"][rows(at, 32), :] = value
            v["mixg"][at] = value.astype(BF).reshape(2, 16, 768)
            return carry

        lax.fori_loop(0, 6, back_second, 0, unroll=2)
        third.start(half)

    for copy in shared:
        copy.wait_recv()
    half_lanes = lanes(384 * c, 384)
    for g, (act, tok, act_s, tok_s) in enumerate((
        ("cgrad", v["ns"], "cgrad_s", "ns_s"), ("cact", cot, "cact_s", "cot_s"),
    )):
        def channel_sum(y, carry):
            part = lanes(384 * y, 384)
            total = dot(v[act][:, part], tok[:, half_lanes], TN)
            total += dot(v[act_s][:, part], v[tok_s][...], TN)
            total = total.astype(BF).reshape(2, 4, 48, 384)
            for p in range(3):
                v["g%d" % p][y, :, :, g] = total[..., 128 * p:128 * p + 128]
            return carry

        lax.fori_loop(0, 4, channel_sum, 0)

    parts = [
        PartSum(here, p, v["g%d" % p], bufs[5 * p:5 * p + 5], v["r_send"], v["r_recv"])
        for p in range(6)
    ]
    channel_parts, token_parts = parts[:3], parts[3:]
    for part in channel_parts:
        part.begin()

    third.arrive()
    share_cols2 = share(v["cols2"].at[:, 1 - c], v["cols2_s"])
    project(v["cols2"], v["wout"], 0, True)
    lax.fori_loop(1, 4, lambda y, carry: project(v["cols2"], v["wout"], y, False), None)

    def token_grad(i, carry):
        at = rows(i, 16)
        v["hg"][at, :] = (v["hidden"][at, :] * v["slope"][at, :]).astype(BF)
        return carry

    lax.fori_loop(0, 16, token_grad, 0)
    share_hg = share(v["hg"], v["hg_s"])
    for part in channel_parts:
        part.relay()

    def token_sum(left, left_s, right, right_s, targets):
        def step(y, carry):
            own = v[left][pl.ds(16 * y, 16), c].reshape(256, 256)
            other = v[left_s][pl.ds(16 * y, 16)].reshape(256, 256)
            total = dot(own, v[right][...], NN) + dot(other, v[right_s][...], NN)
            total = total.astype(BF).reshape(2, 4, 2, 16, 1024)
            for name, place, take in targets:
                v[name][y, :, :, :, :, place] = total[..., take]
            return carry

        lax.fori_loop(0, 4, step, 0)

    share_cols2.wait_recv()
    token_sum(
        "cols2", "cols2_s", "act", "act_s",
        (("g3", pl.ds(0, 640), slice(0, 640)), ("g4", pl.ds(0, 384), slice(640, 1024))),
    )
    token_parts[0].begin()
    share_hg.wait_recv()
    token_sum(
        "cols", "cols_s", "hg", "hg_s",
        (("g4", pl.ds(384, 384), slice(0, 384)), ("g5", pl.ds(0, 640), slice(384, 1024))),
    )
    token_parts[1].begin()
    token_parts[2].begin()
    fourth = ToPatches(
        here, v["ncg"], v["ng"], (v["a4_send"], v["a4_recv"], v["a4_esend"])
    )
    lax.fori_loop(
        0, 4, lambda i, carry: spread(v["win"], v["hg"], v["ncg"], fourth, (here.z + i) % 4), None
    )
    for part in token_parts:
        part.relay()
    for part in channel_parts:
        part.cross()

    def input_grad(half):
        fourth.arrive(half)

        def step(i, carry):
            at = half * 6 + i
            unit, scale = normalize(spectra[rows(at, 32), :].astype(F32))
            upstream = v["ng"][at].reshape(32, 768).astype(F32)
            value = v["mg"][rows(at, 32), :] + norm_back(unit, scale, upstream)
            grad_input[rows(at, 32), :] = value.astype(BF)
            return carry

        lax.fori_loop(0, 6, step, 0, unroll=2)

    input_grad(0)
    input_grad(1)
    for part in token_parts:
        part.cross()
    for p, part in enumerate(channel_parts):
        v["fin"][here.d, :, 128 * p:128 * p + 128] = part.end()
    swaps = []
    for k, device in enumerate((sib, here.at(x=here.xh * 2 + 1 - here.xl), cross)):
        copy = remote(
            v["fin"].at[here.d], v["fin"].at[here.d], v["f_send"].at[k], v["f_recv"].at[k], device
        )
        copy.start()
        swaps.append(copy)
    o1[:, 0:640] = token_parts[0].end()
    middle = token_parts[1].end()
    o1[:, 640:1024] = middle[:, 0:384]
    o0[:, 0:384] = middle[:, 384:768]
    o0[:, 384:1024] = token_parts[2].end()
    for copy in swaps:
        copy.wait()
    for d in range(4):
        @pl.when(here.d == d)
        def _():
            for out, g in ((o2, 0), (o3, 2)):
                for k in range(2):
                    out[:, 384 * k:384 * k + 384] = v["fin"][g + k, 12 * d:12 * d + 12]

    gather.finish()
    for part in parts:
        part.finish()
    for copy in shared:
        copy.wait_send()
    for transfer in (first, second, third, fourth):
        transfer.finish()


def hand_over(*refs):
    for src, dst in zip(refs[:5], refs[5:]):
        dst[...] = src[...]


def local(spectra_in, cotangent, tok_in_w, tok_out_w, ch_in_w, ch_out_w):
    vmem = pl.BlockSpec(memory_space=pltpu.VMEM)
    scratch = [pltpu.VMEM(shape, kind) for shape, kind in SCRATCH.values()]
    scratch += [DMA(shape) if shape else DMA for shape in SEMS.values()]
    for p in range(6):
        scratch += part_buffers(p)
    shapes = (
        jax.ShapeDtypeStruct((384, 768), BF),
        jax.ShapeDtypeStruct((16, 1024), F32),
        jax.ShapeDtypeStruct((16, 1024), F32),
        jax.ShapeDtypeStruct((12, 768), F32),
        jax.ShapeDtypeStruct((12, 768), F32),
    )
    outs = pl.pallas_call(
        block_kernel,
        out_shape=shapes,
        in_specs=[vmem, vmem, ANY, ANY, ANY, ANY], out_specs=(vmem,) * 5,
        scratch_shapes=scratch,
        compiler_params=pltpu.CompilerParams(
            collective_id=0, has_side_effects=True, vmem_limit_bytes=60 * 1024 * 1024
        ),
        name="mixer_block_backward",
    )(
        spectra_in.reshape(384, 768), cotangent.reshape(384, 768),
        tok_in_w.reshape(2, 32, 1024), tok_out_w.reshape(2, 32, 1024), ch_in_w, ch_out_w,
    )
    grad_input, *weights = pl.pallas_call(
        hand_over, out_shape=shapes, in_specs=[vmem] * 5, out_specs=(vmem,) * 5, name="hand_over",
    )(*outs)
    return (grad_input.reshape(6, 64, 768), *weights)


def solution(mesh):
    in_specs = (
        P("dp", "seq", None),
        P("dp", "seq", None),
        P("seq", None),
        P("seq", None),
        P(),
        P(),
    )
    out_specs = (
        P("dp", "seq", None),
        P(("seq", "dp"), None),
        P(("seq", "dp"), None),
        P(("seq", "dp"), None),
        P(("seq", "dp"), None),
    )
    return jax.shard_map(local, mesh=mesh, in_specs=in_specs, out_specs=out_specs, check_vma=False)
```

```python
import math

import jax
import jax.numpy as jnp
from jax import lax
from jax.experimental import pallas as pl
from jax.experimental.pallas import tpu as pltpu
from jax.sharding import PartitionSpec as P

BF = jnp.bfloat16
F32 = jnp.float32
MESH = pl.DeviceIdType.MESH
ANY = pl.BlockSpec(memory_space=pl.ANY)
LANES = 128


def normalize(values):
    center = values - jnp.mean(values, axis=-1, keepdims=True)
    inv_scale = lax.rsqrt(jnp.mean(center * center, axis=-1, keepdims=True) + 1e-05)
    return (center * inv_scale, inv_scale)


def norm_back(unit, inv_scale, upstream):
    first = jnp.mean(upstream, axis=-1, keepdims=True)
    second = jnp.mean(upstream * unit, axis=-1, keepdims=True)
    return inv_scale * (upstream - first - unit * second)


def gelu_pair(values):
    factor = math.sqrt(2.0 / math.pi)
    inner = factor * (values + 0.044715 * values * values * values)
    tangent = jnp.tanh(inner)
    result = 0.5 * values * (1.0 + tangent)
    slope = 0.5 * (1.0 + tangent) + 0.5 * values * (1.0 - tangent * tangent) * factor * (
        1.0 + 3.0 * 0.044715 * values * values
    )
    return (result, slope)


class Here:
    def __init__(self):
        self.q = lax.axis_index("seq")
        self.d = lax.axis_index("dp")
        self.y = self.q // 8
        self.xh = (self.q // 4) % 2
        self.z = self.q % 4
        self.xl = self.d // 2
        self.c = self.d % 2
        self.x = self.xh * 2 + self.xl

    def at(self, x=None, y=None, z=None, c=None):
        x = self.x if x is None else x
        y = self.y if y is None else y
        z = self.z if z is None else z
        c = self.c if c is None else c
        return {"seq": (y * 2 + x // 2) * 4 + z, "dp": (x % 2) * 2 + c}

    def peer(self, q):
        return {"seq": q, "dp": self.d}

    def sibling(self):
        return {"seq": self.q, "dp": self.d + 1 - 2 * self.c}

    def extra_of(self, e):
        return 8 * e + ((e + self.d // 2) % 2) * 4 + (e + self.d) % 4

    def has_extra(self):
        return self.q == self.extra_of(self.y)


def remote(src, dst, send, recv, device):
    return pltpu.make_async_remote_copy(
        src_ref=src, dst_ref=dst, send_sem=send, recv_sem=recv,
        device_id=device, device_id_type=MESH,
    )


def drain(ref, sem):
    pltpu.make_async_copy(ref, ref, sem).wait()


def greet(devices):
    barrier = pltpu.get_barrier_semaphore()
    for device in devices:
        pl.semaphore_signal(barrier, inc=1, device_id=device, device_id_type=MESH)
    return len(devices)


def greet_seq(here):
    barrier = pltpu.get_barrier_semaphore()

    def body(i, carry):
        pl.semaphore_signal(
            barrier, inc=1, device_id=here.peer((here.q + i) % 32), device_id_type=MESH
        )
        return carry

    lax.fori_loop(1, 32, body, 0)
    return 31


def rows(start, size):
    return pl.ds(pl.multiple_of(start * size, size), size)


TN = (((0,), (0,)), ((), ()))
NT = (((1,), (1,)), ((), ()))
NN = (((1,), (0,)), ((), ()))


def dot(a, b, dims):
    return lax.dot_general(a, b, dims, preferred_element_type=F32)


def lanes(start, size):
    return pl.ds(pl.multiple_of(start, LANES), size)


def block_of(ref, s, b):
    return ref.at[pl.ds(2 * s, 2), :, :, lanes(b * LANES, LANES)]


def column(ref, q, slot):
    return ref.at[pl.ds(2 * q, 2), :, :, pl.ds(slot * LANES, LANES)]


class ToChannels:
    def __init__(self, here, src, cols, sems):
        self.here, self.src, self.cols = here, src, cols
        self.send, self.recv, self.esend, self.erecv = sems

        @pl.when(jnp.logical_not(here.has_extra()))
        def _():
            cols[:, :, :, LANES:] = jnp.zeros((64, 2, 16, LANES), BF)

    def start(self, half):
        here, src, cols = self.here, self.src, self.cols
        first, count = ((0, 18), (18, 14))[half]

        def body(i, carry):
            dest = first + (i + here.q) % count
            block, place = block_of(src, dest // 6, dest % 6), column(cols, here.q, 0)

            @pl.when(dest != here.q)
            def _():
                remote(block, place, self.send, self.recv, here.peer(dest)).start()

            @pl.when(dest == here.q)
            def _():
                pltpu.make_async_copy(block, place, self.recv).start()

            return carry

        lax.fori_loop(0, count, body, 0)
        if half == 1:
            for e in range(4):
                dest = here.extra_of(e)
                block, place = block_of(src, 5, 2 + e), column(cols, here.q, 1)

                @pl.when(dest != here.q)
                def _():
                    remote(block, place, self.esend.at[e], self.erecv, here.peer(dest)).start()

                @pl.when(dest == here.q)
                def _():
                    pltpu.make_async_copy(block, place, self.erecv).start()

    def arrive(self):
        drain(self.cols.at[:, :, :, pl.ds(0, LANES)], self.recv)

        @pl.when(self.here.has_extra())
        def _():
            drain(self.cols.at[:, :, :, pl.ds(LANES, LANES)], self.erecv)

    def finish(self):
        drain(self.cols.at[pl.ds(0, 62), :, :, pl.ds(0, LANES)], self.send)
        for e in range(4):
            @pl.when(self.here.extra_of(e) != self.here.q)
            def _():
                drain(self.cols.at[pl.ds(0, 2), :, :, pl.ds(0, LANES)], self.esend.at[e])


class ToPatches:
    def __init__(self, here, cols, out, sems):
        self.here, self.cols, self.out = here, cols, out
        self.send, self.recv, self.esend = sems

    def start(self, dest):
        here, cols, out = self.here, self.cols, self.out
        place = block_of(out, here.q // 6, here.q % 6)
        extra = block_of(out, 5, 2 + here.y)
        sem = self.recv.at[here.q // 18]

        @pl.when(dest != here.q)
        def _():
            remote(column(cols, dest, 0), place, self.send, sem, here.peer(dest)).start()

            @pl.when(here.has_extra())
            def _():
                remote(
                    column(cols, dest, 1), extra, self.esend, self.recv.at[1], here.peer(dest)
                ).start()

        @pl.when(dest == here.q)
        def _():
            pltpu.make_async_copy(column(cols, dest, 0), place, sem).start()

            @pl.when(here.has_extra())
            def _():
                pltpu.make_async_copy(column(cols, dest, 1), extra, self.recv.at[1]).start()

    def arrive(self, half):
        drain(self.out.at[pl.ds(6 * half, 6)], self.recv.at[half])

    def finish(self):
        many = self.cols.at[pl.ds(0, 62), :, :, pl.ds(0, LANES)]
        drain(many, self.send)

        @pl.when(self.here.has_extra())
        def _():
            drain(many, self.esend)


class Gather:
    def __init__(self, here, parts, fulls, sems):
        self.here, self.fulls, self.parts = here, fulls, parts
        self.own, self.send, self.recv, self.bsend, self.brecv = sems
        self.copies = []
        self.legs = [{}, {}]
        c, y, xh, z = here.c, here.y, here.xh, here.z
        self.locals = []
        for w in range(2):
            copy = pltpu.make_async_copy(parts[w], fulls[w].at[y, xh, z], self.own.at[w])
            copy.start()
            self.locals.append(copy)
            self.push(w, 0, fulls[w].at[y, xh, z, c], here.at(x=(here.x + 2) % 4), parts[w].at[c])

    def piece(self, w, first, second, c, half=None):
        here = self.here
        y = (here.y + c * first + (1 - c) * second) % 4
        z = (here.z + (1 - c) * first + c * second) % 4
        h = slice(None) if half is None else half
        return self.fulls[w].at[y, h, z, c]

    def towards(self, axis, step):
        here = self.here
        along_y = here.c if axis == 0 else 1 - here.c
        return here.at(y=(here.y + along_y * step) % 4, z=(here.z + (1 - along_y) * step) % 4)

    def push(self, w, k, ref, device, src=None):
        copy = remote(
            ref if src is None else src, ref, self.send.at[w, k], self.recv.at[w, k], device
        )
        copy.start()
        self.copies.append(copy)
        self.legs[w][k] = copy

    def share(self, w, k, ref):
        copy = remote(ref, ref, self.bsend.at[w, k], self.brecv.at[w, k], self.here.sibling())
        copy.start()
        self.copies.append(copy)

    def around(self, w, ks, half, src=None):
        ref = self.piece(w, 0, 0, self.here.c, half)
        for k, axis, step in zip(ks, (0, 0, 1, 1), (1, 3, 1, 3)):
            self.push(w, k, ref, self.towards(axis, step), src)

    def launch(self, w):
        self.around(w, (1, 2, 5, 6), self.here.xh, self.parts[w].at[self.here.c])

    def crossed(self, w):
        here = self.here
        self.legs[w][0].wait_recv()
        self.around(w, (21, 22, 23, 24), 1 - here.xh)
        self.share(w, 0, self.piece(w, 0, 0, here.c, 1 - here.xh))
        self.locals[w].wait()

    def second(self, w, o):
        ref = self.piece(w, o, 0, self.here.c)
        self.push(w, 5 + 4 * o, ref, self.towards(1, 1))
        self.push(w, 6 + 4 * o, ref, self.towards(1, 3))

    def first_near(self, w):
        c = self.here.c
        self.legs[w][1].wait_recv()
        self.legs[w][21].wait_recv()
        self.push(w, 3, self.piece(w, 3, 0, c, 0), self.towards(0, 1))
        self.second(w, 3)
        self.share(w, 1, self.piece(w, 3, 0, c))
        self.legs[w][2].wait_recv()
        self.legs[w][22].wait_recv()
        self.push(w, 4, self.piece(w, 1, 0, c, 1), self.towards(0, 3))
        self.second(w, 1)
        self.share(w, 2, self.piece(w, 1, 0, c))

    def first_far(self, w):
        self.legs[w][3].wait_recv()
        self.legs[w][4].wait_recv()
        self.second(w, 2)
        self.share(w, 3, self.piece(w, 2, 0, self.here.c))

    def second_near(self, w, o):
        c = self.here.c
        self.legs[w][5 + 4 * o].wait_recv()
        if o == 0:
            self.legs[w][23].wait_recv()
        self.push(w, 7 + 4 * o, self.piece(w, o, 3, c, 0), self.towards(1, 1))
        self.share(w, 4 + 3 * o, self.piece(w, o, 3, c))
        self.legs[w][6 + 4 * o].wait_recv()
        if o == 0:
            self.legs[w][24].wait_recv()
        self.push(w, 8 + 4 * o, self.piece(w, o, 1, c, 1), self.towards(1, 3))
        self.share(w, 5 + 3 * o, self.piece(w, o, 1, c))

    def second_far(self, w, o):
        self.legs[w][7 + 4 * o].wait_recv()
        self.legs[w][8 + 4 * o].wait_recv()
        self.share(w, 6 + 3 * o, self.piece(w, o, 2, self.here.c))

    def shared_near(self, w):
        other = 1 - self.here.c
        drain(self.piece(w, 0, 0, other, 1 - self.here.xh), self.brecv.at[w, 0])
        for k, o in ((1, 3), (2, 1), (3, 2)):
            drain(self.piece(w, o, 0, other), self.brecv.at[w, k])
        for o in range(4):
            drain(self.piece(w, o, 3, other), self.brecv.at[w, 4 + 3 * o])
            drain(self.piece(w, o, 1, other), self.brecv.at[w, 5 + 3 * o])

    def shared_far(self, w):
        for o in range(4):
            drain(self.piece(w, o, 2, 1 - self.here.c), self.brecv.at[w, 6 + 3 * o])

    def finish(self):
        for copy in self.copies:
            copy.wait_send()


def add_into(target, *others):
    lead = target.shape[:-2]

    def body(i, carry):
        index = []
        rest = i
        for size in reversed(lead):
            index.append(rest % size)
            rest = rest // size
        index = tuple(reversed(index))
        total = target[index].astype(F32)
        for other in others:
            total += other[index].astype(F32)
        target[index] = total.astype(BF)
        return carry

    lax.fori_loop(0, math.prod(lead), body, 0, unroll=4)


PARTS = (
    ("x", 48, 128), ("y", 48, 128), ("z", 48, 128),
    ("y", 16, 384), ("z", 16, 384), ("x", 16, 256),
    ("y", 16, 256), ("z", 16, 384), ("x", 16, 384),
)
PLANES = {"x": ("y", "z"), "y": ("z", "x"), "z": ("x", "y")}


class PartSum:
    def __init__(self, here, p, acc, bufs, send, recv):
        self.here, self.p, self.acc = here, p, acc
        self.low, self.high, self.up_buf, self.down_buf, self.turn_buf, self.end_buf = bufs
        self.send, self.recv = send, recv
        self.copies = []
        self.axis = PARTS[p][0]
        self.me = getattr(here, self.axis)

    def index(self, at):
        full = slice(None)
        if "x" in at:
            return (at.get("y", full), at["x"] // 2, at.get("z", full), at["x"] % 2)
        return (at.get("y", full), full, at.get("z", full), full)

    def chunk(self, pos, half=None):
        index = list(self.index({self.axis: pos}))
        if half is not None:
            if self.axis == "y":
                index[1] = half
            else:
                index[0] = pl.ds(2 * half, 2)
        return self.acc.at[tuple(index)]

    def to(self, step):
        return self.here.at(**{self.axis: (self.me + step) % 4})

    def push(self, k, src, dst, device):
        copy = remote(src, dst, self.send.at[self.p, k], self.recv.at[self.p, k], device)
        copy.start()
        self.copies.append(copy)
        return copy

    def begin(self):
        far = (self.me + 2) % 4
        self.legs = (
            self.push(0, self.chunk(far, 0), self.low, self.to(1)),
            self.push(1, self.chunk(far, 1), self.high, self.to(3)),
        )

    def relay(self):
        up, down = (self.me + 1) % 4, (self.me + 3) % 4
        self.legs[0].wait_recv()
        add_into(self.chunk(up, 0), self.low)
        one = self.push(2, self.chunk(up), self.up_buf, self.to(1))
        self.legs[1].wait_recv()
        add_into(self.chunk(down, 1), self.high)
        two = self.push(3, self.chunk(down), self.down_buf, self.to(3))
        self.legs = (one, two)

    def across(self, k, name, buf, at):
        me = getattr(self.here, name)
        for step in (1, 3, 2):
            pos = (me + step) % 4
            remote(
                self.acc.at[self.index({**at, name: pos})], buf.at[me],
                self.send.at[self.p, k], self.recv.at[self.p, k], self.here.at(**{name: pos}),
            ).start()

    def cross(self):
        self.legs[0].wait_recv()
        self.legs[1].wait_recv()
        add_into(self.chunk(self.me), self.up_buf, self.down_buf)
        self.across(4, PLANES[self.axis][0], self.turn_buf, {self.axis: self.me})

    def turn(self):
        a, b = PLANES[self.axis]
        me = getattr(self.here, a)
        at = {self.axis: self.me, a: me}
        drain(self.turn_buf.at[pl.ds(0, 3)], self.recv.at[self.p, 4])
        add_into(
            self.acc.at[self.index(at)], *[self.turn_buf.at[(me + k) % 4] for k in (1, 2, 3)]
        )
        self.across(5, b, self.end_buf, at)

    def end(self):
        a, b = PLANES[self.axis]
        me = getattr(self.here, b)
        at = {self.axis: self.me, a: getattr(self.here, a), b: me}
        drain(self.end_buf.at[pl.ds(0, 3)], self.recv.at[self.p, 5])
        total = self.acc[self.index(at)].astype(F32)
        for k in (1, 2, 3):
            total += self.end_buf[(me + k) % 4].astype(F32)
        return total

    def finish(self):
        for copy in self.copies:
            copy.wait_send()
        drain(self.turn_buf.at[pl.ds(0, 3)], self.send.at[self.p, 4])
        drain(self.end_buf.at[pl.ds(0, 3)], self.send.at[self.p, 5])


def part_shape(p):
    return (4, 2, 4, 2) + PARTS[p][1:]


def part_buffers(p):
    axis, tail = PARTS[p][0], PARTS[p][1:]
    whole = {"x": (4, 4), "y": (2, 4, 2), "z": (4, 2, 2)}[axis]
    half = whole[1:] if axis == "y" else (2,) + whole[1:]
    last = (2, 2) if PLANES[axis][1] == "x" else (4,)
    shapes = [half + tail] * 2 + [whole + tail] * 2 + [(4,) + last + tail, (4,) + tail]
    return [pltpu.VMEM(s, BF) for s in shapes]


DMA = pltpu.SemaphoreType.DMA
SCRATCH = {
    "spectra": ((384, 768), BF), "cot": ((384, 768), BF), "grad_input": ((384, 768), BF),
    "win": ((4, 2, 4, 2, 32, 1024), BF), "wout": ((4, 2, 4, 2, 32, 1024), BF),
    "chin": ((1536, 768), BF), "chout": ((1536, 768), BF),
    "normed": ((12, 2, 16, 768), BF), "tm": ((12, 2, 16, 768), BF), "ng": ((12, 2, 16, 768), BF),
    "mixg": ((12, 2, 16, 768), BF), "ns": ((384, 768), BF), "mg": ((384, 768), F32),
    "cact": ((384, 1536), BF), "cgrad": ((384, 1536), BF),
    "cact_s": ((384, 1536), BF), "cgrad_s": ((384, 1536), BF),
    "ns_s": ((384, 384), BF), "cot_s": ((384, 384), BF),
    "cols_t": ((256, 2048), BF), "second": ((192, 768), F32), "down": ((384, 1536), F32),
    "cols": ((64, 2, 16, 256), BF), "cols2": ((64, 2, 16, 256), BF),
    "cols_s": ((64, 16, 256), BF), "cols2_s": ((64, 16, 256), BF),
    "hidden": ((256, 1024), F32), "slope": ((256, 1024), F32),
    "act": ((256, 1024), BF), "act_s": ((256, 1024), BF),
    "hg": ((256, 1024), BF), "hg_s": ((256, 1024), BF),
    "mixb": ((64, 2, 16, 256), BF), "ncg": ((64, 2, 16, 256), BF),
    **{"g%d" % p: (part_shape(p), BF) for p in range(len(PARTS))},
    "fin": ((4, 48, 384), F32), "sum0": ((16, 1024), F32), "sum1": ((16, 1024), F32),
    "sum2": ((12, 768), F32), "sum3": ((12, 768), F32),
}
SEMS = {
    "load": (5,), "a1_send": (), "a1_recv": (), "a1_esend": (4,), "a1_erecv": (),
    "a3_send": (), "a3_recv": (), "a3_esend": (4,), "a3_erecv": (),
    "a2_send": (), "a2_recv": (2,), "a2_esend": (),
    "a4_send": (), "a4_recv": (2,), "a4_esend": (),
    "w_own": (2,), "w_send": (2, 25), "w_recv": (2, 25), "w_bsend": (2, 16), "w_brecv": (2, 16),
    "r_send": (9, 6), "r_recv": (9, 6),
    "s_send": (11,), "s_recv": (11,), "f_send": (3,), "f_recv": (3,),
}


def block_kernel(
    spectra_in, cot_in, w_in, w_out, ch_in, ch_out, grad_out, o0, o1, o2, o3, *scratch
):
    v = dict(zip(list(SCRATCH) + list(SEMS), scratch))
    spectra, cot, grad_input = v["spectra"], v["cot"], v["grad_input"]
    bufs = scratch[len(v):]
    here = Here()
    c = here.c
    sib = here.sibling()
    cross = here.at(x=here.xh * 2 + 1 - here.xl, c=1 - c)
    partners = [sib, cross]
    for k in (1, 3):
        x = (here.x + k) % 4
        partners += [here.at(x=x, z=(here.z + n) % 4) for n in range(4)]
        partners += [here.at(x=x, y=(here.y + n) % 4) for n in range(1, 4)]
    count = greet_seq(here) + greet(partners)
    loads = [
        pltpu.make_async_copy(src, dst, v["load"].at[k])
        for k, (src, dst) in enumerate((
            (spectra_in, spectra), (cot_in, cot), (ch_in, v["chin"]), (ch_out, v["chout"]),
        ))
    ]
    for copy in loads:
        copy.start()
    loads.pop(0).wait()

    def norm_first(i, carry):
        unit, _ = normalize(spectra[rows(i, 32), :].astype(F32))
        v["normed"][i] = unit.astype(BF).reshape(2, 16, 768)
        return carry

    lax.fori_loop(0, 12, norm_first, 0, unroll=4)
    pl.semaphore_wait(pltpu.get_barrier_semaphore(), count)

    shared = []

    def share(src, dst):
        k = len(shared)
        copy = remote(src, dst, v["s_send"].at[k], v["s_recv"].at[k], sib)
        copy.start()
        shared.append(copy)
        return copy

    gather = Gather(
        here, (w_in, w_out), (v["win"], v["wout"]),
        (v["w_own"], v["w_send"], v["w_recv"], v["w_bsend"], v["w_brecv"]),
    )
    first = ToChannels(
        here, v["normed"], v["cols"], (v["a1_send"], v["a1_recv"], v["a1_esend"], v["a1_erecv"])
    )
    both = range(2)
    for w in both:
        gather.launch(w)
    first.start(0)
    first.start(1)
    for w in both:
        gather.crossed(w)
    for copy in loads:
        copy.wait()
    share(cot.at[:, lanes(384 * (1 - c), 384)], v["cot_s"])

    def channel_down(i, carry):
        v["down"][:, lanes(256 * i, 256)] = dot(cot[...], v["chout"][rows(i, 256), :], NT)
        return carry

    for w in both:
        gather.first_near(w)
    lax.fori_loop(0, 3, channel_down, 0)
    for w in both:
        gather.second_near(w, 0)
    for w in both:
        gather.first_far(w)
    lax.fori_loop(3, 6, channel_down, 0)
    for o in (3, 1):
        for w in both:
            gather.second_near(w, o)
    first.arrive()
    share(v["cols"].at[:, 1 - c], v["cols_s"])
    for w in both:
        gather.second_near(w, 2)

    def turn_cols(y, carry):
        v["cols_t"][:, lanes(512 * y, 512)] = v["cols"][pl.ds(16 * y, 16)].reshape(512, 256).T
        return carry

    lax.fori_loop(0, 4, turn_cols, 0)
    for o in (0, 3, 1, 2):
        gather.second_far(0, o)
    gather.shared_near(0)
    gather.shared_far(0)

    def project(source, weight):
        def step(y, start):
            left = source[pl.ds(16 * y, 16)].reshape(512, 256)
            part = dot(left, weight[y].reshape(512, 1024), TN)
            if start:
                v["hidden"][...] = part
            else:
                v["hidden"][...] += part

        step(0, True)
        lax.fori_loop(1, 4, lambda y, carry: step(y, False), None)

    def hidden_of(i, carry):
        part = lanes(256 * i, 256)
        weight = v["win"][:, :, :, :, :, part].reshape(2048, 256)
        v["hidden"][:, part] = dot(v["cols_t"][...], weight, NN)
        return carry

    lax.fori_loop(0, 4, hidden_of, 0)

    def token_gelu(i, carry):
        at = rows(i, 16)
        value, slope = gelu_pair(v["hidden"][at, :])
        v["act"][at, :] = value.astype(BF)
        v["slope"][at, :] = slope
        return carry

    lax.fori_loop(0, 16, token_gelu, 0, unroll=4)
    share(v["act"], v["act_s"])

    def spread(weight, source, target, transfer, spots):
        left = jnp.concatenate([weight[y, :, z].reshape(128, 1024) for y, z in spots], axis=0)
        value = dot(left, source[...], NT).astype(BF).reshape(len(spots), 2, 2, 2, 16, 256)
        for k, (y, z) in enumerate(spots):
            for xh in range(2):
                dest = 8 * y + 4 * xh + z
                target[pl.ds(2 * dest, 2)] = value[k, xh]
                transfer.start(dest)

    def off(name, step):
        return (getattr(here, name) + step) % 4

    second = ToPatches(
        here, v["mixb"], v["tm"], (v["a2_send"], v["a2_recv"], v["a2_esend"])
    )
    gather.shared_near(1)

    def near(i, carry):
        z = off("z", i + i // 2)
        spread(
            v["wout"], v["act"], v["mixb"], second, [(off("y", step), z) for step in (1, 3, 0)]
        )
        return carry

    lax.fori_loop(0, 3, near, 0)
    for o in (0, 3, 1, 2):
        gather.second_far(1, o)
    gather.shared_far(1)
    spread(
        v["wout"], v["act"], v["mixb"], second,
        [(off("y", 2), off("z", step)) for step in (1, 3, 0)],
    )
    spread(
        v["wout"], v["act"], v["mixb"], second,
        [(off("y", step), off("z", 2)) for step in (2, 1, 3, 0)],
    )
    gather.finish()
    first.finish()

    third = ToChannels(
        here, v["mixg"], v["cols2"], (v["a3_send"], v["a3_recv"], v["a3_esend"], v["a3_erecv"])
    )

    def middle_of(at):
        source = spectra[rows(at, 32), :].astype(F32)
        mix = v["tm"][at].reshape(32, 768).astype(F32)
        return (source + mix).astype(BF).astype(F32)

    for half in range(2):
        second.arrive(half)
        span = pl.ds(192 * half, 192)

        def norm_second(i, carry):
            at = half * 6 + i
            v["ns"][rows(at, 32), :] = normalize(middle_of(at))[0].astype(BF)
            return carry

        lax.fori_loop(0, 6, norm_second, 0, unroll=3)

        def hidden_units(i, carry):
            part = lanes(256 * i, 256)
            own = rows(i, 256)
            value, slope = gelu_pair(dot(v["ns"][span, :], v["chin"][own, :], NT))
            v["cact"][span, part] = value.astype(BF)
            v["cgrad"][span, part] = (v["down"][span, part] * slope).astype(BF)
            return carry

        lax.fori_loop(0, 6, hidden_units, 0, unroll=2)
        for name in ("cgrad", "cact"):
            share(v[name].at[span], v[name + "_s"].at[span])
        share(v["ns"].at[span, lanes(384 * (1 - c), 384)], v["ns_s"].at[span])
        v["second"][...] = dot(v["cgrad"][span, :], v["chin"][...], NN)

        def back_second(i, carry):
            at = half * 6 + i
            unit, scale = normalize(middle_of(at))
            upstream = v["second"][rows(i, 32), :]
            value = cot[rows(at, 32), :].astype(F32) + norm_back(unit, scale, upstream)
            v["mg"][rows(at, 32), :] = value
            v["mixg"][at] = value.astype(BF).reshape(2, 16, 768)
            return carry

        lax.fori_loop(0, 6, back_second, 0, unroll=3)
        third.start(half)

    for copy in shared:
        copy.wait_recv()
    half_lanes = lanes(384 * c, 384)
    for g, (act, tok, act_s, tok_s) in enumerate((
        ("cgrad", v["ns"], "cgrad_s", "ns_s"), ("cact", cot, "cact_s", "cot_s"),
    )):
        def channel_sum(y, carry):
            part = lanes(384 * y, 384)
            total = dot(v[act][:, part], tok[:, half_lanes], TN)
            total += dot(v[act_s][:, part], v[tok_s][...], TN)
            total = total.astype(BF).reshape(2, 4, 48, 384)
            for p in range(3):
                v["g%d" % p][y, :, :, g] = total[..., 128 * p:128 * p + 128]
            return carry

        lax.fori_loop(0, 4, channel_sum, 0)

    parts = [
        PartSum(here, p, v["g%d" % p], bufs[6 * p:6 * p + 6], v["r_send"], v["r_recv"])
        for p in range(len(PARTS))
    ]
    channel_parts, early, late = parts[:3], parts[3:6], parts[6:]
    for part in channel_parts:
        part.begin()
    for part in channel_parts:
        part.relay()

    second.finish()
    third.arrive()
    share_cols2 = share(v["cols2"].at[:, 1 - c], v["cols2_s"])
    project(v["cols2"], v["wout"])

    def token_grad(i, carry):
        at = rows(i, 16)
        v["hg"][at, :] = (v["hidden"][at, :] * v["slope"][at, :]).astype(BF)
        return carry

    lax.fori_loop(0, 16, token_grad, 0, unroll=4)
    share_hg = share(v["hg"], v["hg_s"])

    def token_sum(left, left_s, right, right_s, targets):
        def step(y, carry):
            own = v[left][pl.ds(16 * y, 16), c].reshape(256, 256)
            other = v[left_s][pl.ds(16 * y, 16)].reshape(256, 256)
            total = dot(own, v[right][...], NN) + dot(other, v[right_s][...], NN)
            total = total.astype(BF).reshape(2, 4, 2, 16, 1024)
            for name, take in targets:
                v[name][y] = total[..., take]
            return carry

        lax.fori_loop(0, 4, step, 0)

    share_cols2.wait_recv()
    token_sum(
        "cols2", "cols2_s", "act", "act_s",
        (("g3", slice(0, 384)), ("g4", slice(384, 768)), ("g5", slice(768, 1024))),
    )
    for part in early:
        part.begin()
    for part in channel_parts:
        part.cross()
    share_hg.wait_recv()
    token_sum(
        "cols", "cols_s", "hg", "hg_s",
        (("g6", slice(0, 256)), ("g7", slice(256, 640)), ("g8", slice(640, 1024))),
    )
    for part in late:
        part.begin()
    for part in early:
        part.relay()
    for part in channel_parts:
        part.turn()
    fourth = ToPatches(
        here, v["ncg"], v["ng"], (v["a4_send"], v["a4_recv"], v["a4_esend"])
    )

    def back(i, carry):
        z = off("z", 3 - i)
        spread(
            v["win"], v["hg"], v["ncg"], fourth, [(off("y", step), z) for step in (2, 1, 3, 0)]
        )
        return carry

    lax.fori_loop(0, 4, back, 0)
    for part in late:
        part.relay()
    for part in early:
        part.cross()

    def input_grad(half):
        fourth.arrive(half)

        def step(i, carry):
            at = half * 6 + i
            unit, scale = normalize(spectra[rows(at, 32), :].astype(F32))
            upstream = v["ng"][at].reshape(32, 768).astype(F32)
            value = v["mg"][rows(at, 32), :] + norm_back(unit, scale, upstream)
            grad_input[rows(at, 32), :] = value.astype(BF)
            return carry

        lax.fori_loop(0, 6, step, 0, unroll=3)

    for p, part in enumerate(channel_parts):
        v["fin"][here.d, :, 128 * p:128 * p + 128] = part.end()
    input_grad(0)
    swaps = []
    for k, device in enumerate((sib, here.at(x=here.xh * 2 + 1 - here.xl), cross)):
        copy = remote(
            v["fin"].at[here.d], v["fin"].at[here.d], v["f_send"].at[k], v["f_recv"].at[k], device
        )
        copy.start()
        swaps.append(copy)
    for part in early:
        part.turn()
    for part in late:
        part.cross()
    input_grad(1)
    stores = [pltpu.make_async_copy(grad_input, grad_out, v["load"].at[4])]
    stores[0].start()
    for part in late:
        part.turn()

    def gather_up(out, group):
        place = 0
        for part in group:
            width = PARTS[part.p][2]
            out[:, place:place + width] = part.end()
            place += width

    def keep(k, src, dst):
        copy = pltpu.make_async_copy(src, dst, v["load"].at[k])
        copy.start()
        return copy

    gather_up(v["sum1"], early)
    stores.append(keep(0, v["sum1"], o1))
    for copy in swaps:
        copy.wait()
    for d in range(4):
        @pl.when(here.d == d)
        def _():
            for name, g in (("sum2", 0), ("sum3", 2)):
                for k in range(2):
                    v[name][:, 384 * k:384 * k + 384] = v["fin"][g + k, 12 * d:12 * d + 12]
    stores.append(keep(1, v["sum2"], o2))
    stores.append(keep(2, v["sum3"], o3))
    for part in channel_parts + early:
        part.finish()
    for copy in shared:
        copy.wait_send()
    third.finish()
    fourth.finish()
    gather_up(v["sum0"], late)
    stores.append(keep(3, v["sum0"], o0))
    for part in late:
        part.finish()
    for copy in stores:
        copy.wait()


def hand_over(*refs):
    for src, dst in zip(refs[:5], refs[5:]):
        dst[...] = src[...]


def local(spectra_in, cotangent, tok_in_w, tok_out_w, ch_in_w, ch_out_w):
    vmem = pl.BlockSpec(memory_space=pltpu.VMEM)
    scratch = [pltpu.VMEM(shape, kind) for shape, kind in SCRATCH.values()]
    scratch += [DMA(shape) if shape else DMA for shape in SEMS.values()]
    for p in range(len(PARTS)):
        scratch += part_buffers(p)
    shapes = (
        jax.ShapeDtypeStruct((384, 768), BF),
        jax.ShapeDtypeStruct((16, 1024), F32),
        jax.ShapeDtypeStruct((16, 1024), F32),
        jax.ShapeDtypeStruct((12, 768), F32),
        jax.ShapeDtypeStruct((12, 768), F32),
    )
    outs = pl.pallas_call(
        block_kernel,
        out_shape=shapes,
        in_specs=[ANY] * 6, out_specs=(ANY,) * 5,
        scratch_shapes=scratch,
        compiler_params=pltpu.CompilerParams(
            collective_id=0, has_side_effects=True, vmem_limit_bytes=60 * 1024 * 1024
        ),
        name="mixer_block_backward",
    )(
        spectra_in.reshape(384, 768), cotangent.reshape(384, 768),
        tok_in_w.reshape(2, 32, 1024), tok_out_w.reshape(2, 32, 1024), ch_in_w, ch_out_w,
    )
    grad_input, *weights = pl.pallas_call(
        hand_over, out_shape=shapes, in_specs=[vmem] * 5, out_specs=(vmem,) * 5, name="hand_over",
    )(*outs)
    return (grad_input.reshape(6, 64, 768), *weights)


def solution(mesh):
    in_specs = (
        P("dp", "seq", None),
        P("dp", "seq", None),
        P("seq", None),
        P("seq", None),
        P(),
        P(),
    )
    out_specs = (
        P("dp", "seq", None),
        P(("seq", "dp"), None),
        P(("seq", "dp"), None),
        P(("seq", "dp"), None),
        P(("seq", "dp"), None),
    )
    return jax.shard_map(local, mesh=mesh, in_specs=in_specs, out_specs=out_specs, check_vma=False)
```

```python
import math
import types

import jax
import jax.numpy as jnp
from jax import lax
from jax.experimental import pallas as pl
from jax.experimental.pallas import tpu as pltpu
from jax.sharding import PartitionSpec as P

BF = jnp.bfloat16
F32 = jnp.float32
MESH = pl.DeviceIdType.MESH
ANY = pl.BlockSpec(memory_space=pl.ANY)
LANES = 128


def normalize(values):
    center = values - jnp.mean(values, axis=-1, keepdims=True)
    inv_scale = lax.rsqrt(jnp.mean(center * center, axis=-1, keepdims=True) + 1e-05)
    return (center * inv_scale, inv_scale)


def norm_back(unit, inv_scale, upstream):
    first = jnp.mean(upstream, axis=-1, keepdims=True)
    second = jnp.mean(upstream * unit, axis=-1, keepdims=True)
    return inv_scale * (upstream - first - unit * second)


def gelu_pair(values):
    factor = math.sqrt(2.0 / math.pi)
    inner = factor * (values + 0.044715 * values * values * values)
    tangent = jnp.tanh(inner)
    result = 0.5 * values * (1.0 + tangent)
    slope = 0.5 * (1.0 + tangent) + 0.5 * values * (1.0 - tangent * tangent) * factor * (
        1.0 + 3.0 * 0.044715 * values * values
    )
    return (result, slope)


class Here:
    def __init__(self):
        self.q = lax.axis_index("seq")
        self.d = lax.axis_index("dp")
        self.y = self.q // 8
        self.xh = (self.q // 4) % 2
        self.z = self.q % 4
        self.xl = self.d // 2
        self.c = self.d % 2
        self.x = self.xh * 2 + self.xl

    def at(self, x=None, y=None, z=None, c=None):
        x = self.x if x is None else x
        y = self.y if y is None else y
        z = self.z if z is None else z
        c = self.c if c is None else c
        return {"seq": (y * 2 + x // 2) * 4 + z, "dp": (x % 2) * 2 + c}

    def peer(self, q):
        return {"seq": q, "dp": self.d}

    def sibling(self):
        return {"seq": self.q, "dp": self.d + 1 - 2 * self.c}

    def extra_of(self, e):
        return 8 * e + ((e + self.d // 2) % 2) * 4 + (e + self.d) % 4

    def has_extra(self):
        return self.q == self.extra_of(self.y)


def remote(src, dst, send, recv, device):
    return pltpu.make_async_remote_copy(
        src_ref=src, dst_ref=dst, send_sem=send, recv_sem=recv,
        device_id=device, device_id_type=MESH,
    )


def drain(ref, sem):
    pltpu.make_async_copy(ref, ref, sem).wait()


def greet(devices):
    barrier = pltpu.get_barrier_semaphore()
    for device in devices:
        pl.semaphore_signal(barrier, inc=1, device_id=device, device_id_type=MESH)
    return len(devices)


def greet_seq(here):
    barrier = pltpu.get_barrier_semaphore()

    def body(i, carry):
        pl.semaphore_signal(
            barrier, inc=1, device_id=here.peer((here.q + i) % 32), device_id_type=MESH
        )
        return carry

    lax.fori_loop(1, 32, body, 0)
    return 31


def rows(start, size):
    return pl.ds(pl.multiple_of(start * size, size), size)


TN = (((0,), (0,)), ((), ()))
NT = (((1,), (1,)), ((), ()))
NN = (((1,), (0,)), ((), ()))


def dot(a, b, dims):
    return lax.dot_general(a, b, dims, preferred_element_type=F32)


def lanes(start, size):
    return pl.ds(pl.multiple_of(start, LANES), size)


def block_of(ref, s, b):
    return ref.at[pl.ds(2 * s, 2), :, :, lanes(b * LANES, LANES)]


def column(ref, q, slot):
    return ref.at[pl.ds(2 * q, 2), :, :, pl.ds(slot * LANES, LANES)]


class ToChannels:
    def __init__(self, here, src, cols, sems):
        self.here, self.src, self.cols = here, src, cols
        self.send, self.recv, self.esend, self.erecv = sems

        @pl.when(jnp.logical_not(here.has_extra()))
        def _():
            cols[:, :, :, LANES:] = jnp.zeros((64, 2, 16, LANES), BF)

    def start(self, half):
        here, src, cols = self.here, self.src, self.cols
        first, count = ((0, 18), (18, 14))[half]

        def body(i, carry):
            dest = first + (i + here.q) % count
            block, place = block_of(src, dest // 6, dest % 6), column(cols, here.q, 0)

            @pl.when(dest != here.q)
            def _():
                remote(block, place, self.send, self.recv, here.peer(dest)).start()

            @pl.when(dest == here.q)
            def _():
                pltpu.make_async_copy(block, place, self.recv).start()

            return carry

        lax.fori_loop(0, count, body, 0)
        if half == 1:
            for e in range(4):
                dest = here.extra_of(e)
                block, place = block_of(src, 5, 2 + e), column(cols, here.q, 1)

                @pl.when(dest != here.q)
                def _():
                    remote(block, place, self.esend.at[e], self.erecv, here.peer(dest)).start()

                @pl.when(dest == here.q)
                def _():
                    pltpu.make_async_copy(block, place, self.erecv).start()

    def arrive(self):
        drain(self.cols.at[:, :, :, pl.ds(0, LANES)], self.recv)

        @pl.when(self.here.has_extra())
        def _():
            drain(self.cols.at[:, :, :, pl.ds(LANES, LANES)], self.erecv)

    def finish(self):
        drain(self.cols.at[pl.ds(0, 62), :, :, pl.ds(0, LANES)], self.send)
        for e in range(4):
            @pl.when(self.here.extra_of(e) != self.here.q)
            def _():
                drain(self.cols.at[pl.ds(0, 2), :, :, pl.ds(0, LANES)], self.esend.at[e])


class ToPatches:
    def __init__(self, here, cols, out, sems):
        self.here, self.cols, self.out = here, cols, out
        self.send, self.recv, self.esend = sems

    def start(self, dest):
        here, cols, out = self.here, self.cols, self.out
        place = block_of(out, here.q // 6, here.q % 6)
        extra = block_of(out, 5, 2 + here.y)
        sem = self.recv.at[here.q // 18]

        @pl.when(dest != here.q)
        def _():
            remote(column(cols, dest, 0), place, self.send, sem, here.peer(dest)).start()

            @pl.when(here.has_extra())
            def _():
                remote(
                    column(cols, dest, 1), extra, self.esend, self.recv.at[1], here.peer(dest)
                ).start()

        @pl.when(dest == here.q)
        def _():
            pltpu.make_async_copy(column(cols, dest, 0), place, sem).start()

            @pl.when(here.has_extra())
            def _():
                pltpu.make_async_copy(column(cols, dest, 1), extra, self.recv.at[1]).start()

    def arrive(self, half):
        drain(self.out.at[pl.ds(6 * half, 6)], self.recv.at[half])

    def finish(self):
        many = self.cols.at[pl.ds(0, 62), :, :, pl.ds(0, LANES)]
        drain(many, self.send)

        @pl.when(self.here.has_extra())
        def _():
            drain(many, self.esend)


class Gather:
    def __init__(self, here, parts, fulls, sems):
        self.here, self.fulls, self.parts = here, fulls, parts
        self.own, self.send, self.recv, self.bsend, self.brecv = sems
        self.copies = []
        self.legs = [{}, {}]
        c, y, xh, z = here.c, here.y, here.xh, here.z
        self.locals = []
        for w in range(2):
            copy = pltpu.make_async_copy(parts[w], fulls[w].at[y, xh, z], self.own.at[w])
            copy.start()
            self.locals.append(copy)
            self.push(w, 0, fulls[w].at[y, xh, z, c], here.at(x=(here.x + 2) % 4), parts[w].at[c])

    def piece(self, w, first, second, c, half=None):
        here = self.here
        y = (here.y + c * first + (1 - c) * second) % 4
        z = (here.z + (1 - c) * first + c * second) % 4
        h = slice(None) if half is None else half
        return self.fulls[w].at[y, h, z, c]

    def towards(self, axis, step):
        here = self.here
        along_y = here.c if axis == 0 else 1 - here.c
        return here.at(y=(here.y + along_y * step) % 4, z=(here.z + (1 - along_y) * step) % 4)

    def push(self, w, k, ref, device, src=None):
        copy = remote(
            ref if src is None else src, ref, self.send.at[w, k], self.recv.at[w, k], device
        )
        copy.start()
        self.copies.append(copy)
        self.legs[w][k] = copy

    def share(self, w, k, ref):
        copy = remote(ref, ref, self.bsend.at[w, k], self.brecv.at[w, k], self.here.sibling())
        copy.start()
        self.copies.append(copy)

    def around(self, w, ks, half, src=None):
        ref = self.piece(w, 0, 0, self.here.c, half)
        for k, axis, step in zip(ks, (0, 0, 1, 1), (1, 3, 1, 3)):
            self.push(w, k, ref, self.towards(axis, step), src)

    def launch(self, w):
        self.around(w, (1, 2, 5, 6), self.here.xh, self.parts[w].at[self.here.c])

    def crossed(self, w):
        here = self.here
        self.legs[w][0].wait_recv()
        self.around(w, (21, 22, 23, 24), 1 - here.xh)
        self.share(w, 0, self.piece(w, 0, 0, here.c, 1 - here.xh))
        self.locals[w].wait()

    def second(self, w, o):
        ref = self.piece(w, o, 0, self.here.c)
        self.push(w, 5 + 4 * o, ref, self.towards(1, 1))
        self.push(w, 6 + 4 * o, ref, self.towards(1, 3))

    def first_near(self, w):
        c = self.here.c
        self.legs[w][1].wait_recv()
        self.legs[w][21].wait_recv()
        self.push(w, 3, self.piece(w, 3, 0, c, 0), self.towards(0, 1))
        self.second(w, 3)
        self.share(w, 1, self.piece(w, 3, 0, c))
        self.legs[w][2].wait_recv()
        self.legs[w][22].wait_recv()
        self.push(w, 4, self.piece(w, 1, 0, c, 1), self.towards(0, 3))
        self.second(w, 1)
        self.share(w, 2, self.piece(w, 1, 0, c))

    def first_far(self, w):
        self.legs[w][3].wait_recv()
        self.legs[w][4].wait_recv()
        self.second(w, 2)
        self.share(w, 3, self.piece(w, 2, 0, self.here.c))

    def second_near(self, w, o):
        c = self.here.c
        self.legs[w][5 + 4 * o].wait_recv()
        if o == 0:
            self.legs[w][23].wait_recv()
        self.push(w, 7 + 4 * o, self.piece(w, o, 3, c, 0), self.towards(1, 1))
        self.share(w, 4 + 3 * o, self.piece(w, o, 3, c))
        self.legs[w][6 + 4 * o].wait_recv()
        if o == 0:
            self.legs[w][24].wait_recv()
        self.push(w, 8 + 4 * o, self.piece(w, o, 1, c, 1), self.towards(1, 3))
        self.share(w, 5 + 3 * o, self.piece(w, o, 1, c))

    def second_far(self, w, o):
        self.legs[w][7 + 4 * o].wait_recv()
        self.legs[w][8 + 4 * o].wait_recv()
        self.share(w, 6 + 3 * o, self.piece(w, o, 2, self.here.c))

    def shared_near(self, w):
        other = 1 - self.here.c
        drain(self.piece(w, 0, 0, other, 1 - self.here.xh), self.brecv.at[w, 0])
        for k, o in ((1, 3), (2, 1), (3, 2)):
            drain(self.piece(w, o, 0, other), self.brecv.at[w, k])
        for o in range(4):
            drain(self.piece(w, o, 3, other), self.brecv.at[w, 4 + 3 * o])
            drain(self.piece(w, o, 1, other), self.brecv.at[w, 5 + 3 * o])

    def shared_far(self, w):
        for o in range(4):
            drain(self.piece(w, o, 2, 1 - self.here.c), self.brecv.at[w, 6 + 3 * o])

    def finish(self):
        for copy in self.copies:
            copy.wait_send()


def add_into(target, *others):
    lead = target.shape[:-2]

    def body(i, carry):
        index = []
        rest = i
        for size in reversed(lead):
            index.append(rest % size)
            rest = rest // size
        index = tuple(reversed(index))
        total = target[index].astype(F32)
        for other in others:
            total += other[index].astype(F32)
        target[index] = total.astype(BF)
        return carry

    lax.fori_loop(0, math.prod(lead), body, 0, unroll=min(8, math.prod(lead)))


PARTS = (
    ("x", 48, 128), ("y", 48, 128), ("z", 48, 128),
    ("y", 16, 384), ("z", 16, 384), ("x", 16, 256),
    ("y", 16, 256), ("z", 16, 384), ("x", 16, 384),
)
PLANES = {"x": ("y", "z"), "y": ("z", "x"), "z": ("x", "y")}


class PartSum:
    def __init__(self, here, p, acc, bufs, send, recv):
        self.here, self.p, self.acc = here, p, acc
        self.low, self.high, self.up_buf, self.down_buf, self.turn_buf, self.end_buf = bufs
        self.send, self.recv = send, recv
        self.copies = []
        self.axis = PARTS[p][0]
        self.me = getattr(here, self.axis)

    def index(self, at):
        full = slice(None)
        if "x" in at:
            return (at.get("y", full), at["x"] // 2, at.get("z", full), at["x"] % 2)
        return (at.get("y", full), full, at.get("z", full), full)

    def chunk(self, pos, half=None):
        index = list(self.index({self.axis: pos}))
        if half is not None:
            if self.axis == "y":
                index[1] = half
            else:
                index[0] = pl.ds(2 * half, 2)
        return self.acc.at[tuple(index)]

    def to(self, step):
        return self.here.at(**{self.axis: (self.me + step) % 4})

    def push(self, k, src, dst, device):
        copy = remote(src, dst, self.send.at[self.p, k], self.recv.at[self.p, k], device)
        copy.start()
        self.copies.append(copy)
        return copy

    def begin(self):
        far = (self.me + 2) % 4
        self.legs = (
            self.push(0, self.chunk(far, 0), self.low, self.to(1)),
            self.push(1, self.chunk(far, 1), self.high, self.to(3)),
        )

    def relay(self):
        up, down = (self.me + 1) % 4, (self.me + 3) % 4
        self.legs[0].wait_recv()
        add_into(self.chunk(up, 0), self.low)
        one = self.push(2, self.chunk(up), self.up_buf, self.to(1))
        self.legs[1].wait_recv()
        add_into(self.chunk(down, 1), self.high)
        two = self.push(3, self.chunk(down), self.down_buf, self.to(3))
        self.legs = (one, two)

    def across(self, k, name, buf, at):
        me = getattr(self.here, name)
        for step in (1, 3, 2):
            pos = (me + step) % 4
            remote(
                self.acc.at[self.index({**at, name: pos})], buf.at[me],
                self.send.at[self.p, k], self.recv.at[self.p, k], self.here.at(**{name: pos}),
            ).start()

    def cross(self):
        self.legs[0].wait_recv()
        self.legs[1].wait_recv()
        add_into(self.chunk(self.me), self.up_buf, self.down_buf)
        self.across(4, PLANES[self.axis][0], self.turn_buf, {self.axis: self.me})

    def turn(self):
        a, b = PLANES[self.axis]
        me = getattr(self.here, a)
        at = {self.axis: self.me, a: me}
        drain(self.turn_buf.at[pl.ds(0, 3)], self.recv.at[self.p, 4])
        add_into(
            self.acc.at[self.index(at)], *[self.turn_buf.at[(me + k) % 4] for k in (1, 2, 3)]
        )
        self.across(5, b, self.end_buf, at)

    def end(self):
        a, b = PLANES[self.axis]
        me = getattr(self.here, b)
        at = {self.axis: self.me, a: getattr(self.here, a), b: me}
        drain(self.end_buf.at[pl.ds(0, 3)], self.recv.at[self.p, 5])
        total = self.acc[self.index(at)].astype(F32)
        for k in (1, 2, 3):
            total += self.end_buf[(me + k) % 4].astype(F32)
        return total

    def finish(self):
        for copy in self.copies:
            copy.wait_send()
        drain(self.turn_buf.at[pl.ds(0, 3)], self.send.at[self.p, 4])
        drain(self.end_buf.at[pl.ds(0, 3)], self.send.at[self.p, 5])


def part_shape(p):
    return (4, 2, 4, 2) + PARTS[p][1:]


def part_buffers(p):
    axis, tail = PARTS[p][0], PARTS[p][1:]
    whole = {"x": (4, 4), "y": (2, 4, 2), "z": (4, 2, 2)}[axis]
    half = whole[1:] if axis == "y" else (2,) + whole[1:]
    last = (2, 2) if PLANES[axis][1] == "x" else (4,)
    shapes = [half + tail] * 2 + [whole + tail] * 2 + [(4,) + last + tail, (4,) + tail]
    return [pltpu.VMEM(s, BF) for s in shapes]


DMA = pltpu.SemaphoreType.DMA
SCRATCH = dict(
    spectra=((384, 768), BF), cot=((384, 768), BF), grad_input=((384, 768), BF),
    win=((4, 2, 4, 2, 32, 1024), BF), wout=((4, 2, 4, 2, 32, 1024), BF),
    chin=((1536, 768), BF), chout=((1536, 768), BF),
    normed=((12, 2, 16, 768), BF), tm=((12, 2, 16, 768), BF), ng=((12, 2, 16, 768), BF),
    mixg=((12, 2, 16, 768), BF), ns=((384, 768), BF), mg=((384, 768), F32),
    cact=((384, 1536), BF), cgrad=((384, 1536), BF),
    cact_s=((384, 1536), BF), cgrad_s=((384, 1536), BF),
    ns_s=((384, 384), BF), cot_s=((384, 384), BF),
    cols_t=((256, 2048), BF), second=((192, 768), F32), down=((384, 1536), F32),
    cols=((64, 2, 16, 256), BF), cols2=((64, 2, 16, 256), BF),
    cols_s=((64, 16, 256), BF), cols2_s=((64, 16, 256), BF),
    hidden=((256, 1024), F32), slope=((256, 1024), F32),
    act=((256, 1024), BF), act_s=((256, 1024), BF),
    hg=((256, 1024), BF), hg_s=((256, 1024), BF),
    mixb=((64, 2, 16, 256), BF), ncg=((64, 2, 16, 256), BF),
    fin=((4, 48, 384), F32), sum0=((16, 1024), F32), sum1=((16, 1024), F32),
    sum2=((12, 768), F32), sum3=((12, 768), F32),
)
SEMS = dict(
    load=(5,), a1_send=(), a1_recv=(), a1_esend=(4,), a1_erecv=(),
    a3_send=(), a3_recv=(), a3_esend=(4,), a3_erecv=(),
    a2_send=(), a2_recv=(2,), a2_esend=(),
    a4_send=(), a4_recv=(2,), a4_esend=(),
    w_own=(2,), w_send=(2, 25), w_recv=(2, 25), w_bsend=(2, 16), w_brecv=(2, 16),
    r_send=(9, 6), r_recv=(9, 6),
    s_send=(11,), s_recv=(11,), f_send=(3,), f_recv=(3,),
)


def block_kernel(
    spectra_in, cot_in, w_in, w_out, ch_in, ch_out, grad_out, o0, o1, o2, o3, *scratch
):
    v = types.SimpleNamespace(**dict(zip(list(SCRATCH) + list(SEMS), scratch)))
    spectra, cot, grad_input = v.spectra, v.cot, v.grad_input
    bufs = scratch[len(SCRATCH) + len(SEMS):]
    sums = scratch[len(SCRATCH) + len(SEMS) + 6 * len(PARTS):]
    here = Here()
    c = here.c
    sib = here.sibling()
    cross = here.at(x=here.xh * 2 + 1 - here.xl, c=1 - c)
    partners = [sib, cross]
    for k in (1, 3):
        x = (here.x + k) % 4
        partners += [here.at(x=x, z=(here.z + n) % 4) for n in range(4)]
        partners += [here.at(x=x, y=(here.y + n) % 4) for n in range(1, 4)]
    count = greet_seq(here) + greet(partners)
    loads = [
        pltpu.make_async_copy(src, dst, v.load.at[k])
        for k, (src, dst) in enumerate((
            (spectra_in, spectra), (cot_in, cot), (ch_in, v.chin), (ch_out, v.chout),
        ))
    ]
    for copy in loads:
        copy.start()
    loads.pop(0).wait()

    def norm_first(i, carry):
        unit, _ = normalize(spectra[rows(i, 32), :].astype(F32))
        v.normed[i] = unit.astype(BF).reshape(2, 16, 768)
        return carry

    lax.fori_loop(0, 12, norm_first, 0, unroll=6)
    pl.semaphore_wait(pltpu.get_barrier_semaphore(), count)

    shared = []

    def share(src, dst):
        k = len(shared)
        copy = remote(src, dst, v.s_send.at[k], v.s_recv.at[k], sib)
        copy.start()
        shared.append(copy)
        return copy

    gather = Gather(
        here, (w_in, w_out), (v.win, v.wout),
        (v.w_own, v.w_send, v.w_recv, v.w_bsend, v.w_brecv),
    )
    first = ToChannels(
        here, v.normed, v.cols, (v.a1_send, v.a1_recv, v.a1_esend, v.a1_erecv)
    )
    both = range(2)
    for w in both:
        gather.launch(w)
    first.start(0)
    first.start(1)
    for w in both:
        gather.crossed(w)
    for copy in loads:
        copy.wait()
    share(cot.at[:, lanes(384 * (1 - c), 384)], v.cot_s)

    def channel_down(i, carry):
        v.down[:, lanes(256 * i, 256)] = dot(cot[...], v.chout[rows(i, 256), :], NT)
        return carry

    for w in both:
        gather.first_near(w)
    lax.fori_loop(0, 3, channel_down, 0)
    for w in both:
        gather.second_near(w, 0)
    for w in both:
        gather.first_far(w)
    lax.fori_loop(3, 6, channel_down, 0)
    for o in (3, 1):
        for w in both:
            gather.second_near(w, o)
    first.arrive()
    share(v.cols.at[:, 1 - c], v.cols_s)
    for w in both:
        gather.second_near(w, 2)

    def turn_cols(y, carry):
        v.cols_t[:, lanes(512 * y, 512)] = v.cols[pl.ds(16 * y, 16)].reshape(512, 256).T
        return carry

    lax.fori_loop(0, 4, turn_cols, 0, unroll=2)
    for o in (0, 3, 1, 2):
        gather.second_far(0, o)
    gather.shared_near(0)
    gather.shared_far(0)

    def project(source, weight):
        def step(y, start):
            left = source[pl.ds(16 * y, 16)].reshape(512, 256)
            part = dot(left, weight[y].reshape(512, 1024), TN)
            if start:
                v.hidden[...] = part
            else:
                v.hidden[...] += part

        step(0, True)
        for y in range(1, 4):
            step(y, False)

    def hidden_of(i, carry):
        part = lanes(256 * i, 256)
        weight = v.win[:, :, :, :, :, part].reshape(2048, 256)
        v.hidden[:, part] = dot(v.cols_t[...], weight, NN)
        return carry

    lax.fori_loop(0, 4, hidden_of, 0, unroll=4)

    def token_gelu(i, carry):
        at = rows(i, 16)
        value, slope = gelu_pair(v.hidden[at, :])
        v.act[at, :] = value.astype(BF)
        v.slope[at, :] = slope
        return carry

    lax.fori_loop(0, 16, token_gelu, 0, unroll=8)
    share(v.act, v.act_s)

    def spread(weight, source, target, transfer, spots):
        left = jnp.concatenate([weight[y, :, z].reshape(128, 1024) for y, z in spots], axis=0)
        value = dot(left, source[...], NT).astype(BF).reshape(len(spots), 2, 2, 2, 16, 256)
        for k, (y, z) in enumerate(spots):
            for xh in range(2):
                dest = 8 * y + 4 * xh + z
                target[pl.ds(2 * dest, 2)] = value[k, xh]
                transfer.start(dest)

    def off(name, step):
        return (getattr(here, name) + step) % 4

    second = ToPatches(
        here, v.mixb, v.tm, (v.a2_send, v.a2_recv, v.a2_esend)
    )
    gather.shared_near(1)

    def near(i, carry):
        z = off("z", i + i // 2)
        spread(
            v.wout, v.act, v.mixb, second, [(off("y", step), z) for step in (1, 3, 0)]
        )
        return carry

    lax.fori_loop(0, 3, near, 0)
    for o in (0, 3, 1, 2):
        gather.second_far(1, o)
    gather.shared_far(1)
    spread(
        v.wout, v.act, v.mixb, second,
        [(off("y", 2), off("z", step)) for step in (1, 3, 0)],
    )
    spread(
        v.wout, v.act, v.mixb, second,
        [(off("y", step), off("z", 2)) for step in (2, 1, 3, 0)],
    )
    gather.finish()
    first.finish()

    third = ToChannels(
        here, v.mixg, v.cols2, (v.a3_send, v.a3_recv, v.a3_esend, v.a3_erecv)
    )

    def middle_of(at):
        source = spectra[rows(at, 32), :].astype(F32)
        mix = v.tm[at].reshape(32, 768).astype(F32)
        return (source + mix).astype(BF).astype(F32)

    for half in range(2):
        second.arrive(half)
        span = pl.ds(192 * half, 192)

        def norm_second(i, carry):
            at = half * 6 + i
            v.ns[rows(at, 32), :] = normalize(middle_of(at))[0].astype(BF)
            return carry

        lax.fori_loop(0, 6, norm_second, 0, unroll=6)

        def hidden_units(i, carry):
            part = lanes(256 * i, 256)
            own = rows(i, 256)
            value, slope = gelu_pair(dot(v.ns[span, :], v.chin[own, :], NT))
            v.cact[span, part] = value.astype(BF)
            v.cgrad[span, part] = (v.down[span, part] * slope).astype(BF)
            return carry

        lax.fori_loop(0, 6, hidden_units, 0, unroll=3)
        for src, dst in ((v.cgrad, v.cgrad_s), (v.cact, v.cact_s)):
            share(src.at[span], dst.at[span])
        share(v.ns.at[span, lanes(384 * (1 - c), 384)], v.ns_s.at[span])
        v.second[...] = dot(v.cgrad[span, :], v.chin[...], NN)

        def back_second(i, carry):
            at = half * 6 + i
            unit, scale = normalize(middle_of(at))
            upstream = v.second[rows(i, 32), :]
            value = cot[rows(at, 32), :].astype(F32) + norm_back(unit, scale, upstream)
            v.mg[rows(at, 32), :] = value
            v.mixg[at] = value.astype(BF).reshape(2, 16, 768)
            return carry

        lax.fori_loop(0, 6, back_second, 0, unroll=6)
        third.start(half)

    for copy in shared:
        copy.wait_recv()
    half_lanes = lanes(384 * c, 384)
    for g, (act, tok, act_s, tok_s) in enumerate((
        (v.cgrad, v.ns, v.cgrad_s, v.ns_s), (v.cact, cot, v.cact_s, v.cot_s),
    )):
        def channel_sum(y, carry):
            part = lanes(384 * y, 384)
            total = dot(act[:, part], tok[:, half_lanes], TN)
            total += dot(act_s[:, part], tok_s[...], TN)
            total = total.astype(BF).reshape(2, 4, 48, 384)
            for p in range(3):
                sums[p][y, :, :, g] = total[..., 128 * p:128 * p + 128]
            return carry

        lax.fori_loop(0, 4, channel_sum, 0, unroll=4)

    parts = [
        PartSum(here, p, sums[p], bufs[6 * p:6 * p + 6], v.r_send, v.r_recv)
        for p in range(len(PARTS))
    ]
    channel_parts, early, late = parts[:3], parts[3:6], parts[6:]
    for part in channel_parts:
        part.begin()
    for part in channel_parts:
        part.relay()

    second.finish()
    third.arrive()
    share_cols2 = share(v.cols2.at[:, 1 - c], v.cols2_s)
    project(v.cols2, v.wout)

    def token_grad(i, carry):
        at = rows(i, 16)
        v.hg[at, :] = (v.hidden[at, :] * v.slope[at, :]).astype(BF)
        return carry

    lax.fori_loop(0, 16, token_grad, 0, unroll=8)
    share_hg = share(v.hg, v.hg_s)

    def token_sum(left, left_s, right, right_s, targets):
        def step(y, carry):
            own = left[pl.ds(16 * y, 16), c].reshape(256, 256)
            other = left_s[pl.ds(16 * y, 16)].reshape(256, 256)
            total = dot(own, right[...], NN) + dot(other, right_s[...], NN)
            total = total.astype(BF).reshape(2, 4, 2, 16, 1024)
            place = 0
            for p in targets:
                width = PARTS[p][2]
                sums[p][y] = total[..., place:place + width]
                place += width
            return carry

        lax.fori_loop(0, 4, step, 0, unroll=4)

    share_cols2.wait_recv()
    token_sum(
        v.cols2, v.cols2_s, v.act, v.act_s, (3, 4, 5),
    )
    for part in early:
        part.begin()
    for part in channel_parts:
        part.cross()
    share_hg.wait_recv()
    token_sum(
        v.cols, v.cols_s, v.hg, v.hg_s, (6, 7, 8),
    )
    for part in late:
        part.begin()
    for part in early:
        part.relay()
    for part in channel_parts:
        part.turn()
    fourth = ToPatches(
        here, v.ncg, v.ng, (v.a4_send, v.a4_recv, v.a4_esend)
    )

    def back(i, carry):
        z = off("z", 3 - i)
        spread(
            v.win, v.hg, v.ncg, fourth, [(off("y", step), z) for step in (2, 1, 3, 0)]
        )
        return carry

    lax.fori_loop(0, 4, back, 0, unroll=2)
    for part in late:
        part.relay()
    for part in early:
        part.cross()

    def input_grad(half):
        fourth.arrive(half)

        def step(i, carry):
            at = half * 6 + i
            unit, scale = normalize(spectra[rows(at, 32), :].astype(F32))
            upstream = v.ng[at].reshape(32, 768).astype(F32)
            value = v.mg[rows(at, 32), :] + norm_back(unit, scale, upstream)
            grad_input[rows(at, 32), :] = value.astype(BF)
            return carry

        lax.fori_loop(0, 6, step, 0, unroll=6)

    for p, part in enumerate(channel_parts):
        v.fin[here.d, :, 128 * p:128 * p + 128] = part.end()
    input_grad(0)
    swaps = []
    for k, device in enumerate((sib, here.at(x=here.xh * 2 + 1 - here.xl), cross)):
        copy = remote(
            v.fin.at[here.d], v.fin.at[here.d], v.f_send.at[k], v.f_recv.at[k], device
        )
        copy.start()
        swaps.append(copy)
    for part in early:
        part.turn()
    for part in late:
        part.cross()
    input_grad(1)
    stores = [pltpu.make_async_copy(grad_input, grad_out, v.load.at[4])]
    stores[0].start()
    for part in late:
        part.turn()

    def gather_up(out, group):
        place = 0
        for part in group:
            width = PARTS[part.p][2]
            out[:, place:place + width] = part.end()
            place += width

    def keep(k, src, dst):
        copy = pltpu.make_async_copy(src, dst, v.load.at[k])
        copy.start()
        return copy

    gather_up(v.sum1, early)
    stores.append(keep(0, v.sum1, o1))
    for copy in swaps:
        copy.wait()
    for d in range(4):
        @pl.when(here.d == d)
        def _():
            for total, g in ((v.sum2, 0), (v.sum3, 2)):
                for k in range(2):
                    total[:, 384 * k:384 * k + 384] = v.fin[g + k, 12 * d:12 * d + 12]
    stores.append(keep(1, v.sum2, o2))
    stores.append(keep(2, v.sum3, o3))
    for part in channel_parts + early:
        part.finish()
    for copy in shared:
        copy.wait_send()
    third.finish()
    fourth.finish()
    gather_up(v.sum0, late)
    stores.append(keep(3, v.sum0, o0))
    for part in late:
        part.finish()
    for copy in stores:
        copy.wait()


def hand_over(*refs):
    for src, dst in zip(refs[:5], refs[5:]):
        dst[...] = src[...]


def local(spectra_in, cotangent, tok_in_w, tok_out_w, ch_in_w, ch_out_w):
    vmem = pl.BlockSpec(memory_space=pltpu.VMEM)
    scratch = [pltpu.VMEM(shape, kind) for shape, kind in SCRATCH.values()]
    scratch += [DMA(shape) if shape else DMA for shape in SEMS.values()]
    for p in range(len(PARTS)):
        scratch += part_buffers(p)
    scratch += [pltpu.VMEM(part_shape(p), BF) for p in range(len(PARTS))]
    shapes = (
        jax.ShapeDtypeStruct((384, 768), BF),
        jax.ShapeDtypeStruct((16, 1024), F32),
        jax.ShapeDtypeStruct((16, 1024), F32),
        jax.ShapeDtypeStruct((12, 768), F32),
        jax.ShapeDtypeStruct((12, 768), F32),
    )
    outs = pl.pallas_call(
        block_kernel,
        out_shape=shapes,
        in_specs=[ANY] * 6, out_specs=(ANY,) * 5,
        scratch_shapes=scratch,
        compiler_params=pltpu.CompilerParams(
            collective_id=0, has_side_effects=True, vmem_limit_bytes=60 * 1024 * 1024
        ),
        name="mixer_block_backward",
    )(
        spectra_in.reshape(384, 768), cotangent.reshape(384, 768),
        tok_in_w.reshape(2, 32, 1024), tok_out_w.reshape(2, 32, 1024), ch_in_w, ch_out_w,
    )
    grad_input, *weights = pl.pallas_call(
        hand_over, out_shape=shapes, in_specs=[vmem] * 5, out_specs=(vmem,) * 5, name="hand_over",
    )(*outs)
    return (grad_input.reshape(6, 64, 768), *weights)


def solution(mesh):
    in_specs = (
        P("dp", "seq", None),
        P("dp", "seq", None),
        P("seq", None),
        P("seq", None),
        P(),
        P(),
    )
    out_specs = (
        P("dp", "seq", None),
        P(("seq", "dp"), None),
        P(("seq", "dp"), None),
        P(("seq", "dp"), None),
        P(("seq", "dp"), None),
    )
    return jax.shard_map(local, mesh=mesh, in_specs=in_specs, out_specs=out_specs, check_vma=False)
```

```python
import math
import types

import jax
import jax.numpy as jnp
from jax import lax
from jax.experimental import pallas as pl
from jax.experimental.pallas import tpu as pltpu
from jax.sharding import PartitionSpec as P

BF = jnp.bfloat16
F32 = jnp.float32
MESH = pl.DeviceIdType.MESH
ANY = pl.BlockSpec(memory_space=pl.ANY)
LANES = 128


def normalize(values):
    center = values - jnp.mean(values, axis=-1, keepdims=True)
    inv_scale = lax.rsqrt(jnp.mean(center * center, axis=-1, keepdims=True) + 1e-05)
    return (center * inv_scale, inv_scale)


def norm_back(unit, inv_scale, upstream):
    first = jnp.mean(upstream, axis=-1, keepdims=True)
    second = jnp.mean(upstream * unit, axis=-1, keepdims=True)
    return inv_scale * (upstream - first - unit * second)


def gelu_pair(values):
    factor = math.sqrt(2.0 / math.pi)
    square = values * values
    half = 0.5 + 0.5 * jnp.tanh(values * (factor + (factor * 0.044715) * square))
    result = values * half
    slope = half + result * (1.0 - half) * (2.0 * factor + (6.0 * factor * 0.044715) * square)
    return (result, slope)


class Here:
    def __init__(self):
        self.q = lax.axis_index("seq")
        self.d = lax.axis_index("dp")
        self.y = self.q // 8
        self.xh = (self.q // 4) % 2
        self.z = self.q % 4
        self.xl = self.d // 2
        self.c = self.d % 2
        self.x = self.xh * 2 + self.xl

    def at(self, x=None, y=None, z=None, c=None):
        x = self.x if x is None else x
        y = self.y if y is None else y
        z = self.z if z is None else z
        c = self.c if c is None else c
        return {"seq": (y * 2 + x // 2) * 4 + z, "dp": (x % 2) * 2 + c}

    def peer(self, q):
        return {"seq": q, "dp": self.d}

    def sibling(self):
        return {"seq": self.q, "dp": self.d + 1 - 2 * self.c}

    def extra_of(self, e):
        return 8 * e + ((e + self.d // 2) % 2) * 4 + (e + self.d) % 4

    def has_extra(self):
        return self.q == self.extra_of(self.y)


def remote(src, dst, send, recv, device):
    return pltpu.make_async_remote_copy(
        src_ref=src, dst_ref=dst, send_sem=send, recv_sem=recv,
        device_id=device, device_id_type=MESH,
    )


def drain(ref, sem):
    pltpu.make_async_copy(ref, ref, sem).wait()


def greet(devices):
    barrier = pltpu.get_barrier_semaphore()
    for device in devices:
        pl.semaphore_signal(barrier, inc=1, device_id=device, device_id_type=MESH)
    return len(devices)


def greet_seq(here):
    barrier = pltpu.get_barrier_semaphore()

    def body(i, carry):
        pl.semaphore_signal(
            barrier, inc=1, device_id=here.peer((here.q + i) % 32), device_id_type=MESH
        )
        return carry

    lax.fori_loop(1, 32, body, 0)
    return 31


def rows(start, size):
    return pl.ds(pl.multiple_of(start * size, size), size)


TN = (((0,), (0,)), ((), ()))
NT = (((1,), (1,)), ((), ()))
NN = (((1,), (0,)), ((), ()))


def dot(a, b, dims):
    return lax.dot_general(a, b, dims, preferred_element_type=F32)


def lanes(start, size):
    return pl.ds(pl.multiple_of(start, LANES), size)


def block_of(ref, s, b):
    return ref.at[pl.ds(2 * s, 2), :, :, lanes(b * LANES, LANES)]


def column(ref, q, slot):
    return ref.at[pl.ds(2 * q, 2), :, :, pl.ds(slot * LANES, LANES)]


class ToChannels:
    def __init__(self, here, src, cols, sems):
        self.here, self.src, self.cols = here, src, cols
        self.send, self.recv, self.esend, self.erecv = sems

        @pl.when(jnp.logical_not(here.has_extra()))
        def _():
            cols[:, :, :, LANES:] = jnp.zeros((64, 2, 16, LANES), BF)

    def start(self, half):
        here, src, cols = self.here, self.src, self.cols
        first, count = ((0, 18), (18, 14))[half]

        def body(i, carry):
            dest = first + (i + here.q) % count
            block, place = block_of(src, dest // 6, dest % 6), column(cols, here.q, 0)

            @pl.when(dest != here.q)
            def _():
                remote(block, place, self.send, self.recv, here.peer(dest)).start()

            @pl.when(dest == here.q)
            def _():
                pltpu.make_async_copy(block, place, self.recv).start()

            return carry

        lax.fori_loop(0, count, body, 0)
        if half == 1:
            for e in range(4):
                dest = here.extra_of(e)
                block, place = block_of(src, 5, 2 + e), column(cols, here.q, 1)

                @pl.when(dest != here.q)
                def _():
                    remote(block, place, self.esend.at[e], self.erecv, here.peer(dest)).start()

                @pl.when(dest == here.q)
                def _():
                    pltpu.make_async_copy(block, place, self.erecv).start()

    def arrive(self):
        drain(self.cols.at[:, :, :, pl.ds(0, LANES)], self.recv)

        @pl.when(self.here.has_extra())
        def _():
            drain(self.cols.at[:, :, :, pl.ds(LANES, LANES)], self.erecv)

    def finish(self):
        drain(self.cols.at[pl.ds(0, 62), :, :, pl.ds(0, LANES)], self.send)
        for e in range(4):
            @pl.when(self.here.extra_of(e) != self.here.q)
            def _():
                drain(self.cols.at[pl.ds(0, 2), :, :, pl.ds(0, LANES)], self.esend.at[e])


class ToPatches:
    def __init__(self, here, cols, out, sems):
        self.here, self.cols, self.out = here, cols, out
        self.send, self.recv, self.esend = sems

    def start(self, dest):
        here, cols, out = self.here, self.cols, self.out
        place = block_of(out, here.q // 6, here.q % 6)
        extra = block_of(out, 5, 2 + here.y)
        sem = self.recv.at[here.q // 18]

        @pl.when(dest != here.q)
        def _():
            remote(column(cols, dest, 0), place, self.send, sem, here.peer(dest)).start()

            @pl.when(here.has_extra())
            def _():
                remote(
                    column(cols, dest, 1), extra, self.esend, self.recv.at[1], here.peer(dest)
                ).start()

        @pl.when(dest == here.q)
        def _():
            pltpu.make_async_copy(column(cols, dest, 0), place, sem).start()

            @pl.when(here.has_extra())
            def _():
                pltpu.make_async_copy(column(cols, dest, 1), extra, self.recv.at[1]).start()

    def arrive(self, half):
        drain(self.out.at[pl.ds(6 * half, 6)], self.recv.at[half])

    def finish(self):
        many = self.cols.at[pl.ds(0, 62), :, :, pl.ds(0, LANES)]
        drain(many, self.send)

        @pl.when(self.here.has_extra())
        def _():
            drain(many, self.esend)


class Gather:
    def __init__(self, here, parts, fulls, sems):
        self.here, self.fulls, self.parts = here, fulls, parts
        self.own, self.send, self.recv, self.bsend, self.brecv = sems
        self.copies = []
        self.legs = [{}, {}]
        c, y, xh, z = here.c, here.y, here.xh, here.z
        self.locals = []
        for w in range(2):
            copy = pltpu.make_async_copy(parts[w], fulls[w].at[y, xh, z], self.own.at[w])
            copy.start()
            self.locals.append(copy)
            self.push(w, 0, fulls[w].at[y, xh, z, c], here.at(x=(here.x + 2) % 4), parts[w].at[c])

    def piece(self, w, first, second, c, half=None):
        here = self.here
        y = (here.y + c * first + (1 - c) * second) % 4
        z = (here.z + (1 - c) * first + c * second) % 4
        h = slice(None) if half is None else half
        return self.fulls[w].at[y, h, z, c]

    def towards(self, axis, step):
        here = self.here
        along_y = here.c if axis == 0 else 1 - here.c
        return here.at(y=(here.y + along_y * step) % 4, z=(here.z + (1 - along_y) * step) % 4)

    def push(self, w, k, ref, device, src=None):
        copy = remote(
            ref if src is None else src, ref, self.send.at[w, k], self.recv.at[w, k], device
        )
        copy.start()
        self.copies.append(copy)
        self.legs[w][k] = copy

    def share(self, w, k, ref):
        copy = remote(ref, ref, self.bsend.at[w, k], self.brecv.at[w, k], self.here.sibling())
        copy.start()
        self.copies.append(copy)

    def around(self, w, ks, half, src=None):
        ref = self.piece(w, 0, 0, self.here.c, half)
        for k, axis, step in zip(ks, (0, 0, 1, 1), (1, 3, 1, 3)):
            self.push(w, k, ref, self.towards(axis, step), src)

    def launch(self, w):
        self.around(w, (1, 2, 5, 6), self.here.xh, self.parts[w].at[self.here.c])

    def crossed(self, w):
        here = self.here
        self.legs[w][0].wait_recv()
        self.around(w, (21, 22, 23, 24), 1 - here.xh)
        self.share(w, 0, self.piece(w, 0, 0, here.c, 1 - here.xh))
        self.locals[w].wait()

    def second(self, w, o):
        ref = self.piece(w, o, 0, self.here.c)
        self.push(w, 5 + 4 * o, ref, self.towards(1, 1))
        self.push(w, 6 + 4 * o, ref, self.towards(1, 3))

    def first_near(self, w):
        c = self.here.c
        self.legs[w][1].wait_recv()
        self.legs[w][21].wait_recv()
        self.push(w, 3, self.piece(w, 3, 0, c, 0), self.towards(0, 1))
        self.second(w, 3)
        self.share(w, 1, self.piece(w, 3, 0, c))
        self.legs[w][2].wait_recv()
        self.legs[w][22].wait_recv()
        self.push(w, 4, self.piece(w, 1, 0, c, 1), self.towards(0, 3))
        self.second(w, 1)
        self.share(w, 2, self.piece(w, 1, 0, c))

    def first_far(self, w):
        self.legs[w][3].wait_recv()
        self.legs[w][4].wait_recv()
        self.second(w, 2)
        self.share(w, 3, self.piece(w, 2, 0, self.here.c))

    def second_near(self, w, o):
        c = self.here.c
        self.legs[w][5 + 4 * o].wait_recv()
        if o == 0:
            self.legs[w][23].wait_recv()
        self.push(w, 7 + 4 * o, self.piece(w, o, 3, c, 0), self.towards(1, 1))
        self.share(w, 4 + 3 * o, self.piece(w, o, 3, c))
        self.legs[w][6 + 4 * o].wait_recv()
        if o == 0:
            self.legs[w][24].wait_recv()
        self.push(w, 8 + 4 * o, self.piece(w, o, 1, c, 1), self.towards(1, 3))
        self.share(w, 5 + 3 * o, self.piece(w, o, 1, c))

    def second_far(self, w, o):
        self.legs[w][7 + 4 * o].wait_recv()
        self.legs[w][8 + 4 * o].wait_recv()
        self.share(w, 6 + 3 * o, self.piece(w, o, 2, self.here.c))

    def shared_near(self, w):
        other = 1 - self.here.c
        drain(self.piece(w, 0, 0, other, 1 - self.here.xh), self.brecv.at[w, 0])
        for k, o in ((1, 3), (2, 1), (3, 2)):
            drain(self.piece(w, o, 0, other), self.brecv.at[w, k])
        for o in range(4):
            drain(self.piece(w, o, 3, other), self.brecv.at[w, 4 + 3 * o])
            drain(self.piece(w, o, 1, other), self.brecv.at[w, 5 + 3 * o])

    def shared_far(self, w):
        for o in range(4):
            drain(self.piece(w, o, 2, 1 - self.here.c), self.brecv.at[w, 6 + 3 * o])

    def finish(self):
        for copy in self.copies:
            copy.wait_send()


def add_into(target, *others):
    lead = target.shape[:-2]

    def body(i, carry):
        index = []
        rest = i
        for size in reversed(lead):
            index.append(rest % size)
            rest = rest // size
        index = tuple(reversed(index))
        total = target[index].astype(F32)
        for other in others:
            total += other[index].astype(F32)
        target[index] = total.astype(BF)
        return carry

    lax.fori_loop(0, math.prod(lead), body, 0, unroll=min(8, math.prod(lead)))


PARTS = (
    ("x", 48, 128), ("y", 48, 128), ("z", 48, 128),
    ("y", 16, 384), ("z", 16, 384), ("x", 16, 256),
    ("y", 16, 256), ("z", 16, 384), ("x", 16, 384),
)
PLANES = {"x": ("y", "z"), "y": ("z", "x"), "z": ("x", "y")}


class PartSum:
    def __init__(self, here, p, acc, bufs, send, recv):
        self.here, self.p, self.acc = here, p, acc
        self.low, self.high, self.up_buf, self.down_buf, self.turn_buf, self.end_buf = bufs
        self.send, self.recv = send, recv
        self.copies = []
        self.axis = PARTS[p][0]
        self.me = getattr(here, self.axis)

    def index(self, at):
        full = slice(None)
        if "x" in at:
            return (at.get("y", full), at["x"] // 2, at.get("z", full), at["x"] % 2)
        return (at.get("y", full), full, at.get("z", full), full)

    def chunk(self, pos, half=None):
        index = list(self.index({self.axis: pos}))
        if half is not None:
            if self.axis == "y":
                index[1] = half
            else:
                index[0] = pl.ds(2 * half, 2)
        return self.acc.at[tuple(index)]

    def to(self, step):
        return self.here.at(**{self.axis: (self.me + step) % 4})

    def push(self, k, src, dst, device):
        copy = remote(src, dst, self.send.at[self.p, k], self.recv.at[self.p, k], device)
        copy.start()
        self.copies.append(copy)
        return copy

    def begin(self):
        far = (self.me + 2) % 4
        self.legs = (
            self.push(0, self.chunk(far, 0), self.low, self.to(1)),
            self.push(1, self.chunk(far, 1), self.high, self.to(3)),
        )

    def relay(self):
        up, down = (self.me + 1) % 4, (self.me + 3) % 4
        self.legs[0].wait_recv()
        add_into(self.chunk(up, 0), self.low)
        one = self.push(2, self.chunk(up), self.up_buf, self.to(1))
        self.legs[1].wait_recv()
        add_into(self.chunk(down, 1), self.high)
        two = self.push(3, self.chunk(down), self.down_buf, self.to(3))
        self.legs = (one, two)

    def across(self, k, name, buf, at):
        me = getattr(self.here, name)
        for step in (1, 3, 2):
            pos = (me + step) % 4
            remote(
                self.acc.at[self.index({**at, name: pos})], buf.at[me],
                self.send.at[self.p, k], self.recv.at[self.p, k], self.here.at(**{name: pos}),
            ).start()

    def cross(self):
        self.legs[0].wait_recv()
        self.legs[1].wait_recv()
        add_into(self.chunk(self.me), self.up_buf, self.down_buf)
        self.across(4, PLANES[self.axis][0], self.turn_buf, {self.axis: self.me})

    def turn(self):
        a, b = PLANES[self.axis]
        me = getattr(self.here, a)
        at = {self.axis: self.me, a: me}
        drain(self.turn_buf.at[pl.ds(0, 3)], self.recv.at[self.p, 4])
        add_into(
            self.acc.at[self.index(at)], *[self.turn_buf.at[(me + k) % 4] for k in (1, 2, 3)]
        )
        self.across(5, b, self.end_buf, at)

    def end(self):
        a, b = PLANES[self.axis]
        me = getattr(self.here, b)
        at = {self.axis: self.me, a: getattr(self.here, a), b: me}
        drain(self.end_buf.at[pl.ds(0, 3)], self.recv.at[self.p, 5])
        total = self.acc[self.index(at)].astype(F32)
        for k in (1, 2, 3):
            total += self.end_buf[(me + k) % 4].astype(F32)
        return total

    def finish(self):
        for copy in self.copies:
            copy.wait_send()
        drain(self.turn_buf.at[pl.ds(0, 3)], self.send.at[self.p, 4])
        drain(self.end_buf.at[pl.ds(0, 3)], self.send.at[self.p, 5])


def part_shape(p):
    return (4, 2, 4, 2) + PARTS[p][1:]


def part_buffers(p):
    axis, tail = PARTS[p][0], PARTS[p][1:]
    whole = {"x": (4, 4), "y": (2, 4, 2), "z": (4, 2, 2)}[axis]
    half = whole[1:] if axis == "y" else (2,) + whole[1:]
    last = (2, 2) if PLANES[axis][1] == "x" else (4,)
    shapes = [half + tail] * 2 + [whole + tail] * 2 + [(4,) + last + tail, (4,) + tail]
    return [pltpu.VMEM(s, BF) for s in shapes]


DMA = pltpu.SemaphoreType.DMA
SCRATCH = dict(
    scale_first=((384, 1), F32), scale_second=((384, 1), F32),
    spectra=((384, 768), BF), cot=((384, 768), BF), grad_input=((384, 768), BF),
    win=((4, 2, 4, 2, 32, 1024), BF), wout=((4, 2, 4, 2, 32, 1024), BF),
    chin=((1536, 768), BF), chout=((1536, 768), BF),
    normed=((12, 2, 16, 768), BF), tm=((12, 2, 16, 768), BF), ng=((12, 2, 16, 768), BF),
    mixg=((12, 2, 16, 768), BF), ns=((384, 768), BF), mg=((384, 768), F32),
    cact=((384, 1536), BF), cgrad=((384, 1536), BF),
    cact_s=((384, 1536), BF), cgrad_s=((384, 1536), BF),
    ns_s=((384, 384), BF), cot_s=((384, 384), BF),
    cols_t=((256, 2048), BF), second=((192, 768), F32), down=((384, 1536), F32),
    cols=((64, 2, 16, 256), BF), cols2=((64, 2, 16, 256), BF),
    cols_s=((64, 16, 256), BF), cols2_s=((64, 16, 256), BF),
    hidden=((256, 1024), F32), slope=((256, 1024), F32),
    act=((256, 1024), BF), act_s=((256, 1024), BF),
    hg=((256, 1024), BF), hg_s=((256, 1024), BF),
    mixb=((64, 2, 16, 256), BF), ncg=((64, 2, 16, 256), BF),
    fin=((4, 48, 384), F32), sum0=((16, 1024), F32), sum1=((16, 1024), F32),
    sum2=((12, 768), F32), sum3=((12, 768), F32),
)
SEMS = dict(
    load=(5,), a1_send=(), a1_recv=(), a1_esend=(4,), a1_erecv=(),
    a3_send=(), a3_recv=(), a3_esend=(4,), a3_erecv=(),
    a2_send=(), a2_recv=(2,), a2_esend=(),
    a4_send=(), a4_recv=(2,), a4_esend=(),
    w_own=(2,), w_send=(2, 25), w_recv=(2, 25), w_bsend=(2, 16), w_brecv=(2, 16),
    r_send=(9, 6), r_recv=(9, 6),
    s_send=(11,), s_recv=(11,), f_send=(3,), f_recv=(3,),
)


def block_kernel(
    spectra_in, cot_in, w_in, w_out, ch_in, ch_out, grad_out, o0, o1, o2, o3, *scratch
):
    v = types.SimpleNamespace(**dict(zip(list(SCRATCH) + list(SEMS), scratch)))
    spectra, cot, grad_input = v.spectra, v.cot, v.grad_input
    bufs = scratch[len(SCRATCH) + len(SEMS):]
    sums = scratch[len(SCRATCH) + len(SEMS) + 6 * len(PARTS):]
    here = Here()
    c = here.c
    sib = here.sibling()
    cross = here.at(x=here.xh * 2 + 1 - here.xl, c=1 - c)
    partners = [sib, cross]
    for k in (1, 3):
        x = (here.x + k) % 4
        partners += [here.at(x=x, z=(here.z + n) % 4) for n in range(4)]
        partners += [here.at(x=x, y=(here.y + n) % 4) for n in range(1, 4)]
    loads = [
        pltpu.make_async_copy(src, dst, v.load.at[k])
        for k, (src, dst) in enumerate((
            (spectra_in, spectra), (cot_in, cot), (ch_in, v.chin), (ch_out, v.chout),
        ))
    ]
    for copy in loads:
        copy.start()
    count = greet_seq(here) + greet(partners)
    loads.pop(0).wait()

    def norm_first(i, carry):
        unit, scale = normalize(spectra[rows(i, 32), :].astype(F32))
        v.normed[i] = unit.astype(BF).reshape(2, 16, 768)
        v.scale_first[rows(i, 32), :] = scale
        return carry

    lax.fori_loop(0, 12, norm_first, 0, unroll=6)
    pl.semaphore_wait(pltpu.get_barrier_semaphore(), count)

    shared = []

    def share(src, dst):
        k = len(shared)
        copy = remote(src, dst, v.s_send.at[k], v.s_recv.at[k], sib)
        copy.start()
        shared.append(copy)
        return copy

    gather = Gather(
        here, (w_in, w_out), (v.win, v.wout),
        (v.w_own, v.w_send, v.w_recv, v.w_bsend, v.w_brecv),
    )
    first = ToChannels(
        here, v.normed, v.cols, (v.a1_send, v.a1_recv, v.a1_esend, v.a1_erecv)
    )
    both = range(2)
    for w in both:
        gather.launch(w)
    first.start(0)
    first.start(1)
    for w in both:
        gather.crossed(w)
    for copy in loads:
        copy.wait()
    share(cot.at[:, lanes(384 * (1 - c), 384)], v.cot_s)

    def channel_down(i, carry):
        v.down[:, lanes(256 * i, 256)] = dot(cot[...], v.chout[rows(i, 256), :], NT)
        return carry

    for w in both:
        gather.first_near(w)
    lax.fori_loop(0, 3, channel_down, 0)
    for w in both:
        gather.second_near(w, 0)
    for w in both:
        gather.first_far(w)
    lax.fori_loop(3, 6, channel_down, 0)
    for o in (3, 1):
        for w in both:
            gather.second_near(w, o)
    first.arrive()
    share(v.cols.at[:, 1 - c], v.cols_s)
    for w in both:
        gather.second_near(w, 2)

    def turn_cols(y, carry):
        v.cols_t[:, lanes(512 * y, 512)] = v.cols[pl.ds(16 * y, 16)].reshape(512, 256).T
        return carry

    lax.fori_loop(0, 4, turn_cols, 0, unroll=2)
    for o in (0, 3, 1, 2):
        gather.second_far(0, o)
    gather.shared_near(0)
    gather.shared_far(0)

    def project(source, weight):
        def step(y, start):
            left = source[pl.ds(16 * y, 16)].reshape(512, 256)
            part = dot(left, weight[y].reshape(512, 1024), TN)
            if start:
                v.hidden[...] = part
            else:
                v.hidden[...] += part

        step(0, True)
        for y in range(1, 4):
            step(y, False)

    def hidden_of(i, carry):
        part = lanes(256 * i, 256)
        weight = v.win[:, :, :, :, :, part].reshape(2048, 256)
        v.hidden[:, part] = dot(v.cols_t[...], weight, NN)
        return carry

    lax.fori_loop(0, 4, hidden_of, 0, unroll=4)

    def token_gelu(i, carry):
        at = rows(i, 16)
        value, slope = gelu_pair(v.hidden[at, :])
        v.act[at, :] = value.astype(BF)
        v.slope[at, :] = slope
        return carry

    lax.fori_loop(0, 16, token_gelu, 0, unroll=8)
    share(v.act, v.act_s)

    def spread(weight, source, target, transfer, spots):
        left = jnp.concatenate([weight[y, :, z].reshape(128, 1024) for y, z in spots], axis=0)
        value = dot(left, source[...], NT).astype(BF).reshape(len(spots), 2, 2, 2, 16, 256)
        for k, (y, z) in enumerate(spots):
            for xh in range(2):
                dest = 8 * y + 4 * xh + z
                target[pl.ds(2 * dest, 2)] = value[k, xh]
                transfer.start(dest)

    def off(name, step):
        return (getattr(here, name) + step) % 4

    second = ToPatches(
        here, v.mixb, v.tm, (v.a2_send, v.a2_recv, v.a2_esend)
    )
    gather.shared_near(1)

    def near(i, carry):
        z = off("z", i + i // 2)
        spread(
            v.wout, v.act, v.mixb, second, [(off("y", step), z) for step in (1, 3, 0)]
        )
        return carry

    lax.fori_loop(0, 3, near, 0)
    for o in (0, 3, 1, 2):
        gather.second_far(1, o)
    gather.shared_far(1)
    spread(
        v.wout, v.act, v.mixb, second,
        [(off("y", 2), off("z", step)) for step in (1, 3, 0)],
    )
    spread(
        v.wout, v.act, v.mixb, second,
        [(off("y", step), off("z", 2)) for step in (2, 1, 3, 0)],
    )
    gather.finish()
    first.finish()

    third = ToChannels(
        here, v.mixg, v.cols2, (v.a3_send, v.a3_recv, v.a3_esend, v.a3_erecv)
    )

    def middle_of(at):
        source = spectra[rows(at, 32), :].astype(F32)
        mix = v.tm[at].reshape(32, 768).astype(F32)
        return (source + mix).astype(BF).astype(F32)

    for half in range(2):
        second.arrive(half)
        span = pl.ds(192 * half, 192)

        def norm_second(i, carry):
            at = half * 6 + i
            unit, scale = normalize(middle_of(at))
            v.ns[rows(at, 32), :] = unit.astype(BF)
            v.scale_second[rows(at, 32), :] = scale
            return carry

        lax.fori_loop(0, 6, norm_second, 0, unroll=6)

        def hidden_units(i, carry):
            part = lanes(256 * i, 256)
            own = rows(i, 256)
            value, slope = gelu_pair(dot(v.ns[span, :], v.chin[own, :], NT))
            v.cact[span, part] = value.astype(BF)
            v.cgrad[span, part] = (v.down[span, part] * slope).astype(BF)
            return carry

        lax.fori_loop(0, 6, hidden_units, 0, unroll=3)
        for src, dst in ((v.cgrad, v.cgrad_s), (v.cact, v.cact_s)):
            share(src.at[span], dst.at[span])
        share(v.ns.at[span, lanes(384 * (1 - c), 384)], v.ns_s.at[span])
        v.second[...] = dot(v.cgrad[span, :], v.chin[...], NN)

        def back_second(i, carry):
            at = half * 6 + i
            unit = v.ns[rows(at, 32), :].astype(F32)
            scale = v.scale_second[rows(at, 32), :]
            upstream = v.second[rows(i, 32), :]
            value = cot[rows(at, 32), :].astype(F32) + norm_back(unit, scale, upstream)
            v.mg[rows(at, 32), :] = value
            v.mixg[at] = value.astype(BF).reshape(2, 16, 768)
            return carry

        lax.fori_loop(0, 6, back_second, 0, unroll=6)
        third.start(half)

    for copy in shared:
        copy.wait_recv()
    half_lanes = lanes(384 * c, 384)
    for g, (act, tok, act_s, tok_s) in enumerate((
        (v.cgrad, v.ns, v.cgrad_s, v.ns_s), (v.cact, cot, v.cact_s, v.cot_s),
    )):
        def channel_sum(y, carry):
            part = lanes(384 * y, 384)
            total = dot(act[:, part], tok[:, half_lanes], TN)
            total += dot(act_s[:, part], tok_s[...], TN)
            total = total.astype(BF).reshape(2, 4, 48, 384)
            for p in range(3):
                sums[p][y, :, :, g] = total[..., 128 * p:128 * p + 128]
            return carry

        lax.fori_loop(0, 4, channel_sum, 0, unroll=4)

    parts = [
        PartSum(here, p, sums[p], bufs[6 * p:6 * p + 6], v.r_send, v.r_recv)
        for p in range(len(PARTS))
    ]
    channel_parts, early, late = parts[:3], parts[3:6], parts[6:]
    for part in channel_parts:
        part.begin()
    for part in channel_parts:
        part.relay()

    second.finish()
    third.arrive()
    share_cols2 = share(v.cols2.at[:, 1 - c], v.cols2_s)
    project(v.cols2, v.wout)

    def token_grad(i, carry):
        at = rows(i, 16)
        v.hg[at, :] = (v.hidden[at, :] * v.slope[at, :]).astype(BF)
        return carry

    lax.fori_loop(0, 16, token_grad, 0, unroll=8)
    share_hg = share(v.hg, v.hg_s)

    def token_sum(left, left_s, right, right_s, targets):
        def step(y, carry):
            own = left[pl.ds(16 * y, 16), c].reshape(256, 256)
            other = left_s[pl.ds(16 * y, 16)].reshape(256, 256)
            total = dot(own, right[...], NN) + dot(other, right_s[...], NN)
            total = total.astype(BF).reshape(2, 4, 2, 16, 1024)
            place = 0
            for p in targets:
                width = PARTS[p][2]
                sums[p][y] = total[..., place:place + width]
                place += width
            return carry

        lax.fori_loop(0, 4, step, 0, unroll=4)

    share_cols2.wait_recv()
    token_sum(
        v.cols2, v.cols2_s, v.act, v.act_s, (3, 4, 5),
    )
    for part in early:
        part.begin()
    for part in channel_parts:
        part.cross()
    share_hg.wait_recv()
    token_sum(
        v.cols, v.cols_s, v.hg, v.hg_s, (6, 7, 8),
    )
    for part in late:
        part.begin()
    for part in early:
        part.relay()
    for part in channel_parts:
        part.turn()
    fourth = ToPatches(
        here, v.ncg, v.ng, (v.a4_send, v.a4_recv, v.a4_esend)
    )

    def back(i, carry):
        z = off("z", 3 - i)
        spread(
            v.win, v.hg, v.ncg, fourth, [(off("y", step), z) for step in (2, 1, 3, 0)]
        )
        return carry

    lax.fori_loop(0, 4, back, 0, unroll=2)
    for part in late:
        part.relay()
    for part in early:
        part.cross()

    def input_grad(half):
        fourth.arrive(half)

        def step(i, carry):
            at = half * 6 + i
            unit = v.normed[at].reshape(32, 768).astype(F32)
            scale = v.scale_first[rows(at, 32), :]
            upstream = v.ng[at].reshape(32, 768).astype(F32)
            value = v.mg[rows(at, 32), :] + norm_back(unit, scale, upstream)
            grad_input[rows(at, 32), :] = value.astype(BF)
            return carry

        lax.fori_loop(0, 6, step, 0, unroll=6)

    for p, part in enumerate(channel_parts):
        v.fin[here.d, :, 128 * p:128 * p + 128] = part.end()
    input_grad(0)
    swaps = []
    for k, device in enumerate((sib, here.at(x=here.xh * 2 + 1 - here.xl), cross)):
        copy = remote(
            v.fin.at[here.d], v.fin.at[here.d], v.f_send.at[k], v.f_recv.at[k], device
        )
        copy.start()
        swaps.append(copy)
    for part in early:
        part.turn()
    for part in late:
        part.cross()
    input_grad(1)
    stores = [pltpu.make_async_copy(grad_input, grad_out, v.load.at[4])]
    stores[0].start()
    for part in late:
        part.turn()

    def gather_up(out, group):
        place = 0
        for part in group:
            width = PARTS[part.p][2]
            out[:, place:place + width] = part.end()
            place += width

    def keep(k, src, dst):
        copy = pltpu.make_async_copy(src, dst, v.load.at[k])
        copy.start()
        return copy

    gather_up(v.sum1, early)
    stores.append(keep(0, v.sum1, o1))
    for copy in swaps:
        copy.wait()
    for d in range(4):
        @pl.when(here.d == d)
        def _():
            for total, g in ((v.sum2, 0), (v.sum3, 2)):
                for k in range(2):
                    total[:, 384 * k:384 * k + 384] = v.fin[g + k, 12 * d:12 * d + 12]
    stores.append(keep(1, v.sum2, o2))
    stores.append(keep(2, v.sum3, o3))
    for part in channel_parts + early:
        part.finish()
    for copy in shared:
        copy.wait_send()
    third.finish()
    fourth.finish()
    gather_up(v.sum0, late)
    stores.append(keep(3, v.sum0, o0))
    for part in late:
        part.finish()
    for copy in stores:
        copy.wait()


def hand_over(*refs):
    for src, dst in zip(refs[:5], refs[5:]):
        dst[...] = src[...]


def local(spectra_in, cotangent, tok_in_w, tok_out_w, ch_in_w, ch_out_w):
    vmem = pl.BlockSpec(memory_space=pltpu.VMEM)
    scratch = [pltpu.VMEM(shape, kind) for shape, kind in SCRATCH.values()]
    scratch += [DMA(shape) if shape else DMA for shape in SEMS.values()]
    for p in range(len(PARTS)):
        scratch += part_buffers(p)
    scratch += [pltpu.VMEM(part_shape(p), BF) for p in range(len(PARTS))]
    shapes = (
        jax.ShapeDtypeStruct((384, 768), BF),
        jax.ShapeDtypeStruct((16, 1024), F32),
        jax.ShapeDtypeStruct((16, 1024), F32),
        jax.ShapeDtypeStruct((12, 768), F32),
        jax.ShapeDtypeStruct((12, 768), F32),
    )
    outs = pl.pallas_call(
        block_kernel,
        out_shape=shapes,
        in_specs=[ANY] * 6, out_specs=(ANY,) * 5,
        scratch_shapes=scratch,
        compiler_params=pltpu.CompilerParams(
            collective_id=0, has_side_effects=True, vmem_limit_bytes=60 * 1024 * 1024
        ),
        name="mixer_block_backward",
    )(
        spectra_in.reshape(384, 768), cotangent.reshape(384, 768),
        tok_in_w.reshape(2, 32, 1024), tok_out_w.reshape(2, 32, 1024), ch_in_w, ch_out_w,
    )
    grad_input, *weights = pl.pallas_call(
        hand_over, out_shape=shapes, in_specs=[vmem] * 5, out_specs=(vmem,) * 5, name="hand_over",
    )(*outs)
    return (grad_input.reshape(6, 64, 768), *weights)


def solution(mesh):
    in_specs = (
        P("dp", "seq", None),
        P("dp", "seq", None),
        P("seq", None),
        P("seq", None),
        P(),
        P(),
    )
    out_specs = (
        P("dp", "seq", None),
        P(("seq", "dp"), None),
        P(("seq", "dp"), None),
        P(("seq", "dp"), None),
        P(("seq", "dp"), None),
    )
    return jax.shard_map(local, mesh=mesh, in_specs=in_specs, out_specs=out_specs, check_vma=False)
```

```python
import math
import types

import jax
import jax.numpy as jnp
from jax import lax
from jax.experimental import pallas as pl
from jax.experimental.pallas import tpu as pltpu
from jax.sharding import PartitionSpec as P

BF = jnp.bfloat16
F32 = jnp.float32
MESH = pl.DeviceIdType.MESH
ANY = pl.BlockSpec(memory_space=pl.ANY)
LANES = 128


def normalize(values):
    center = values - jnp.mean(values, axis=-1, keepdims=True)
    inv_scale = lax.rsqrt(jnp.mean(center * center, axis=-1, keepdims=True) + 1e-05)
    return (center * inv_scale, inv_scale)


def norm_back(unit, inv_scale, upstream):
    first = jnp.mean(upstream, axis=-1, keepdims=True)
    second = jnp.mean(upstream * unit, axis=-1, keepdims=True)
    return inv_scale * (upstream - first - unit * second)


def gelu_pair(values):
    factor = math.sqrt(2.0 / math.pi)
    square = values * values
    half = 0.5 + 0.5 * jnp.tanh(values * (factor + (factor * 0.044715) * square))
    result = values * half
    slope = half + result * (1.0 - half) * (2.0 * factor + (6.0 * factor * 0.044715) * square)
    return (result, slope)


class Here:
    def __init__(self):
        self.q = lax.axis_index("seq")
        self.d = lax.axis_index("dp")
        self.y = self.q // 8
        self.xh = (self.q // 4) % 2
        self.z = self.q % 4
        self.xl = self.d // 2
        self.c = self.d % 2
        self.x = self.xh * 2 + self.xl

    def at(self, x=None, y=None, z=None, c=None):
        x = self.x if x is None else x
        y = self.y if y is None else y
        z = self.z if z is None else z
        c = self.c if c is None else c
        return {"seq": (y * 2 + x // 2) * 4 + z, "dp": (x % 2) * 2 + c}

    def peer(self, q):
        return {"seq": q, "dp": self.d}

    def sibling(self):
        return {"seq": self.q, "dp": self.d + 1 - 2 * self.c}

    def extra_of(self, e):
        return 8 * e + ((e + self.d // 2) % 2) * 4 + (e + self.d) % 4

    def has_extra(self):
        return self.q == self.extra_of(self.y)


def remote(src, dst, send, recv, device):
    return pltpu.make_async_remote_copy(
        src_ref=src, dst_ref=dst, send_sem=send, recv_sem=recv,
        device_id=device, device_id_type=MESH,
    )


def drain(ref, sem):
    pltpu.make_async_copy(ref, ref, sem).wait()


def greet(devices):
    barrier = pltpu.get_barrier_semaphore()
    for device in devices:
        pl.semaphore_signal(barrier, inc=1, device_id=device, device_id_type=MESH)
    return len(devices)


def greet_seq(here):
    barrier = pltpu.get_barrier_semaphore()

    def body(i, carry):
        pl.semaphore_signal(
            barrier, inc=1, device_id=here.peer((here.q + i) % 32), device_id_type=MESH
        )
        return carry

    lax.fori_loop(1, 32, body, 0)
    return 31


def rows(start, size):
    return pl.ds(pl.multiple_of(start * size, size), size)


TN = (((0,), (0,)), ((), ()))
NT = (((1,), (1,)), ((), ()))
NN = (((1,), (0,)), ((), ()))


def dot(a, b, dims):
    return lax.dot_general(a, b, dims, preferred_element_type=F32)


def lanes(start, size):
    return pl.ds(pl.multiple_of(start, LANES), size)


def block_of(ref, s, b):
    return ref.at[pl.ds(2 * s, 2), :, :, lanes(b * LANES, LANES)]


def column(ref, q, slot):
    return ref.at[pl.ds(2 * q, 2), :, :, pl.ds(slot * LANES, LANES)]


class ToChannels:
    def __init__(self, here, src, cols, sems):
        self.here, self.src, self.cols = here, src, cols
        self.send, self.recv, self.esend, self.erecv = sems

        @pl.when(jnp.logical_not(here.has_extra()))
        def _():
            cols[:, :, :, LANES:] = jnp.zeros((64, 2, 16, LANES), BF)

    def start(self, half):
        here, src, cols = self.here, self.src, self.cols
        first, count = ((0, 18), (18, 14))[half]

        def body(i, carry):
            dest = first + (i + here.q) % count
            block, place = block_of(src, dest // 6, dest % 6), column(cols, here.q, 0)

            @pl.when(dest != here.q)
            def _():
                remote(block, place, self.send, self.recv, here.peer(dest)).start()

            @pl.when(dest == here.q)
            def _():
                pltpu.make_async_copy(block, place, self.recv).start()

            return carry

        lax.fori_loop(0, count, body, 0)
        if half == 1:
            for e in range(4):
                dest = here.extra_of(e)
                block, place = block_of(src, 5, 2 + e), column(cols, here.q, 1)

                @pl.when(dest != here.q)
                def _():
                    remote(block, place, self.esend.at[e], self.erecv, here.peer(dest)).start()

                @pl.when(dest == here.q)
                def _():
                    pltpu.make_async_copy(block, place, self.erecv).start()

    def arrive(self):
        drain(self.cols.at[:, :, :, pl.ds(0, LANES)], self.recv)

        @pl.when(self.here.has_extra())
        def _():
            drain(self.cols.at[:, :, :, pl.ds(LANES, LANES)], self.erecv)

    def finish(self):
        drain(self.cols.at[pl.ds(0, 62), :, :, pl.ds(0, LANES)], self.send)
        for e in range(4):
            @pl.when(self.here.extra_of(e) != self.here.q)
            def _():
                drain(self.cols.at[pl.ds(0, 2), :, :, pl.ds(0, LANES)], self.esend.at[e])


class ToPatches:
    def __init__(self, here, cols, out, sems):
        self.here, self.cols, self.out = here, cols, out
        self.send, self.recv, self.esend = sems

    def start(self, dest, other):
        here, cols, out = self.here, self.cols, self.out
        place = block_of(out, here.q // 6, here.q % 6)
        extra = block_of(out, 5, 2 + here.y)
        sem = self.recv.at[here.q // 18]

        def away():
            remote(column(cols, dest, 0), place, self.send, sem, here.peer(dest)).start()

            @pl.when(here.has_extra())
            def _():
                remote(
                    column(cols, dest, 1), extra, self.esend, self.recv.at[1], here.peer(dest)
                ).start()

        if other:
            away()
            return
        pl.when(dest != here.q)(away)

        @pl.when(dest == here.q)
        def _():
            pltpu.make_async_copy(column(cols, dest, 0), place, sem).start()

            @pl.when(here.has_extra())
            def _():
                pltpu.make_async_copy(column(cols, dest, 1), extra, self.recv.at[1]).start()

    def arrive(self, half):
        drain(self.out.at[pl.ds(6 * half, 6)], self.recv.at[half])

    def finish(self):
        many = self.cols.at[pl.ds(0, 62), :, :, pl.ds(0, LANES)]
        drain(many, self.send)

        @pl.when(self.here.has_extra())
        def _():
            drain(many, self.esend)


class Gather:
    def __init__(self, here, parts, fulls, sems):
        self.here, self.fulls, self.parts = here, fulls, parts
        self.own, self.send, self.recv, self.bsend, self.brecv = sems
        self.copies = []
        self.legs = [{}, {}]
        c, y, xh, z = here.c, here.y, here.xh, here.z
        self.locals = []
        for w in range(2):
            copy = pltpu.make_async_copy(parts[w], fulls[w].at[y, xh, z], self.own.at[w])
            copy.start()
            self.locals.append(copy)
            self.push(w, 0, fulls[w].at[y, xh, z, c], here.at(x=(here.x + 2) % 4), parts[w].at[c])

    def piece(self, w, first, second, c, half=None):
        here = self.here
        y = (here.y + c * first + (1 - c) * second) % 4
        z = (here.z + (1 - c) * first + c * second) % 4
        h = slice(None) if half is None else half
        return self.fulls[w].at[y, h, z, c]

    def towards(self, axis, step):
        here = self.here
        along_y = here.c if axis == 0 else 1 - here.c
        return here.at(y=(here.y + along_y * step) % 4, z=(here.z + (1 - along_y) * step) % 4)

    def push(self, w, k, ref, device, src=None):
        copy = remote(
            ref if src is None else src, ref, self.send.at[w, k], self.recv.at[w, k], device
        )
        copy.start()
        self.copies.append(copy)
        self.legs[w][k] = copy

    def share(self, w, k, ref):
        copy = remote(ref, ref, self.bsend.at[w, k], self.brecv.at[w, k], self.here.sibling())
        copy.start()
        self.copies.append(copy)

    def around(self, w, ks, half, src=None):
        ref = self.piece(w, 0, 0, self.here.c, half)
        for k, axis, step in zip(ks, (0, 0, 1, 1), (1, 3, 1, 3)):
            self.push(w, k, ref, self.towards(axis, step), src)

    def launch(self, w):
        self.around(w, (1, 2, 5, 6), self.here.xh, self.parts[w].at[self.here.c])

    def crossed(self, w):
        here = self.here
        self.legs[w][0].wait_recv()
        self.around(w, (21, 22, 23, 24), 1 - here.xh)
        self.share(w, 0, self.piece(w, 0, 0, here.c, 1 - here.xh))
        self.locals[w].wait()

    def second(self, w, o):
        ref = self.piece(w, o, 0, self.here.c)
        self.push(w, 5 + 4 * o, ref, self.towards(1, 1))
        self.push(w, 6 + 4 * o, ref, self.towards(1, 3))

    def first_near(self, w):
        c = self.here.c
        self.legs[w][1].wait_recv()
        self.legs[w][21].wait_recv()
        self.push(w, 3, self.piece(w, 3, 0, c, 0), self.towards(0, 1))
        self.second(w, 3)
        self.share(w, 1, self.piece(w, 3, 0, c))
        self.legs[w][2].wait_recv()
        self.legs[w][22].wait_recv()
        self.push(w, 4, self.piece(w, 1, 0, c, 1), self.towards(0, 3))
        self.second(w, 1)
        self.share(w, 2, self.piece(w, 1, 0, c))

    def first_far(self, w):
        self.legs[w][3].wait_recv()
        self.legs[w][4].wait_recv()
        self.second(w, 2)
        self.share(w, 3, self.piece(w, 2, 0, self.here.c))

    def second_near(self, w, o):
        c = self.here.c
        self.legs[w][5 + 4 * o].wait_recv()
        if o == 0:
            self.legs[w][23].wait_recv()
        self.push(w, 7 + 4 * o, self.piece(w, o, 3, c, 0), self.towards(1, 1))
        self.share(w, 4 + 3 * o, self.piece(w, o, 3, c))
        self.legs[w][6 + 4 * o].wait_recv()
        if o == 0:
            self.legs[w][24].wait_recv()
        self.push(w, 8 + 4 * o, self.piece(w, o, 1, c, 1), self.towards(1, 3))
        self.share(w, 5 + 3 * o, self.piece(w, o, 1, c))

    def second_far(self, w, o):
        self.legs[w][7 + 4 * o].wait_recv()
        self.legs[w][8 + 4 * o].wait_recv()
        self.share(w, 6 + 3 * o, self.piece(w, o, 2, self.here.c))

    def shared_near(self, w):
        other = 1 - self.here.c
        drain(self.piece(w, 0, 0, other, 1 - self.here.xh), self.brecv.at[w, 0])
        for k, o in ((1, 3), (2, 1), (3, 2)):
            drain(self.piece(w, o, 0, other), self.brecv.at[w, k])
        for o in range(4):
            drain(self.piece(w, o, 3, other), self.brecv.at[w, 4 + 3 * o])
            drain(self.piece(w, o, 1, other), self.brecv.at[w, 5 + 3 * o])

    def shared_far(self, w):
        for o in range(4):
            drain(self.piece(w, o, 2, 1 - self.here.c), self.brecv.at[w, 6 + 3 * o])

    def finish(self):
        for copy in self.copies:
            copy.wait_send()


def add_into(target, *others):
    lead = target.shape[:-2]

    def body(i, carry):
        index = []
        rest = i
        for size in reversed(lead):
            index.append(rest % size)
            rest = rest // size
        index = tuple(reversed(index))
        total = target[index].astype(F32)
        for other in others:
            total += other[index].astype(F32)
        target[index] = total.astype(BF)
        return carry

    lax.fori_loop(0, math.prod(lead), body, 0, unroll=min(8, math.prod(lead)))


PARTS = (
    ("x", 48, 128), ("y", 48, 128), ("z", 48, 128),
    ("y", 16, 384), ("z", 16, 384), ("x", 16, 256),
    ("y", 16, 256), ("z", 16, 384), ("x", 16, 384),
)
PLANES = {"x": ("y", "z"), "y": ("z", "x"), "z": ("x", "y")}


class PartSum:
    def __init__(self, here, p, acc, bufs, send, recv):
        self.here, self.p, self.acc = here, p, acc
        self.low, self.high, self.up_buf, self.down_buf, self.turn_buf, self.end_buf = bufs
        self.send, self.recv = send, recv
        self.copies = []
        self.axis = PARTS[p][0]
        self.me = getattr(here, self.axis)

    def index(self, at):
        full = slice(None)
        if "x" in at:
            return (at.get("y", full), at["x"] // 2, at.get("z", full), at["x"] % 2)
        return (at.get("y", full), full, at.get("z", full), full)

    def chunk(self, pos, half=None):
        index = list(self.index({self.axis: pos}))
        if half is not None:
            if self.axis == "y":
                index[1] = half
            else:
                index[0] = pl.ds(2 * half, 2)
        return self.acc.at[tuple(index)]

    def to(self, step):
        return self.here.at(**{self.axis: (self.me + step) % 4})

    def push(self, k, src, dst, device):
        copy = remote(src, dst, self.send.at[self.p, k], self.recv.at[self.p, k], device)
        copy.start()
        self.copies.append(copy)
        return copy

    def begin(self):
        far = (self.me + 2) % 4
        self.legs = (
            self.push(0, self.chunk(far, 0), self.low, self.to(1)),
            self.push(1, self.chunk(far, 1), self.high, self.to(3)),
        )

    def relay(self):
        up, down = (self.me + 1) % 4, (self.me + 3) % 4
        self.legs[0].wait_recv()
        add_into(self.chunk(up, 0), self.low)
        one = self.push(2, self.chunk(up), self.up_buf, self.to(1))
        self.legs[1].wait_recv()
        add_into(self.chunk(down, 1), self.high)
        two = self.push(3, self.chunk(down), self.down_buf, self.to(3))
        self.legs = (one, two)

    def across(self, k, name, buf, at):
        me = getattr(self.here, name)
        for step in (1, 3, 2):
            pos = (me + step) % 4
            remote(
                self.acc.at[self.index({**at, name: pos})], buf.at[me],
                self.send.at[self.p, k], self.recv.at[self.p, k], self.here.at(**{name: pos}),
            ).start()

    def cross(self):
        self.legs[0].wait_recv()
        self.legs[1].wait_recv()
        add_into(self.chunk(self.me), self.up_buf, self.down_buf)
        self.across(4, PLANES[self.axis][0], self.turn_buf, {self.axis: self.me})

    def turn(self):
        a, b = PLANES[self.axis]
        me = getattr(self.here, a)
        at = {self.axis: self.me, a: me}
        drain(self.turn_buf.at[pl.ds(0, 3)], self.recv.at[self.p, 4])
        add_into(
            self.acc.at[self.index(at)], *[self.turn_buf.at[(me + k) % 4] for k in (1, 2, 3)]
        )
        self.across(5, b, self.end_buf, at)

    def end(self):
        a, b = PLANES[self.axis]
        me = getattr(self.here, b)
        at = {self.axis: self.me, a: getattr(self.here, a), b: me}
        drain(self.end_buf.at[pl.ds(0, 3)], self.recv.at[self.p, 5])
        total = self.acc[self.index(at)].astype(F32)
        for k in (1, 2, 3):
            total += self.end_buf[(me + k) % 4].astype(F32)
        return total

    def finish(self):
        for copy in self.copies:
            copy.wait_send()
        drain(self.turn_buf.at[pl.ds(0, 3)], self.send.at[self.p, 4])
        drain(self.end_buf.at[pl.ds(0, 3)], self.send.at[self.p, 5])


def part_shape(p):
    return (4, 2, 4, 2) + PARTS[p][1:]


def part_buffers(p):
    axis, tail = PARTS[p][0], PARTS[p][1:]
    whole = {"x": (4, 4), "y": (2, 4, 2), "z": (4, 2, 2)}[axis]
    half = whole[1:] if axis == "y" else (2,) + whole[1:]
    last = (2, 2) if PLANES[axis][1] == "x" else (4,)
    shapes = [half + tail] * 2 + [whole + tail] * 2 + [(4,) + last + tail, (4,) + tail]
    return [pltpu.VMEM(s, BF) for s in shapes]


DMA = pltpu.SemaphoreType.DMA
SCRATCH = dict(
    scale_first=((384, 1), F32), scale_second=((384, 1), F32),
    spectra=((384, 768), BF), cot=((384, 768), BF), grad_input=((384, 768), BF),
    win=((4, 2, 4, 2, 32, 1024), BF), wout=((4, 2, 4, 2, 32, 1024), BF),
    chin=((1536, 768), BF), chout=((1536, 768), BF),
    normed=((12, 2, 16, 768), BF), tm=((12, 2, 16, 768), BF), ng=((12, 2, 16, 768), BF),
    mixg=((12, 2, 16, 768), BF), ns=((384, 768), BF), mg=((384, 768), F32),
    cact=((384, 1536), BF), cgrad=((384, 1536), BF),
    cact_s=((384, 1536), BF), cgrad_s=((384, 1536), BF),
    ns_s=((384, 384), BF), cot_s=((384, 384), BF),
    cols_t=((256, 2048), BF), second=((192, 768), F32), down=((384, 1536), F32),
    cols=((64, 2, 16, 256), BF), cols2=((64, 2, 16, 256), BF),
    cols_s=((64, 16, 256), BF), cols2_s=((64, 16, 256), BF),
    hidden=((256, 1024), F32), slope=((256, 1024), F32),
    act=((256, 1024), BF), act_s=((256, 1024), BF),
    hg=((256, 1024), BF), hg_s=((256, 1024), BF),
    mixb=((64, 2, 16, 256), BF), ncg=((64, 2, 16, 256), BF),
    fin=((4, 48, 384), F32), sum0=((16, 1024), F32), sum1=((16, 1024), F32),
    sum2=((12, 768), F32), sum3=((12, 768), F32),
)
SEMS = dict(
    load=(5,), a1_send=(), a1_recv=(), a1_esend=(4,), a1_erecv=(),
    a3_send=(), a3_recv=(), a3_esend=(4,), a3_erecv=(),
    a2_send=(), a2_recv=(2,), a2_esend=(),
    a4_send=(), a4_recv=(2,), a4_esend=(),
    w_own=(2,), w_send=(2, 25), w_recv=(2, 25), w_bsend=(2, 16), w_brecv=(2, 16),
    r_send=(9, 6), r_recv=(9, 6),
    s_send=(11,), s_recv=(11,), f_send=(3,), f_recv=(3,),
)


def block_kernel(
    spectra_in, cot_in, w_in, w_out, ch_in, ch_out, grad_out, o0, o1, o2, o3, *scratch
):
    v = types.SimpleNamespace(**dict(zip(list(SCRATCH) + list(SEMS), scratch)))
    spectra, cot, grad_input = v.spectra, v.cot, v.grad_input
    bufs = scratch[len(SCRATCH) + len(SEMS):]
    sums = scratch[len(SCRATCH) + len(SEMS) + 6 * len(PARTS):]
    here = Here()
    c = here.c
    sib = here.sibling()
    cross = here.at(x=here.xh * 2 + 1 - here.xl, c=1 - c)
    partners = [sib, cross]
    for k in (1, 3):
        x = (here.x + k) % 4
        partners += [here.at(x=x, z=(here.z + n) % 4) for n in range(4)]
        partners += [here.at(x=x, y=(here.y + n) % 4) for n in range(1, 4)]
    loads = [
        pltpu.make_async_copy(src, dst, v.load.at[k])
        for k, (src, dst) in enumerate((
            (spectra_in, spectra), (cot_in, cot), (ch_in, v.chin), (ch_out, v.chout),
        ))
    ]
    for copy in loads:
        copy.start()
    count = greet_seq(here) + greet(partners)
    loads.pop(0).wait()

    def norm_first(i, carry):
        unit, scale = normalize(spectra[rows(i, 32), :].astype(F32))
        v.normed[i] = unit.astype(BF).reshape(2, 16, 768)
        v.scale_first[rows(i, 32), :] = scale
        return carry

    lax.fori_loop(0, 12, norm_first, 0, unroll=6)
    pl.semaphore_wait(pltpu.get_barrier_semaphore(), count)

    shared = []

    def share(src, dst):
        k = len(shared)
        copy = remote(src, dst, v.s_send.at[k], v.s_recv.at[k], sib)
        copy.start()
        shared.append(copy)
        return copy

    gather = Gather(
        here, (w_in, w_out), (v.win, v.wout),
        (v.w_own, v.w_send, v.w_recv, v.w_bsend, v.w_brecv),
    )
    first = ToChannels(
        here, v.normed, v.cols, (v.a1_send, v.a1_recv, v.a1_esend, v.a1_erecv)
    )
    both = range(2)
    for w in both:
        gather.launch(w)
    first.start(0)
    first.start(1)
    for w in both:
        gather.crossed(w)
    for copy in loads:
        copy.wait()
    share(cot.at[:, lanes(384 * (1 - c), 384)], v.cot_s)

    def channel_down(i, carry):
        v.down[:, lanes(256 * i, 256)] = dot(cot[...], v.chout[rows(i, 256), :], NT)
        return carry

    for w in both:
        gather.first_near(w)
    lax.fori_loop(0, 3, channel_down, 0)
    for w in both:
        gather.second_near(w, 0)
    for w in both:
        gather.first_far(w)
    lax.fori_loop(3, 6, channel_down, 0)
    for o in (3, 1):
        for w in both:
            gather.second_near(w, o)
    first.arrive()
    share(v.cols.at[:, 1 - c], v.cols_s)
    for w in both:
        gather.second_near(w, 2)

    def turn_cols(y, carry):
        v.cols_t[:, lanes(512 * y, 512)] = v.cols[pl.ds(16 * y, 16)].reshape(512, 256).T
        return carry

    lax.fori_loop(0, 4, turn_cols, 0, unroll=2)
    for o in (0, 3, 1, 2):
        gather.second_far(0, o)
    gather.shared_near(0)
    gather.shared_far(0)

    def project(source, weight):
        def step(y, start):
            left = source[pl.ds(16 * y, 16)].reshape(512, 256)
            part = dot(left, weight[y].reshape(512, 1024), TN)
            if start:
                v.hidden[...] = part
            else:
                v.hidden[...] += part

        step(0, True)
        for y in range(1, 4):
            step(y, False)

    def hidden_of(i, carry):
        part = lanes(256 * i, 256)
        weight = v.win[:, :, :, :, :, part].reshape(2048, 256)
        v.hidden[:, part] = dot(v.cols_t[...], weight, NN)
        return carry

    lax.fori_loop(0, 4, hidden_of, 0, unroll=4)

    def token_gelu(i, carry):
        at = rows(i, 16)
        value, slope = gelu_pair(v.hidden[at, :])
        v.act[at, :] = value.astype(BF)
        v.slope[at, :] = slope
        return carry

    lax.fori_loop(0, 16, token_gelu, 0, unroll=8)
    share(v.act, v.act_s)

    def spread(weight, source, target, transfer, spots):
        left = jnp.concatenate([weight[y, :, z].reshape(128, 1024) for y, z, _ in spots], axis=0)
        value = dot(left, source[...], NT).astype(BF).reshape(len(spots), 2, 2, 2, 16, 256)
        for k, (y, z, other) in enumerate(spots):
            for xh in range(2):
                dest = 8 * y + 4 * xh + z
                target[pl.ds(2 * dest, 2)] = value[k, xh]
                transfer.start(dest, other)

    def off(name, step):
        return (getattr(here, name) + step) % 4

    second = ToPatches(
        here, v.mixb, v.tm, (v.a2_send, v.a2_recv, v.a2_esend)
    )
    gather.shared_near(1)

    def near(i, carry):
        z = off("z", i + i // 2)
        spread(
            v.wout, v.act, v.mixb, second, [(off("y", step), z, step > 0) for step in (1, 3, 0)]
        )
        return carry

    lax.fori_loop(0, 3, near, 0)
    for o in (0, 3, 1, 2):
        gather.second_far(1, o)
    gather.shared_far(1)
    spread(
        v.wout, v.act, v.mixb, second,
        [(off("y", 2), off("z", step), True) for step in (1, 3, 0)],
    )
    spread(
        v.wout, v.act, v.mixb, second,
        [(off("y", step), off("z", 2), True) for step in (2, 1, 3, 0)],
    )
    gather.finish()
    first.finish()

    third = ToChannels(
        here, v.mixg, v.cols2, (v.a3_send, v.a3_recv, v.a3_esend, v.a3_erecv)
    )

    def middle_of(at):
        source = spectra[rows(at, 32), :].astype(F32)
        mix = v.tm[at].reshape(32, 768).astype(F32)
        return (source + mix).astype(BF).astype(F32)

    for half in range(2):
        second.arrive(half)
        span = pl.ds(192 * half, 192)

        def norm_second(i, carry):
            at = half * 6 + i
            unit, scale = normalize(middle_of(at))
            v.ns[rows(at, 32), :] = unit.astype(BF)
            v.scale_second[rows(at, 32), :] = scale
            return carry

        lax.fori_loop(0, 6, norm_second, 0, unroll=6)

        def hidden_units(i, carry):
            part = lanes(256 * i, 256)
            own = rows(i, 256)
            value, slope = gelu_pair(dot(v.ns[span, :], v.chin[own, :], NT))
            v.cact[span, part] = value.astype(BF)
            v.cgrad[span, part] = (v.down[span, part] * slope).astype(BF)
            return carry

        lax.fori_loop(0, 6, hidden_units, 0, unroll=3)
        for src, dst in ((v.cgrad, v.cgrad_s), (v.cact, v.cact_s)):
            share(src.at[span], dst.at[span])
        share(v.ns.at[span, lanes(384 * (1 - c), 384)], v.ns_s.at[span])
        v.second[...] = dot(v.cgrad[span, :], v.chin[...], NN)

        def back_second(i, carry):
            at = half * 6 + i
            unit = v.ns[rows(at, 32), :].astype(F32)
            scale = v.scale_second[rows(at, 32), :]
            upstream = v.second[rows(i, 32), :]
            value = cot[rows(at, 32), :].astype(F32) + norm_back(unit, scale, upstream)
            v.mg[rows(at, 32), :] = value
            v.mixg[at] = value.astype(BF).reshape(2, 16, 768)
            return carry

        lax.fori_loop(0, 6, back_second, 0, unroll=6)
        third.start(half)

    for copy in shared:
        copy.wait_recv()
    half_lanes = lanes(384 * c, 384)
    for g, (act, tok, act_s, tok_s) in enumerate((
        (v.cgrad, v.ns, v.cgrad_s, v.ns_s), (v.cact, cot, v.cact_s, v.cot_s),
    )):
        def channel_sum(y, carry):
            part = lanes(384 * y, 384)
            total = dot(act[:, part], tok[:, half_lanes], TN)
            total += dot(act_s[:, part], tok_s[...], TN)
            total = total.astype(BF).reshape(2, 4, 48, 384)
            for p in range(3):
                sums[p][y, :, :, g] = total[..., 128 * p:128 * p + 128]
            return carry

        lax.fori_loop(0, 4, channel_sum, 0, unroll=4)

    parts = [
        PartSum(here, p, sums[p], bufs[6 * p:6 * p + 6], v.r_send, v.r_recv)
        for p in range(len(PARTS))
    ]
    channel_parts, early, late = parts[:3], parts[3:6], parts[6:]
    for part in channel_parts:
        part.begin()
    for part in channel_parts:
        part.relay()

    second.finish()
    third.arrive()
    share_cols2 = share(v.cols2.at[:, 1 - c], v.cols2_s)
    project(v.cols2, v.wout)

    def token_grad(i, carry):
        at = rows(i, 16)
        v.hg[at, :] = (v.hidden[at, :] * v.slope[at, :]).astype(BF)
        return carry

    lax.fori_loop(0, 16, token_grad, 0, unroll=8)
    share_hg = share(v.hg, v.hg_s)

    def token_sum(left, left_s, right, right_s, targets):
        def step(y, carry):
            own = left[pl.ds(16 * y, 16), c].reshape(256, 256)
            other = left_s[pl.ds(16 * y, 16)].reshape(256, 256)
            total = dot(own, right[...], NN) + dot(other, right_s[...], NN)
            total = total.astype(BF).reshape(2, 4, 2, 16, 1024)
            place = 0
            for p in targets:
                width = PARTS[p][2]
                sums[p][y] = total[..., place:place + width]
                place += width
            return carry

        lax.fori_loop(0, 4, step, 0, unroll=4)

    share_cols2.wait_recv()
    token_sum(
        v.cols2, v.cols2_s, v.act, v.act_s, (3, 4, 5),
    )
    for part in early:
        part.begin()
    for part in channel_parts:
        part.cross()
    share_hg.wait_recv()
    token_sum(
        v.cols, v.cols_s, v.hg, v.hg_s, (6, 7, 8),
    )
    for part in late:
        part.begin()
    for part in early:
        part.relay()
    for part in channel_parts:
        part.turn()
    fourth = ToPatches(
        here, v.ncg, v.ng, (v.a4_send, v.a4_recv, v.a4_esend)
    )

    def back(i, carry):
        z = off("z", 3 - i)
        spread(
            v.win, v.hg, v.ncg, fourth, [(off("y", step), z, step > 0) for step in (2, 1, 3, 0)]
        )
        return carry

    lax.fori_loop(0, 4, back, 0, unroll=2)
    for part in late:
        part.relay()
    for part in early:
        part.cross()

    def input_grad(half):
        fourth.arrive(half)

        def step(i, carry):
            at = half * 6 + i
            unit = v.normed[at].reshape(32, 768).astype(F32)
            scale = v.scale_first[rows(at, 32), :]
            upstream = v.ng[at].reshape(32, 768).astype(F32)
            value = v.mg[rows(at, 32), :] + norm_back(unit, scale, upstream)
            grad_input[rows(at, 32), :] = value.astype(BF)
            return carry

        lax.fori_loop(0, 6, step, 0, unroll=6)

    for p, part in enumerate(channel_parts):
        v.fin[here.d, :, 128 * p:128 * p + 128] = part.end()
    input_grad(0)
    swaps = []
    for k, device in enumerate((sib, here.at(x=here.xh * 2 + 1 - here.xl), cross)):
        copy = remote(
            v.fin.at[here.d], v.fin.at[here.d], v.f_send.at[k], v.f_recv.at[k], device
        )
        copy.start()
        swaps.append(copy)
    for part in early:
        part.turn()
    for part in late:
        part.cross()
    input_grad(1)
    stores = [pltpu.make_async_copy(grad_input, grad_out, v.load.at[4])]
    stores[0].start()
    for part in late:
        part.turn()

    def gather_up(out, group):
        place = 0
        for part in group:
            width = PARTS[part.p][2]
            out[:, place:place + width] = part.end()
            place += width

    def keep(k, src, dst):
        copy = pltpu.make_async_copy(src, dst, v.load.at[k])
        copy.start()
        return copy

    gather_up(v.sum1, early)
    stores.append(keep(0, v.sum1, o1))
    for copy in swaps:
        copy.wait()
    for d in range(4):
        @pl.when(here.d == d)
        def _():
            for total, g in ((v.sum2, 0), (v.sum3, 2)):
                for k in range(2):
                    total[:, 384 * k:384 * k + 384] = v.fin[g + k, 12 * d:12 * d + 12]
    stores.append(keep(1, v.sum2, o2))
    stores.append(keep(2, v.sum3, o3))
    for part in channel_parts + early:
        part.finish()
    for copy in shared:
        copy.wait_send()
    third.finish()
    fourth.finish()
    gather_up(v.sum0, late)
    stores.append(keep(3, v.sum0, o0))
    for part in late:
        part.finish()
    for copy in stores:
        copy.wait()


def hand_over(*refs):
    for src, dst in zip(refs[:5], refs[5:]):
        dst[...] = src[...]


def local(spectra_in, cotangent, tok_in_w, tok_out_w, ch_in_w, ch_out_w):
    vmem = pl.BlockSpec(memory_space=pltpu.VMEM)
    scratch = [pltpu.VMEM(shape, kind) for shape, kind in SCRATCH.values()]
    scratch += [DMA(shape) if shape else DMA for shape in SEMS.values()]
    for p in range(len(PARTS)):
        scratch += part_buffers(p)
    scratch += [pltpu.VMEM(part_shape(p), BF) for p in range(len(PARTS))]
    shapes = (
        jax.ShapeDtypeStruct((384, 768), BF),
        jax.ShapeDtypeStruct((16, 1024), F32),
        jax.ShapeDtypeStruct((16, 1024), F32),
        jax.ShapeDtypeStruct((12, 768), F32),
        jax.ShapeDtypeStruct((12, 768), F32),
    )
    outs = pl.pallas_call(
        block_kernel,
        out_shape=shapes,
        in_specs=[ANY] * 6, out_specs=(ANY,) * 5,
        scratch_shapes=scratch,
        compiler_params=pltpu.CompilerParams(
            collective_id=0, has_side_effects=True, vmem_limit_bytes=60 * 1024 * 1024
        ),
        name="mixer_block_backward",
    )(
        spectra_in.reshape(384, 768), cotangent.reshape(384, 768),
        tok_in_w.reshape(2, 32, 1024), tok_out_w.reshape(2, 32, 1024), ch_in_w, ch_out_w,
    )
    grad_input, *weights = pl.pallas_call(
        hand_over, out_shape=shapes, in_specs=[vmem] * 5, out_specs=(vmem,) * 5, name="hand_over",
    )(*outs)
    return (grad_input.reshape(6, 64, 768), *weights)


def solution(mesh):
    in_specs = (
        P("dp", "seq", None),
        P("dp", "seq", None),
        P("seq", None),
        P("seq", None),
        P(),
        P(),
    )
    out_specs = (
        P("dp", "seq", None),
        P(("seq", "dp"), None),
        P(("seq", "dp"), None),
        P(("seq", "dp"), None),
        P(("seq", "dp"), None),
    )
    return jax.shard_map(local, mesh=mesh, in_specs=in_specs, out_specs=out_specs, check_vma=False)
```

```python
import math
import types

import jax
import jax.numpy as jnp
from jax import lax
from jax.experimental import pallas as pl
from jax.experimental.pallas import tpu as pltpu
from jax.sharding import PartitionSpec as P

BF = jnp.bfloat16
F32 = jnp.float32
MESH = pl.DeviceIdType.MESH
ANY = pl.BlockSpec(memory_space=pl.ANY)
LANES = 128


def normalize(values):
    center = values - jnp.mean(values, axis=-1, keepdims=True)
    inv_scale = lax.rsqrt(jnp.mean(center * center, axis=-1, keepdims=True) + 1e-05)
    return (center * inv_scale, inv_scale)


def norm_back(unit, inv_scale, upstream):
    first = jnp.mean(upstream, axis=-1, keepdims=True)
    second = jnp.mean(upstream * unit, axis=-1, keepdims=True)
    return inv_scale * (upstream - first - unit * second)


def gelu_pair(values):
    factor = math.sqrt(2.0 / math.pi)
    square = values * values
    half = 0.5 + 0.5 * jnp.tanh(values * (factor + (factor * 0.044715) * square))
    result = values * half
    slope = half + result * (1.0 - half) * (2.0 * factor + (6.0 * factor * 0.044715) * square)
    return (result, slope)


class Here:
    def __init__(self):
        self.q = lax.axis_index("seq")
        self.d = lax.axis_index("dp")
        self.y = self.q // 8
        self.xh = (self.q // 4) % 2
        self.z = self.q % 4
        self.xl = self.d // 2
        self.c = self.d % 2
        self.x = self.xh * 2 + self.xl

    def at(self, x=None, y=None, z=None, c=None):
        x = self.x if x is None else x
        y = self.y if y is None else y
        z = self.z if z is None else z
        c = self.c if c is None else c
        return {"seq": (y * 2 + x // 2) * 4 + z, "dp": (x % 2) * 2 + c}

    def peer(self, q):
        return {"seq": q, "dp": self.d}

    def sibling(self):
        return {"seq": self.q, "dp": self.d + 1 - 2 * self.c}

    def extra_of(self, e):
        return 8 * e + ((e + self.d // 2) % 2) * 4 + (e + self.d) % 4

    def has_extra(self):
        return self.q == self.extra_of(self.y)


def remote(src, dst, send, recv, device):
    return pltpu.make_async_remote_copy(
        src_ref=src, dst_ref=dst, send_sem=send, recv_sem=recv,
        device_id=device, device_id_type=MESH,
    )


def drain(ref, sem):
    pltpu.make_async_copy(ref, ref, sem).wait()


def greet(devices):
    barrier = pltpu.get_barrier_semaphore()
    for device in devices:
        pl.semaphore_signal(barrier, inc=1, device_id=device, device_id_type=MESH)
    return len(devices)


def greet_seq(here):
    barrier = pltpu.get_barrier_semaphore()

    def body(i, carry):
        pl.semaphore_signal(
            barrier, inc=1, device_id=here.peer((here.q + i) % 32), device_id_type=MESH
        )
        return carry

    lax.fori_loop(1, 32, body, 0)
    return 31


def rows(start, size):
    return pl.ds(pl.multiple_of(start * size, size), size)


TN = (((0,), (0,)), ((), ()))
NT = (((1,), (1,)), ((), ()))
NN = (((1,), (0,)), ((), ()))


def dot(a, b, dims):
    return lax.dot_general(a, b, dims, preferred_element_type=F32)


def lanes(start, size):
    return pl.ds(pl.multiple_of(start, LANES), size)


def block_of(ref, s, b):
    return ref.at[pl.ds(2 * s, 2), :, :, lanes(b * LANES, LANES)]


def column(ref, q, slot):
    return ref.at[pl.ds(2 * q, 2), :, :, pl.ds(slot * LANES, LANES)]


class ToChannels:
    def __init__(self, here, src, cols, sems):
        self.here, self.src, self.cols = here, src, cols
        self.send, self.recv, self.esend, self.erecv = sems

        @pl.when(jnp.logical_not(here.has_extra()))
        def _():
            cols[:, :, :, LANES:] = jnp.zeros((64, 2, 16, LANES), BF)

    def start(self, half):
        here, src, cols = self.here, self.src, self.cols
        first, count = ((0, 18), (18, 14))[half]

        def body(i, carry):
            dest = first + (i + here.q) % count
            block, place = block_of(src, dest // 6, dest % 6), column(cols, here.q, 0)

            @pl.when(dest != here.q)
            def _():
                remote(block, place, self.send, self.recv, here.peer(dest)).start()

            @pl.when(dest == here.q)
            def _():
                pltpu.make_async_copy(block, place, self.recv).start()

            return carry

        lax.fori_loop(0, count, body, 0)
        if half == 1:
            for e in range(4):
                dest = here.extra_of(e)
                block, place = block_of(src, 5, 2 + e), column(cols, here.q, 1)

                @pl.when(dest != here.q)
                def _():
                    remote(block, place, self.esend.at[e], self.erecv, here.peer(dest)).start()

                @pl.when(dest == here.q)
                def _():
                    pltpu.make_async_copy(block, place, self.erecv).start()

    def arrive(self):
        drain(self.cols.at[:, :, :, pl.ds(0, LANES)], self.recv)

        @pl.when(self.here.has_extra())
        def _():
            drain(self.cols.at[:, :, :, pl.ds(LANES, LANES)], self.erecv)

    def finish(self):
        drain(self.cols.at[pl.ds(0, 62), :, :, pl.ds(0, LANES)], self.send)
        for e in range(4):
            @pl.when(self.here.extra_of(e) != self.here.q)
            def _():
                drain(self.cols.at[pl.ds(0, 2), :, :, pl.ds(0, LANES)], self.esend.at[e])


class ToPatches:
    def __init__(self, here, cols, out, sems):
        self.here, self.cols, self.out = here, cols, out
        self.send, self.recv, self.esend = sems

    def start(self, dest, other):
        here, cols, out = self.here, self.cols, self.out
        place = block_of(out, here.q // 6, here.q % 6)
        extra = block_of(out, 5, 2 + here.y)
        sem = self.recv.at[here.q // 18]

        def away():
            remote(column(cols, dest, 0), place, self.send, sem, here.peer(dest)).start()

            @pl.when(here.has_extra())
            def _():
                remote(
                    column(cols, dest, 1), extra, self.esend, self.recv.at[1], here.peer(dest)
                ).start()

        if other:
            away()
            return
        pl.when(dest != here.q)(away)

        @pl.when(dest == here.q)
        def _():
            pltpu.make_async_copy(column(cols, dest, 0), place, sem).start()

            @pl.when(here.has_extra())
            def _():
                pltpu.make_async_copy(column(cols, dest, 1), extra, self.recv.at[1]).start()

    def arrive(self, half):
        drain(self.out.at[pl.ds(6 * half, 6)], self.recv.at[half])

    def finish(self):
        many = self.cols.at[pl.ds(0, 62), :, :, pl.ds(0, LANES)]
        drain(many, self.send)

        @pl.when(self.here.has_extra())
        def _():
            drain(many, self.esend)


class Gather:
    def __init__(self, here, parts, fulls, sems):
        self.here, self.fulls, self.parts = here, fulls, parts
        self.own, self.send, self.recv, self.bsend, self.brecv = sems
        self.copies = []
        self.legs = [{}, {}]
        c, y, xh, z = here.c, here.y, here.xh, here.z
        self.locals = []
        for w in range(2):
            copy = pltpu.make_async_copy(parts[w], fulls[w].at[y, xh, z], self.own.at[w])
            copy.start()
            self.locals.append(copy)
            self.push(w, 0, fulls[w].at[y, xh, z, c], here.at(x=(here.x + 2) % 4), parts[w].at[c])

    def piece(self, w, first, second, c, half=None):
        here = self.here
        y = (here.y + c * first + (1 - c) * second) % 4
        z = (here.z + (1 - c) * first + c * second) % 4
        h = slice(None) if half is None else half
        return self.fulls[w].at[y, h, z, c]

    def towards(self, axis, step):
        here = self.here
        along_y = here.c if axis == 0 else 1 - here.c
        return here.at(y=(here.y + along_y * step) % 4, z=(here.z + (1 - along_y) * step) % 4)

    def push(self, w, k, ref, device, src=None):
        copy = remote(
            ref if src is None else src, ref, self.send.at[w, k], self.recv.at[w, k], device
        )
        copy.start()
        self.copies.append(copy)
        self.legs[w][k] = copy

    def share(self, w, k, ref):
        copy = remote(ref, ref, self.bsend.at[w, k], self.brecv.at[w, k], self.here.sibling())
        copy.start()
        self.copies.append(copy)

    def around(self, w, ks, half, src=None):
        ref = self.piece(w, 0, 0, self.here.c, half)
        for k, axis, step in zip(ks, (0, 0, 1, 1), (1, 3, 1, 3)):
            self.push(w, k, ref, self.towards(axis, step), src)

    def launch(self, w):
        self.around(w, (1, 2, 5, 6), self.here.xh, self.parts[w].at[self.here.c])

    def crossed(self, w):
        here = self.here
        self.legs[w][0].wait_recv()
        self.around(w, (21, 22, 23, 24), 1 - here.xh)
        self.share(w, 0, self.piece(w, 0, 0, here.c, 1 - here.xh))
        self.locals[w].wait()

    def second(self, w, o):
        ref = self.piece(w, o, 0, self.here.c)
        self.push(w, 5 + 4 * o, ref, self.towards(1, 1))
        self.push(w, 6 + 4 * o, ref, self.towards(1, 3))

    def first_near(self, w):
        c = self.here.c
        self.legs[w][1].wait_recv()
        self.legs[w][21].wait_recv()
        self.push(w, 3, self.piece(w, 3, 0, c, 0), self.towards(0, 1))
        self.second(w, 3)
        self.share(w, 1, self.piece(w, 3, 0, c))
        self.legs[w][2].wait_recv()
        self.legs[w][22].wait_recv()
        self.push(w, 4, self.piece(w, 1, 0, c, 1), self.towards(0, 3))
        self.second(w, 1)
        self.share(w, 2, self.piece(w, 1, 0, c))

    def first_far(self, w):
        self.legs[w][3].wait_recv()
        self.legs[w][4].wait_recv()
        self.second(w, 2)
        self.share(w, 3, self.piece(w, 2, 0, self.here.c))

    def second_near(self, w, o):
        c = self.here.c
        self.legs[w][5 + 4 * o].wait_recv()
        if o == 0:
            self.legs[w][23].wait_recv()
        self.push(w, 7 + 4 * o, self.piece(w, o, 3, c, 0), self.towards(1, 1))
        self.share(w, 4 + 3 * o, self.piece(w, o, 3, c))
        self.legs[w][6 + 4 * o].wait_recv()
        if o == 0:
            self.legs[w][24].wait_recv()
        self.push(w, 8 + 4 * o, self.piece(w, o, 1, c, 1), self.towards(1, 3))
        self.share(w, 5 + 3 * o, self.piece(w, o, 1, c))

    def second_far(self, w, o):
        self.legs[w][7 + 4 * o].wait_recv()
        self.legs[w][8 + 4 * o].wait_recv()
        self.share(w, 6 + 3 * o, self.piece(w, o, 2, self.here.c))

    def shared_near(self, w):
        other = 1 - self.here.c
        drain(self.piece(w, 0, 0, other, 1 - self.here.xh), self.brecv.at[w, 0])
        for k, o in ((1, 3), (2, 1), (3, 2)):
            drain(self.piece(w, o, 0, other), self.brecv.at[w, k])
        for o in range(4):
            drain(self.piece(w, o, 3, other), self.brecv.at[w, 4 + 3 * o])
            drain(self.piece(w, o, 1, other), self.brecv.at[w, 5 + 3 * o])

    def shared_far(self, w):
        for o in range(4):
            drain(self.piece(w, o, 2, 1 - self.here.c), self.brecv.at[w, 6 + 3 * o])

    def finish(self):
        for copy in self.copies:
            copy.wait_send()


def add_into(target, *others):
    lead = target.shape[:-2]

    def body(i, carry):
        index = []
        rest = i
        for size in reversed(lead):
            index.append(rest % size)
            rest = rest // size
        index = tuple(reversed(index))
        total = target[index].astype(F32)
        for other in others:
            total += other[index].astype(F32)
        target[index] = total.astype(BF)
        return carry

    lax.fori_loop(0, math.prod(lead), body, 0, unroll=min(8, math.prod(lead)))


PARTS = (
    ("x", 48, 128), ("y", 48, 128), ("z", 48, 128),
    ("y", 16, 384), ("z", 16, 384), ("x", 16, 256),
    ("y", 16, 256), ("z", 16, 384), ("x", 16, 384),
)
PLANES = {"x": ("y", "z"), "y": ("z", "x"), "z": ("x", "y")}


class PartSum:
    def __init__(self, here, p, acc, bufs, send, recv):
        self.here, self.p, self.acc = here, p, acc
        self.low, self.high, self.up_buf, self.down_buf, self.turn_buf, self.end_buf = bufs
        self.send, self.recv = send, recv
        self.copies = []
        self.axis = PARTS[p][0]
        self.me = getattr(here, self.axis)

    def index(self, at):
        full = slice(None)
        if "x" in at:
            return (at.get("y", full), at["x"] // 2, at.get("z", full), at["x"] % 2)
        return (at.get("y", full), full, at.get("z", full), full)

    def chunk(self, pos, half=None):
        index = list(self.index({self.axis: pos}))
        if half is not None:
            if self.axis == "y":
                index[1] = half
            else:
                index[0] = pl.ds(2 * half, 2)
        return self.acc.at[tuple(index)]

    def to(self, step):
        return self.here.at(**{self.axis: (self.me + step) % 4})

    def push(self, k, src, dst, device):
        copy = remote(src, dst, self.send.at[self.p, k], self.recv.at[self.p, k], device)
        copy.start()
        self.copies.append(copy)
        return copy

    def begin(self):
        far = (self.me + 2) % 4
        self.legs = (
            self.push(0, self.chunk(far, 0), self.low, self.to(1)),
            self.push(1, self.chunk(far, 1), self.high, self.to(3)),
        )

    def relay(self):
        up, down = (self.me + 1) % 4, (self.me + 3) % 4
        self.legs[0].wait_recv()
        add_into(self.chunk(up, 0), self.low)
        one = self.push(2, self.chunk(up), self.up_buf, self.to(1))
        self.legs[1].wait_recv()
        add_into(self.chunk(down, 1), self.high)
        two = self.push(3, self.chunk(down), self.down_buf, self.to(3))
        self.legs = (one, two)

    def across(self, k, name, buf, at):
        me = getattr(self.here, name)
        for step in (1, 3, 2):
            pos = (me + step) % 4
            remote(
                self.acc.at[self.index({**at, name: pos})], buf.at[me],
                self.send.at[self.p, k], self.recv.at[self.p, k], self.here.at(**{name: pos}),
            ).start()

    def cross(self):
        self.legs[0].wait_recv()
        self.legs[1].wait_recv()
        add_into(self.chunk(self.me), self.up_buf, self.down_buf)
        self.across(4, PLANES[self.axis][0], self.turn_buf, {self.axis: self.me})

    def turn(self):
        a, b = PLANES[self.axis]
        me = getattr(self.here, a)
        at = {self.axis: self.me, a: me}
        drain(self.turn_buf.at[pl.ds(0, 3)], self.recv.at[self.p, 4])
        add_into(
            self.acc.at[self.index(at)], *[self.turn_buf.at[(me + k) % 4] for k in (1, 2, 3)]
        )
        self.across(5, b, self.end_buf, at)

    def end(self):
        a, b = PLANES[self.axis]
        me = getattr(self.here, b)
        at = {self.axis: self.me, a: getattr(self.here, a), b: me}
        drain(self.end_buf.at[pl.ds(0, 3)], self.recv.at[self.p, 5])
        total = self.acc[self.index(at)].astype(F32)
        for k in (1, 2, 3):
            total += self.end_buf[(me + k) % 4].astype(F32)
        return total

    def finish(self):
        for copy in self.copies:
            copy.wait_send()
        drain(self.turn_buf.at[pl.ds(0, 3)], self.send.at[self.p, 4])
        drain(self.end_buf.at[pl.ds(0, 3)], self.send.at[self.p, 5])


def part_shape(p):
    return (4, 2, 4, 2) + PARTS[p][1:]


def part_buffers(p):
    axis, tail = PARTS[p][0], PARTS[p][1:]
    whole = {"x": (4, 4), "y": (2, 4, 2), "z": (4, 2, 2)}[axis]
    half = whole[1:] if axis == "y" else (2,) + whole[1:]
    last = (2, 2) if PLANES[axis][1] == "x" else (4,)
    shapes = [half + tail] * 2 + [whole + tail] * 2 + [(4,) + last + tail, (4,) + tail]
    return [pltpu.VMEM(s, BF) for s in shapes]


DMA = pltpu.SemaphoreType.DMA
SCRATCH = dict(
    scale_first=((384, 1), F32), scale_second=((384, 1), F32),
    spectra=((384, 768), BF), cot=((384, 768), BF), grad_input=((384, 768), BF),
    win=((4, 2, 4, 2, 32, 1024), BF), wout=((4, 2, 4, 2, 32, 1024), BF),
    chin=((1536, 768), BF), chout=((1536, 768), BF),
    normed=((12, 2, 16, 768), BF), tm=((12, 2, 16, 768), BF), ng=((12, 2, 16, 768), BF),
    mixg=((12, 2, 16, 768), BF), ns=((384, 768), BF), mg=((384, 768), F32),
    cact=((384, 1536), BF), cgrad=((384, 1536), BF),
    cact_s=((384, 1536), BF), cgrad_s=((384, 1536), BF),
    ns_s=((384, 384), BF), cot_s=((384, 384), BF),
    cols_t=((256, 2048), BF), second=((192, 768), F32), down=((384, 1536), F32),
    cols=((64, 2, 16, 256), BF), cols2=((64, 2, 16, 256), BF),
    cols_s=((64, 16, 256), BF), cols2_s=((64, 16, 256), BF),
    hidden=((256, 1024), F32), slope=((256, 1024), F32),
    act=((256, 1024), BF), act_s=((256, 1024), BF),
    hg=((256, 1024), BF), hg_s=((256, 1024), BF),
    mixb=((64, 2, 16, 256), BF), ncg=((64, 2, 16, 256), BF),
    fin=((4, 48, 384), F32), sum0=((16, 1024), F32), sum1=((16, 1024), F32),
    sum2=((12, 768), F32), sum3=((12, 768), F32),
)
SEMS = dict(
    load=(5,), a1_send=(), a1_recv=(), a1_esend=(4,), a1_erecv=(),
    a3_send=(), a3_recv=(), a3_esend=(4,), a3_erecv=(),
    a2_send=(), a2_recv=(2,), a2_esend=(),
    a4_send=(), a4_recv=(2,), a4_esend=(),
    w_own=(2,), w_send=(2, 25), w_recv=(2, 25), w_bsend=(2, 16), w_brecv=(2, 16),
    r_send=(9, 6), r_recv=(9, 6),
    s_send=(11,), s_recv=(11,), f_send=(3,), f_recv=(3,),
)


def block_kernel(
    spectra_in, cot_in, w_in, w_out, ch_in, ch_out, grad_out, o0, o1, o2, o3, *scratch
):
    v = types.SimpleNamespace(**dict(zip(list(SCRATCH) + list(SEMS), scratch)))
    spectra, cot, grad_input = v.spectra, v.cot, v.grad_input
    bufs = scratch[len(SCRATCH) + len(SEMS):]
    sums = scratch[len(SCRATCH) + len(SEMS) + 6 * len(PARTS):]
    here = Here()
    c = here.c
    sib = here.sibling()
    cross = here.at(x=here.xh * 2 + 1 - here.xl, c=1 - c)
    partners = [sib, cross]
    for k in (1, 3):
        x = (here.x + k) % 4
        partners += [here.at(x=x, z=(here.z + n) % 4) for n in range(4)]
        partners += [here.at(x=x, y=(here.y + n) % 4) for n in range(1, 4)]
    loads = [
        pltpu.make_async_copy(src, dst, v.load.at[k])
        for k, (src, dst) in enumerate((
            (spectra_in, spectra), (cot_in, cot), (ch_in, v.chin), (ch_out, v.chout),
        ))
    ]
    for copy in loads:
        copy.start()
    count = greet_seq(here) + greet(partners)
    loads.pop(0).wait()

    def norm_first(i, carry):
        unit, scale = normalize(spectra[rows(i, 32), :].astype(F32))
        v.normed[i] = unit.astype(BF).reshape(2, 16, 768)
        v.scale_first[rows(i, 32), :] = scale
        return carry

    lax.fori_loop(0, 12, norm_first, 0, unroll=6)
    pl.semaphore_wait(pltpu.get_barrier_semaphore(), count)

    shared = []

    def share(src, dst):
        k = len(shared)
        copy = remote(src, dst, v.s_send.at[k], v.s_recv.at[k], sib)
        copy.start()
        shared.append(copy)
        return copy

    gather = Gather(
        here, (w_in, w_out), (v.win, v.wout),
        (v.w_own, v.w_send, v.w_recv, v.w_bsend, v.w_brecv),
    )
    first = ToChannels(
        here, v.normed, v.cols, (v.a1_send, v.a1_recv, v.a1_esend, v.a1_erecv)
    )
    both = range(2)
    for w in both:
        gather.launch(w)
    first.start(0)
    first.start(1)
    for w in both:
        gather.crossed(w)
    for copy in loads:
        copy.wait()
    share(cot.at[:, lanes(384 * (1 - c), 384)], v.cot_s)

    def channel_down(i, carry):
        v.down[:, lanes(256 * i, 256)] = dot(cot[...], v.chout[rows(i, 256), :], NT)
        return carry

    for w in both:
        gather.first_near(w)
    for w in both:
        gather.second_near(w, 0)
    for w in both:
        gather.first_far(w)
    for o in (3, 1):
        for w in both:
            gather.second_near(w, o)
    first.arrive()
    share(v.cols.at[:, 1 - c], v.cols_s)
    for w in both:
        gather.second_near(w, 2)

    def turn_cols(y, carry):
        v.cols_t[:, lanes(512 * y, 512)] = v.cols[pl.ds(16 * y, 16)].reshape(512, 256).T
        return carry

    lax.fori_loop(0, 4, turn_cols, 0, unroll=2)
    for o in (0, 3, 1, 2):
        gather.second_far(0, o)
    gather.shared_near(0)
    gather.shared_far(0)

    def project(source, weight):
        def step(y, start):
            left = source[pl.ds(16 * y, 16)].reshape(512, 256)
            part = dot(left, weight[y].reshape(512, 1024), TN)
            if start:
                v.hidden[...] = part
            else:
                v.hidden[...] += part

        step(0, True)
        for y in range(1, 4):
            step(y, False)

    def hidden_of(i, carry):
        part = lanes(256 * i, 256)
        weight = v.win[:, :, :, :, :, part].reshape(2048, 256)
        v.hidden[:, part] = dot(v.cols_t[...], weight, NN)
        return carry

    lax.fori_loop(0, 4, hidden_of, 0, unroll=4)

    def token_gelu(i, carry):
        at = rows(i, 16)
        value, slope = gelu_pair(v.hidden[at, :])
        v.act[at, :] = value.astype(BF)
        v.slope[at, :] = slope
        return carry

    lax.fori_loop(0, 16, token_gelu, 0, unroll=8)
    share(v.act, v.act_s)

    def spread(weight, source, target, transfer, spots):
        left = jnp.concatenate([weight[y, :, z].reshape(128, 1024) for y, z, _ in spots], axis=0)
        value = dot(left, source[...], NT).astype(BF).reshape(len(spots), 2, 2, 2, 16, 256)
        for k, (y, z, other) in enumerate(spots):
            for xh in range(2):
                dest = 8 * y + 4 * xh + z
                target[pl.ds(2 * dest, 2)] = value[k, xh]
                transfer.start(dest, other)

    def off(name, step):
        return (getattr(here, name) + step) % 4

    second = ToPatches(
        here, v.mixb, v.tm, (v.a2_send, v.a2_recv, v.a2_esend)
    )
    gather.shared_near(1)

    def near(i, carry):
        z = off("z", i + i // 2)
        spread(
            v.wout, v.act, v.mixb, second, [(off("y", step), z, step > 0) for step in (1, 3, 0)]
        )
        return carry

    lax.fori_loop(0, 3, near, 0)
    for o in (0, 3, 1, 2):
        gather.second_far(1, o)
    gather.shared_far(1)
    spread(
        v.wout, v.act, v.mixb, second,
        [(off("y", 2), off("z", step), True) for step in (1, 3, 0)],
    )
    spread(
        v.wout, v.act, v.mixb, second,
        [(off("y", step), off("z", 2), True) for step in (2, 1, 3, 0)],
    )
    lax.fori_loop(0, 6, channel_down, 0, unroll=2)
    gather.finish()
    first.finish()

    third = ToChannels(
        here, v.mixg, v.cols2, (v.a3_send, v.a3_recv, v.a3_esend, v.a3_erecv)
    )

    def middle_of(at):
        source = spectra[rows(at, 32), :].astype(F32)
        mix = v.tm[at].reshape(32, 768).astype(F32)
        return (source + mix).astype(BF).astype(F32)

    for half in range(2):
        second.arrive(half)
        span = pl.ds(192 * half, 192)

        def norm_second(i, carry):
            at = half * 6 + i
            unit, scale = normalize(middle_of(at))
            v.ns[rows(at, 32), :] = unit.astype(BF)
            v.scale_second[rows(at, 32), :] = scale
            return carry

        lax.fori_loop(0, 6, norm_second, 0, unroll=6)

        def hidden_units(i, carry):
            part = lanes(256 * i, 256)
            own = rows(i, 256)
            value, slope = gelu_pair(dot(v.ns[span, :], v.chin[own, :], NT))
            v.cact[span, part] = value.astype(BF)
            v.cgrad[span, part] = (v.down[span, part] * slope).astype(BF)
            return carry

        lax.fori_loop(0, 6, hidden_units, 0, unroll=3)
        for src, dst in ((v.cgrad, v.cgrad_s), (v.cact, v.cact_s)):
            share(src.at[span], dst.at[span])
        share(v.ns.at[span, lanes(384 * (1 - c), 384)], v.ns_s.at[span])
        v.second[...] = dot(v.cgrad[span, :], v.chin[...], NN)

        def back_second(i, carry):
            at = half * 6 + i
            unit = v.ns[rows(at, 32), :].astype(F32)
            scale = v.scale_second[rows(at, 32), :]
            upstream = v.second[rows(i, 32), :]
            value = cot[rows(at, 32), :].astype(F32) + norm_back(unit, scale, upstream)
            v.mg[rows(at, 32), :] = value
            v.mixg[at] = value.astype(BF).reshape(2, 16, 768)
            return carry

        lax.fori_loop(0, 6, back_second, 0, unroll=6)
        third.start(half)

    for copy in shared:
        copy.wait_recv()
    half_lanes = lanes(384 * c, 384)
    for g, (act, tok, act_s, tok_s) in enumerate((
        (v.cgrad, v.ns, v.cgrad_s, v.ns_s), (v.cact, cot, v.cact_s, v.cot_s),
    )):
        def channel_sum(y, carry):
            part = lanes(384 * y, 384)
            total = dot(act[:, part], tok[:, half_lanes], TN)
            total += dot(act_s[:, part], tok_s[...], TN)
            total = total.astype(BF).reshape(2, 4, 48, 384)
            for p in range(3):
                sums[p][y, :, :, g] = total[..., 128 * p:128 * p + 128]
            return carry

        lax.fori_loop(0, 4, channel_sum, 0, unroll=4)

    parts = [
        PartSum(here, p, sums[p], bufs[6 * p:6 * p + 6], v.r_send, v.r_recv)
        for p in range(len(PARTS))
    ]
    channel_parts, early, late = parts[:3], parts[3:6], parts[6:]
    for part in channel_parts:
        part.begin()
    for part in channel_parts:
        part.relay()

    second.finish()
    third.arrive()
    share_cols2 = share(v.cols2.at[:, 1 - c], v.cols2_s)
    project(v.cols2, v.wout)

    def token_grad(i, carry):
        at = rows(i, 16)
        v.hg[at, :] = (v.hidden[at, :] * v.slope[at, :]).astype(BF)
        return carry

    lax.fori_loop(0, 16, token_grad, 0, unroll=8)
    share_hg = share(v.hg, v.hg_s)

    def token_sum(left, left_s, right, right_s, targets):
        def step(y, carry):
            own = left[pl.ds(16 * y, 16), c].reshape(256, 256)
            other = left_s[pl.ds(16 * y, 16)].reshape(256, 256)
            total = dot(own, right[...], NN) + dot(other, right_s[...], NN)
            total = total.astype(BF).reshape(2, 4, 2, 16, 1024)
            place = 0
            for p in targets:
                width = PARTS[p][2]
                sums[p][y] = total[..., place:place + width]
                place += width
            return carry

        lax.fori_loop(0, 4, step, 0, unroll=4)

    share_cols2.wait_recv()
    token_sum(
        v.cols2, v.cols2_s, v.act, v.act_s, (3, 4, 5),
    )
    for part in early:
        part.begin()
    for part in channel_parts:
        part.cross()
    share_hg.wait_recv()
    token_sum(
        v.cols, v.cols_s, v.hg, v.hg_s, (6, 7, 8),
    )
    for part in late:
        part.begin()
    for part in early:
        part.relay()
    for part in channel_parts:
        part.turn()
    fourth = ToPatches(
        here, v.ncg, v.ng, (v.a4_send, v.a4_recv, v.a4_esend)
    )

    def back(i, carry):
        z = off("z", 3 - i)
        spread(
            v.win, v.hg, v.ncg, fourth, [(off("y", step), z, step > 0) for step in (2, 1, 3, 0)]
        )
        return carry

    lax.fori_loop(0, 4, back, 0, unroll=2)
    for part in late:
        part.relay()
    for part in early:
        part.cross()

    def input_grad(half):
        fourth.arrive(half)

        def step(i, carry):
            at = half * 6 + i
            unit = v.normed[at].reshape(32, 768).astype(F32)
            scale = v.scale_first[rows(at, 32), :]
            upstream = v.ng[at].reshape(32, 768).astype(F32)
            value = v.mg[rows(at, 32), :] + norm_back(unit, scale, upstream)
            grad_input[rows(at, 32), :] = value.astype(BF)
            return carry

        lax.fori_loop(0, 6, step, 0, unroll=6)

    for p, part in enumerate(channel_parts):
        v.fin[here.d, :, 128 * p:128 * p + 128] = part.end()
    input_grad(0)
    swaps = []
    for k, device in enumerate((sib, here.at(x=here.xh * 2 + 1 - here.xl), cross)):
        copy = remote(
            v.fin.at[here.d], v.fin.at[here.d], v.f_send.at[k], v.f_recv.at[k], device
        )
        copy.start()
        swaps.append(copy)
    for part in early:
        part.turn()
    for part in late:
        part.cross()
    input_grad(1)
    stores = [pltpu.make_async_copy(grad_input, grad_out, v.load.at[4])]
    stores[0].start()
    for part in late:
        part.turn()

    def gather_up(out, group):
        place = 0
        for part in group:
            width = PARTS[part.p][2]
            out[:, place:place + width] = part.end()
            place += width

    def keep(k, src, dst):
        copy = pltpu.make_async_copy(src, dst, v.load.at[k])
        copy.start()
        return copy

    gather_up(v.sum1, early)
    stores.append(keep(0, v.sum1, o1))
    for copy in swaps:
        copy.wait()
    for d in range(4):
        @pl.when(here.d == d)
        def _():
            for total, g in ((v.sum2, 0), (v.sum3, 2)):
                for k in range(2):
                    total[:, 384 * k:384 * k + 384] = v.fin[g + k, 12 * d:12 * d + 12]
    stores.append(keep(1, v.sum2, o2))
    stores.append(keep(2, v.sum3, o3))
    for part in channel_parts + early:
        part.finish()
    for copy in shared:
        copy.wait_send()
    third.finish()
    fourth.finish()
    gather_up(v.sum0, late)
    stores.append(keep(3, v.sum0, o0))
    for part in late:
        part.finish()
    for copy in stores:
        copy.wait()


def hand_over(*refs):
    for src, dst in zip(refs[:5], refs[5:]):
        dst[...] = src[...]


def local(spectra_in, cotangent, tok_in_w, tok_out_w, ch_in_w, ch_out_w):
    vmem = pl.BlockSpec(memory_space=pltpu.VMEM)
    scratch = [pltpu.VMEM(shape, kind) for shape, kind in SCRATCH.values()]
    scratch += [DMA(shape) if shape else DMA for shape in SEMS.values()]
    for p in range(len(PARTS)):
        scratch += part_buffers(p)
    scratch += [pltpu.VMEM(part_shape(p), BF) for p in range(len(PARTS))]
    shapes = (
        jax.ShapeDtypeStruct((384, 768), BF),
        jax.ShapeDtypeStruct((16, 1024), F32),
        jax.ShapeDtypeStruct((16, 1024), F32),
        jax.ShapeDtypeStruct((12, 768), F32),
        jax.ShapeDtypeStruct((12, 768), F32),
    )
    outs = pl.pallas_call(
        block_kernel,
        out_shape=shapes,
        in_specs=[ANY] * 6, out_specs=(ANY,) * 5,
        scratch_shapes=scratch,
        compiler_params=pltpu.CompilerParams(
            collective_id=0, has_side_effects=True, vmem_limit_bytes=60 * 1024 * 1024
        ),
        name="mixer_block_backward",
    )(
        spectra_in.reshape(384, 768), cotangent.reshape(384, 768),
        tok_in_w.reshape(2, 32, 1024), tok_out_w.reshape(2, 32, 1024), ch_in_w, ch_out_w,
    )
    grad_input, *weights = pl.pallas_call(
        hand_over, out_shape=shapes, in_specs=[vmem] * 5, out_specs=(vmem,) * 5, name="hand_over",
    )(*outs)
    return (grad_input.reshape(6, 64, 768), *weights)


def solution(mesh):
    in_specs = (
        P("dp", "seq", None),
        P("dp", "seq", None),
        P("seq", None),
        P("seq", None),
        P(),
        P(),
    )
    out_specs = (
        P("dp", "seq", None),
        P(("seq", "dp"), None),
        P(("seq", "dp"), None),
        P(("seq", "dp"), None),
        P(("seq", "dp"), None),
    )
    return jax.shard_map(local, mesh=mesh, in_specs=in_specs, out_specs=out_specs, check_vma=False)
```
